256 devices in a mesh: slab: 128 (over z, y, x), band: 2 (over core).
Axes of the slice: x: 4, y: 4, z: 8, core: 2. Of those that a mesh axis runs over, the one named last changes fastest.
Arguments:
- block: float32 [32, 3, 256, 32, 128], P('band', None, 'slab'), may hold values from -19 to 19
- labels: int32 [256, 32, 128], P('slab'), may hold values from 0 to 2
- inverse_eps: float32 [3], replicated, may hold values from 0.08 to 1
Outputs:
- next_block: float32 [32, 3, 256, 32, 128], P('band', None, 'slab')
- rayleigh: float32 [64, 64], replicated
The draws below stay inside these ranges and needn't reach their ends.
All inputs are finite; a program needn't handle non-finite values.
Results may differ from the reference program's by a relative error of at most 0.0003.
Values sent between devices are 32-bit elements; how exact they have to be, the bound alone decides.
A program may use at most 64 MiB of HBM per device.

```python
import math
import jax
import jax.numpy as jnp
from jax import lax

BANDS = 32
NY = 32
NZ = 128
REGIONS = 3
NX = 256


def draw_block(key, part):
    key = jax.random.fold_in(key, 11)
    cell_key, noise_key = jax.random.split(key, 2)
    shape = (BANDS, 3, NX, NY, NZ)
    level = jax.random.uniform(cell_key, (NX, NY, NZ), jnp.float32, -0.5, 0.5)
    fields = jnp.clip(jax.random.normal(noise_key, shape, jnp.float32), -6.0, 6.0)
    envelope = jnp.exp(level * math.log(10.0))
    return (fields * envelope[None, None]).astype(jnp.float32)


def touch_ends(result, rng, smallest, top_value):
    dims = result.shape
    spot = [jax.random.randint(jax.random.fold_in(rng, axis), (), 0, dims[axis]) for axis in range(len(dims))]
    result = result.at[tuple(spot)].set(smallest)
    longest = dims.index(max(dims))
    spot[longest] = (spot[longest] + 1) % dims[longest]
    return result.at[tuple(spot)].set(top_value)


def setup_inputs(seed: int = 0) -> dict:
    streams_of = jax.random.split(jax.random.key(seed), 4)
    return {
        "block": draw_block(jax.random.fold_in(streams_of[3], 71), 0),
        "labels": touch_ends(jax.random.randint(streams_of[1], (NX, NY, NZ), 0, REGIONS), jax.random.fold_in(streams_of[1], 1), 0, REGIONS - 1).astype(jnp.int32),
        "inverse_eps": jnp.clip(jnp.exp(jax.random.uniform(streams_of[2], (REGIONS,), jnp.float32, math.log(0.08), math.log(1.0))), 0.08, 1.0),
    }


def forward_curl(field):

    def diff(values, axis):
        return jnp.roll(values, -1, axis) - values
    comp_x, comp_y, comp_z = (field[0], field[1], field[2])
    return jnp.stack([diff(comp_z, 1) - diff(comp_y, 2), diff(comp_x, 2) - diff(comp_z, 0), diff(comp_y, 0) - diff(comp_x, 1)], 0)

def backward_curl(field):

    def diff(values, axis):
        return values - jnp.roll(values, 1, axis)
    comp_x, comp_y, comp_z = (field[0], field[1], field[2])
    return jnp.stack([diff(comp_z, 1) - diff(comp_y, 2), diff(comp_x, 2) - diff(comp_z, 0), diff(comp_y, 0) - diff(comp_x, 1)], 0)

def subspace_step(gram):
    rows = gram.shape[0]
    bands = rows // 2
    correlation = gram[:, :rows]
    correlation = 0.5 * (correlation + correlation.T)
    projected = gram[:, bands:]
    projected = 0.5 * (projected + projected.T)
    lower = jnp.linalg.cholesky(correlation)
    half_solved = jax.scipy.linalg.solve_triangular(lower, projected, lower=True)
    rayleigh = jax.scipy.linalg.solve_triangular(lower, half_solved.T, lower=True)
    coeffs = jax.scipy.linalg.solve_triangular(lower, rayleigh[:, :bands], lower=True, trans=1)
    return (rayleigh, coeffs)

def reference(block, labels, inverse_eps):
    regions = jnp.arange(inverse_eps.shape[0], dtype=jnp.int32)
    eta = jnp.sum((labels[None] == regions[:, None, None, None]).astype(jnp.float32) * inverse_eps[:, None, None, None], 0)

    def operate(field):
        return 0.25 * backward_curl(eta[None] * forward_curl(field))
    first = lax.map(operate, block)
    second = lax.map(operate, first)
    count = 3 * NX * NY * NZ
    basis = jnp.concatenate([block, first], 0).reshape(2 * BANDS, -1)
    whole = jnp.concatenate([block, first, second], 0).reshape(3 * BANDS, -1)
    gram = jnp.einsum('an,bn->ab', basis, whole, precision=lax.Precision.HIGHEST) / count
    rayleigh, coeffs = subspace_step(gram)
    next_block = jnp.einsum('kj,kn->jn', coeffs, basis, precision=lax.Precision.HIGHEST)
    return (next_block.reshape(block.shape), rayleigh)
```

```python
import functools

import jax
import jax.numpy as jnp
from jax import lax
from jax.experimental import pallas as pl
from jax.experimental.pallas import tpu as pltpu
from jax.sharding import PartitionSpec as P

MESH = pl.DeviceIdType.MESH
F32 = jnp.float32
BF16 = jnp.bfloat16
CX, CY, CZ = 4, 4, 8
ROWS = 16
CHUNKS = ((0, 6), (6, 10), (10, 14), (14, 18))
NT = (((1,), (1,)), ((), ()))
NN = (((1,), (0,)), ((), ()))


def rf(v):
    return pltpu.roll(v, v.shape[-1] - 1, v.ndim - 1)


def rb(v):
    return pltpu.roll(v, 1, v.ndim - 1)


def split(v):
    hi = v.astype(BF16)
    return hi, (v - hi.astype(F32)).astype(BF16)


def dot32(a, b, dims):
    return lax.dot_general(
        a, b, dims, precision=lax.Precision.HIGHEST, preferred_element_type=F32
    )


def remote(src, dst, send, recv, to):
    return pltpu.make_async_remote_copy(
        src_ref=src, dst_ref=dst, send_sem=send, recv_sem=recv, device_id=to, device_id_type=MESH
    )


def eliminate(corr):
    n = corr.shape[0]
    row_id = lax.broadcasted_iota(jnp.int32, (8, 2 * n), 0)
    eye = (
        lax.broadcasted_iota(jnp.int32, (n, n), 0) == lax.broadcasted_iota(jnp.int32, (n, n), 1)
    ).astype(F32)
    whole = jnp.concatenate([corr, eye], axis=1)
    parts = [whole[8 * i : 8 * i + 8] for i in range(n // 8)]
    for k in range(n):
        home, at = divmod(k, 8)
        pivot = parts[home][at : at + 1, :]
        scaled = pivot * (1.0 / pivot[:, k : k + 1])
        for i in range(home, n // 8):
            factor = parts[i][:, k : k + 1]
            step = factor * scaled
            if i == home:
                step = jnp.where(row_id > at, step, 0.0)
            parts[i] = parts[i] - step
    whole = jnp.concatenate(parts, axis=0)
    diag = jnp.sum(whole[:, :n] * eye, axis=1, keepdims=True)
    return whole[:, n:] * (1.0 / jnp.sqrt(diag))


def kernel(
    count,
    block,
    labels,
    inv,
    out,
    ray_out,
    xin,
    xt,
    pq,
    sq,
    xw,
    hb,
    ha,
    sa,
    qb,
    eta,
    eta_in,
    hs,
    hyb,
    hzm,
    ax,
    axm,
    tiles,
    ar_src,
    ar1,
    ar2_src,
    ar2,
    ct,
    ysend,
    yrecv,
    in_sem,
    out_sem,
    loc_sem,
    halo_s,
    halo_r,
    late_s,
    late_r,
    swap_s,
    swap_r,
    eta_s,
    eta_r,
    ar1_s,
    ar1_r,
    ar2_s,
    ar2_r,
    y_s,
    y_r,
):
    slabs = CX * CY * CZ
    s = lax.axis_index("slab")
    k = lax.axis_index("band")
    x = lax.rem(s, CX)
    y = lax.rem(lax.div(s, CX), CY)
    z = lax.div(s, CX * CY)
    up = lax.rem(s + 1, slabs)
    down = lax.rem(s + slabs - 1, slabs)
    base = s - x - CX * y
    plane = [
        (base + CX * lax.rem(y + i, CY) + lax.rem(x + j, CX), c)
        for i in range(CY)
        for j in range(CX)
        for c in range(2)
        if (i, j) != (0, 0)
    ]
    column = [
        (s - CX * CY * z + CX * CY * lax.rem(z + i, CZ), c) for i in range(1, CZ) for c in range(2)
    ]
    sibling = (s, 1 - k)
    mine = pl.multiple_of(16 * k, 16)
    theirs = pl.multiple_of(16 * (1 - k), 16)

    barrier = pltpu.get_barrier_semaphore()
    greeted = [sibling, (up, 0), (up, 1), (down, 0), (down, 1)] + plane + column
    for to in greeted:
        pl.semaphore_signal(barrier, inc=1, device_id=to, device_id_type=MESH)

    load = pltpu.make_async_copy(block, xin, in_sem.at[0])
    load.start()

    for p in range(2):
        lab = labels[p]
        value = jnp.zeros(lab.shape, F32)
        for r in range(3):
            value = value + jnp.where(lab == r, 1.0, 0.0) * inv[r]
        eta[p, 1:33] = value
        eta[p, 0:1] = value[31:32]
        eta[p, 33:35] = value[0:2]

    load.wait()

    def turn(row, carry):
        for p in range(2):
            for c in range(3):
                xt[p * 3 + c, row + 1] = xin[pl.ds((c * 2 + p) * 32 + row, 16, stride=192), :]
        return carry

    lax.fori_loop(0, 32, turn, 0, unroll=2)
    for r in range(6):
        xt[r, 0] = xt[r, 32]
        xt[r, 33] = xt[r, 1]
        xt[r, 34] = xt[r, 2]

    pl.semaphore_wait(barrier, len(greeted))

    halos = []
    for n, (lo, hi) in enumerate(CHUNKS):
        for to in range(2):
            i = n * 2 + to
            rows = pl.ds(16 * to + lo, hi - lo)
            halos.append(
                remote(
                    xt.at[pl.ds(1, 2), rows],
                    ha.at[:, pl.ds(lo, hi - lo), pl.ds(mine, 16)],
                    halo_s.at[0, n, to],
                    halo_r.at[0, n, k],
                    (down, to),
                )
            )
    for c in halos:
        c.start()

    own = pltpu.make_async_copy(
        xt.at[:, pl.ds(mine, 19)], xw.at[:, :, pl.ds(mine, 16)], loc_sem.at[0]
    )
    own.start()
    swap = remote(
        xt.at[:, pl.ds(theirs, 19)],
        xw.at[:, :, pl.ds(mine, 16)],
        swap_s.at[0],
        swap_r.at[0],
        sibling,
    )
    swap.start()
    eta_copy = remote(eta.at[1], eta_in, eta_s.at[0], eta_r.at[0], (up, k))
    eta_copy.start()

    def above(row, carry):
        ex = xt[3, row]
        pq[0, row] = xt[4, row] + (xt[3, row + 1] - ex)
        pq[1, row] = (rf(ex) - ex) + xt[5, row]
        return carry

    lax.fori_loop(0, 34, above, 0, unroll=2)
    ups = []
    for n, (lo, hi) in enumerate(CHUNKS):
        for to in range(2):
            rows = pl.ds(16 * to + lo, hi - lo)
            ups.append(
                remote(
                    pq.at[:, rows],
                    hb.at[:, pl.ds(lo, hi - lo), pl.ds(mine, 16)],
                    halo_s.at[1, n, to],
                    halo_r.at[1, n, k],
                    (up, to),
                )
            )
    for c in ups:
        c.start()

    def eta_row(p, row):
        return eta[p, pl.ds(row, 1), :]

    def curl_x(p, row):
        ey = xt[3 * p + 1, row]
        return eta_row(p, row) * ((xt[3 * p + 2, row + 1] - xt[3 * p + 2, row]) - (rf(ey) - ey))

    def late(row, before):
        ea = eta_row(0, row)
        ex, ey, ez = xt[0, row], xt[1, row], xt[2, row]
        now = curl_x(0, row)
        hy = ea * ((rf(ex) - ex) - (xt[5, row] - ez))
        hz = ea * ((xt[4, row] - ey) - (xt[0, row + 1] - ex))
        sq[0, row - 1] = hy - (now - before)
        hx = curl_x(1, row)
        sq[1, row - 1] = (hx - rb(hx)) + hz
        return now

    lax.fori_loop(1, 33, late, curl_x(0, 0))
    lates = []
    for d, to_slab, dst in ((0, down, sa), (1, up, qb)):
        for to in range(2):
            lates.append(
                remote(
                    sq.at[d, pl.ds(16 * to, 16)],
                    dst.at[:, pl.ds(mine, 16)],
                    late_s.at[d, to],
                    late_r.at[d, k],
                    (to_slab, to),
                )
            )
    for c in lates:
        c.start()

    own.wait()
    swap.wait()

    def eta_at(p, row):
        return eta[p, pl.ds(mine + row, 1), :]

    def inside(row, carry):
        ea, eb = eta_at(0, row), eta_at(1, row)
        ex, ey, ez = xw[0, row], xw[1, row], xw[2, row]
        fy, fz = xw[4, row], xw[5, row]
        hs[0, row] = ea * ((xw[2, row + 1] - ez) - (rf(ey) - ey))
        hs[1, row] = ea * ((rf(ex) - ex) - (fz - ez))
        hs[2, row] = ea * ((fy - ey) - (xw[0, row + 1] - ex))
        hs[3, row] = eb * ((xw[5, row + 1] - fz) - (rf(fy) - fy))
        return carry

    lax.fori_loop(0, 18, inside, 0)
    eta_copy.wait()

    def fields(row):
        eb = eta_at(1, row)
        em = eta_in[pl.ds(mine + row, 1), :]
        ex = xw[3, row]
        hy = eb * ((rf(ex) - ex) - (ha[1, row] - xw[5, row]))
        hz = eb * ((ha[0, row] - xw[4, row]) - (xw[3, row + 1] - ex))
        my = em * (hb[1, row] - xw[2, row])
        mz = em * (xw[1, row] - hb[0, row])
        hyb[row] = hy
        hzm[row] = mz
        return hy, hz, my, mz

    def image(row, carry):
        hz_old, mz_old = carry
        hy, hz, my, mz = fields(row)
        ax_, ay_, az_, bx_ = hs[0, row], hs[1, row], hs[2, row], hs[3, row]
        ax[0, row] = 0.25 * ((az_ - hs[2, row - 1]) - (ay_ - rb(ay_)))
        ax[1, row] = 0.25 * ((ax_ - rb(ax_)) - (az_ - mz))
        ax[2, row] = 0.25 * ((ay_ - my) - (ax_ - hs[0, row - 1]))
        ax[3, row] = 0.25 * ((hz - hz_old) - (hy - rb(hy)))
        ax[4, row] = 0.25 * ((bx_ - rb(bx_)) - (hz - az_))
        ax[5, row] = 0.25 * ((hy - ay_) - (bx_ - hs[3, row - 1]))
        axm[row] = 0.25 * ((mz - mz_old) - (my - rb(my)))
        return hz, mz

    def products(row, total):
        for r in range(0, 6, 2):
            pair = []
            for q in (r, r + 1):
                xh, xl = split(xw[q, row])
                ah, al = split(ax[q, row])
                tile = jnp.concatenate([xh, ah, xl, al], axis=0)
                pair.append(tile)
            both = jnp.concatenate(pair, axis=1)
            tiles[(row - 1) * 3 + r // 2] = both
            total = total + lax.dot_general(both, both, NT, preferred_element_type=F32)
        return total

    total = jnp.zeros((128, 128), F32)
    carry = None
    for n, (lo, hi) in enumerate(CHUNKS):
        for d, (dst, slab) in enumerate(((ha, down), (hb, up))):
            for c in range(2):
                arrived = dst.at[:, pl.ds(lo, hi - lo), pl.ds(16 * c, 16)]
                remote(
                    arrived, arrived, halo_s.at[d, n, c], halo_r.at[d, n, c], (slab, c)
                ).wait_recv()
        if n == 0:
            _, hz, _, mz = fields(0)
            carry = (hz, mz)
        carry = lax.fori_loop(max(lo, 1), hi, image, carry)
        total = lax.fori_loop(max(lo - 1, 1), hi - 1, products, total)

    for d, dst in enumerate((sa, qb)):
        for c in range(2):
            arrived = dst.at[:, pl.ds(16 * c, 16)]
            remote(
                arrived, arrived, late_s.at[d, c], late_r.at[d, c], ((down, up)[d], c)
            ).wait_recv()

    def third(row, acc):
        ea, eb = eta_at(0, row), eta_at(1, row)
        em = eta_in[pl.ds(mine + row, 1), :]
        ux, uy, uz = ax[0, row], ax[1, row], ax[2, row]
        vx, vy, vz = ax[3, row], ax[4, row], ax[5, row]
        pz = 0.25 * (sa[row - 1] - hyb[row])
        my = 0.25 * (qb[row - 1] - hzm[row])
        curls = (
            (ea, (ax[2, row + 1] - uz) - (rf(uy) - uy)),
            (ea, (rf(ux) - ux) - (vz - uz)),
            (ea, (vy - uy) - (ax[0, row + 1] - ux)),
            (eb, (ax[5, row + 1] - vz) - (rf(vy) - vy)),
            (eb, (rf(vx) - vx) - (pz - vz)),
            (em, (uy - my) - (axm[row + 1] - axm[row])),
        )
        for i in range(0, 6, 2):
            left, right = [], []
            for e, v in curls[i : i + 2]:
                left.append(jnp.concatenate(split(v), axis=0))
                right.append(jnp.concatenate(split(e * v), axis=0))
            acc = acc + lax.dot_general(
                jnp.concatenate(left, axis=1),
                jnp.concatenate(right, axis=1),
                NT,
                preferred_element_type=F32,
            )
        return acc

    acc = lax.fori_loop(1, 17, third, jnp.zeros((64, 64), F32))

    g = (total[:64, :64] + total[64:, 64:]) + (total[:64, 64:] + total[64:, :64])
    g3 = 0.25 * ((acc[:32, :32] + acc[32:, 32:]) + (acc[:32, 32:] + acc[32:, :32]))
    packed = jnp.concatenate([g[:32, :32], g[:32, 32:], g[32:, 32:], g3], axis=1)
    ar_src[0] = packed[:16]
    ar_src[1] = packed[16:]
    slot = (y * CX + x) * 2 + k
    firsts = []
    i = 0
    for to in plane:
        firsts.append(
            remote(ar_src.at[to[1]], ar1.at[slot], ar1_s.at[i], ar1_r.at[(i // 2) * 2 + k], to)
        )
        i += 1
    firsts.append(remote(ar_src.at[1 - k], ar1.at[slot], ar1_s.at[i], ar1_r.at[i], sibling))
    for c in firsts:
        c.start()
    ar1[slot] = ar_src[k]
    for i in range(len(plane) + 1):
        remote(ar_src.at[0], ar1.at[0], ar1_s.at[i], ar1_r.at[i], sibling).wait_recv()
    half = ar1[0]
    for i in range(1, 2 * CX * CY):
        half = half + ar1[i]
    ar2_src[...] = half
    ar2[k, z] = half
    seconds = []
    for i, to in enumerate(column):
        seconds.append(
            remote(ar2_src, ar2.at[k, z], ar2_s.at[i], ar2_r.at[(i // 2) * 2 + k], to)
        )
    i = len(column)
    seconds.append(remote(ar2_src, ar2.at[k, z], ar2_s.at[i], ar2_r.at[i], sibling))
    for c in seconds:
        c.start()
    for i in range(len(column) + 1):
        remote(ar2_src, ar2.at[0, 0], ar2_s.at[i], ar2_r.at[i], sibling).wait_recv()
    halves = []
    for c in range(2):
        half = ar2[c, 0]
        for i in range(1, CZ):
            half = half + ar2[c, i]
        halves.append(half)
    packed = jnp.concatenate(halves, axis=0) * (1.0 / count)

    g0, g1, g2, g3 = (packed[:, 32 * i : 32 * i + 32] for i in range(4))
    flip = packed.T
    g0 = 0.5 * (g0 + flip[0:32])
    g1t = flip[32:64]
    g2 = 0.5 * (g2 + flip[64:96])
    g3 = 0.5 * (g3 + flip[96:128])
    corr = jnp.concatenate(
        [jnp.concatenate([g0, g1], axis=1), jnp.concatenate([g1t, g2], axis=1)], axis=0
    )
    proj = jnp.concatenate(
        [
            jnp.concatenate([0.5 * (g1 + g1t), g2], axis=1),
            jnp.concatenate([g2, g3], axis=1),
        ],
        axis=0,
    )
    inverse = eliminate(corr)
    solved = dot32(inverse, proj, NN)
    ray_out[...] = dot32(inverse, solved, NT)
    coeffs = dot32(dot32(solved[:32], inverse, NT), inverse, NN)
    ct[...] = coeffs
    own_h, own_l = split(ct[pl.ds(mine, 16), :])
    oth_h, oth_l = split(ct[pl.ds(theirs, 16), :])
    left = jnp.concatenate([own_h, oth_h, own_l, oth_l], axis=0)
    left = jnp.concatenate([left, left], axis=1)

    ys = []
    for r in range(0, 6, 2):

        def fresh(row, carry):
            res = lax.dot_general(
                left, tiles[row * 3 + r // 2], NN, preferred_element_type=F32
            )
            res = res[:32] + res[32:]
            for q in range(2):
                p, c = divmod(r + q, 3)
                part = res[:, 128 * q : 128 * q + 128]
                xin[pl.ds((c * 2 + p) * 32 + mine + row, 16, stride=192), :] = part[:16]
                ysend[r + q, row] = part[16:]
            return carry

        lax.fori_loop(0, 16, fresh, 0, unroll=2)
        copy = remote(
            ysend.at[pl.ds(r, 2)],
            yrecv.at[pl.ds(r, 2)],
            y_s.at[r // 2],
            y_r.at[r // 2],
            sibling,
        )
        copy.start()
        ys.append(copy)
    for r in range(0, 6, 2):
        ys[r // 2].wait_recv()

        def place(row, carry):
            for q in range(2):
                p, c = divmod(r + q, 3)
                xin[pl.ds((c * 2 + p) * 32 + theirs + row, 16, stride=192), :] = yrecv[r + q, row]
            return carry

        lax.fori_loop(0, 16, place, 0, unroll=2)
    store = pltpu.make_async_copy(xin, out, out_sem.at[0])
    store.start()
    for c in halos + ups + lates + firsts + seconds + ys:
        c.wait_send()
    store.wait()


def on_device(block, labels, inverse_eps):
    bands, comps, planes, ny, nz = block.shape
    count = comps * planes * CX * CY * CZ * ny * nz
    dma = pltpu.SemaphoreType.DMA
    vmem = pltpu.VMEM
    chips = CX * CY
    next_block, rayleigh = pl.pallas_call(
        functools.partial(kernel, count),
        out_shape=(
            jax.ShapeDtypeStruct((bands * comps * planes * ny, nz), F32),
            jax.ShapeDtypeStruct((64, 64), F32),
        ),
        in_specs=[
            pl.BlockSpec(memory_space=pl.ANY),
            pl.BlockSpec(memory_space=pltpu.VMEM),
            pl.BlockSpec(memory_space=pltpu.SMEM),
        ],
        out_specs=(pl.BlockSpec(memory_space=pl.ANY), pl.BlockSpec(memory_space=pltpu.VMEM)),
        scratch_shapes=[
            vmem((3072, 128), F32),
            vmem((6, 35, 16, 128), F32),
            vmem((2, 35, 16, 128), F32),
            vmem((2, 32, 16, 128), F32),
            vmem((6, 19, 32, 128), F32),
            vmem((2, 18, 32, 128), F32),
            vmem((2, 18, 32, 128), F32),
            vmem((16, 32, 128), F32),
            vmem((16, 32, 128), F32),
            vmem((2, 40, 128), F32),
            vmem((40, 128), F32),
            vmem((4, 18, 32, 128), F32),
            vmem((18, 32, 128), F32),
            vmem((18, 32, 128), F32),
            vmem((6, 18, 32, 128), F32),
            vmem((18, 32, 128), F32),
            vmem((48, 128, 256), BF16),
            vmem((2, 16, 128), F32),
            vmem((2 * chips, 16, 128), F32),
            vmem((16, 128), F32),
            vmem((2, CZ, 16, 128), F32),
            vmem((32, 64), F32),
            vmem((6, 16, 16, 128), F32),
            vmem((6, 16, 16, 128), F32),
            dma((1,)),
            dma((1,)),
            dma((1,)),
            dma((2, len(CHUNKS), 2)),
            dma((2, len(CHUNKS), 2)),
            dma((2, 2)),
            dma((2, 2)),
            dma((1,)),
            dma((1,)),
            dma((1,)),
            dma((1,)),
            dma((2 * chips - 1,)),
            dma((2 * chips - 1,)),
            dma((2 * CZ - 1,)),
            dma((2 * CZ - 1,)),
            dma((3,)),
            dma((3,)),
        ],
        compiler_params=pltpu.CompilerParams(
            collective_id=0, has_side_effects=True, vmem_limit_bytes=48 << 20
        ),
        name="subspace",
    )(block.reshape(bands * comps * planes * ny, nz), labels, inverse_eps)
    return next_block.reshape(block.shape), rayleigh


def solution(mesh):
    in_specs = (P("band", None, "slab", None, None), P("slab", None, None), P())
    out_specs = (P("band", None, "slab", None, None), P())
    return jax.shard_map(
        on_device, mesh=mesh, in_specs=in_specs, out_specs=out_specs, check_vma=False
    )
```

```python
import functools

import jax
import jax.numpy as jnp
from jax import lax
from jax.experimental import pallas as pl
from jax.experimental.pallas import tpu as pltpu
from jax.sharding import PartitionSpec as P

MESH = pl.DeviceIdType.MESH
F32 = jnp.float32
BF16 = jnp.bfloat16
CX, CY, CZ = 4, 4, 8
PIECE = 4
PIECES = 16 // PIECE
NT = (((1,), (1,)), ((), ()))
NN = (((1,), (0,)), ((), ()))


def rf(v):
    return pltpu.roll(v, v.shape[-1] - 1, v.ndim - 1)


def rb(v):
    return pltpu.roll(v, 1, v.ndim - 1)


def split(v):
    hi = v.astype(BF16)
    return hi, (v - hi.astype(F32)).astype(BF16)


def dot32(a, b, dims):
    return lax.dot_general(
        a, b, dims, precision=lax.Precision.HIGHEST, preferred_element_type=F32
    )


def remote(src, dst, send, recv, to):
    return pltpu.make_async_remote_copy(
        src_ref=src, dst_ref=dst, send_sem=send, recv_sem=recv, device_id=to, device_id_type=MESH
    )


def pack(m):
    return jnp.concatenate([m[8 * i : 8 * i + 8] for i in range(4)], axis=1)


def unpack(v):
    return jnp.concatenate([v[:, 32 * i : 32 * i + 32] for i in range(4)], axis=0)


def identity(n):
    rows = lax.broadcasted_iota(jnp.int32, (n, n), 0)
    return (rows == lax.broadcasted_iota(jnp.int32, (n, n), 1)).astype(F32)


def eliminate(matrix, *others):
    n = matrix.shape[0]
    eye = identity(n)
    whole = jnp.concatenate([matrix, eye, *others], axis=1)
    row_id = lax.broadcasted_iota(jnp.int32, (8, whole.shape[1]), 0)
    parts = [whole[8 * i : 8 * i + 8] for i in range(n // 8)]
    for k in range(n):
        home, at = divmod(k, 8)
        factors = [parts[i][:, k : k + 1] for i in range(home, n // 8)]
        scaled = parts[home][at : at + 1, :] * (1.0 / factors[0][at : at + 1, :])
        for i in range(home, n // 8):
            step = factors[i - home] * scaled
            if i == home:
                step = jnp.where(row_id > at, step, 0.0)
            parts[i] = parts[i] - step
    whole = jnp.concatenate(parts, axis=0)
    diag = jnp.sum(whole[:, :n] * eye, axis=1, keepdims=True)
    whole = whole * (1.0 / jnp.sqrt(diag))
    return [whole[:, n * i : n * i + n] for i in range(1, 2 + len(others))]


def kernel(
    count,
    block,
    labels,
    inv,
    out,
    ray_out,
    xin,
    lab,
    inv_s,
    xt,
    pq,
    sq,
    hb,
    ha,
    sa,
    qb,
    eta,
    eta_in,
    hs,
    hyb,
    hzm,
    ax,
    axm,
    tiles,
    plain_src,
    plain_1,
    plain_mid,
    plain_2,
    split_src,
    split_1,
    split_mid,
    split_2,
    ct,
    in_sem,
    halo_s,
    halo_r,
    late_s,
    late_r,
    swap_s,
    swap_r,
    eta_s,
    eta_r,
    plain_s,
    plain_r,
    split_s,
    split_r,
):
    slabs = CX * CY * CZ
    chips = CX * CY
    s = lax.axis_index("slab")
    k = lax.axis_index("band")
    x = lax.rem(s, CX)
    y = lax.rem(lax.div(s, CX), CY)
    z = lax.div(s, chips)
    up = lax.rem(s + 1, slabs)
    down = lax.rem(s + slabs - 1, slabs)
    base = s - x - CX * y
    sibling = (s, 1 - k)
    plane = [
        base + CX * lax.rem(y + i, CY) + lax.rem(x + j, CX)
        for i in range(CY)
        for j in range(CX)
        if (i, j) != (0, 0)
    ]
    column = [s - chips * z + chips * lax.rem(z + i, CZ) for i in range(1, CZ)]
    plane_both = [(chip, c) for chip in plane for c in range(2)]
    column_both = [(chip, c) for chip in column for c in range(2)]
    mine = pl.multiple_of(16 * k, 16)
    theirs = pl.multiple_of(16 * (1 - k), 16)
    own = pl.ds(mine, 16)

    order = (2, 4, 1, 3, 5, 0)
    loads = {
        cp: pltpu.make_async_copy(
            block.at[:, pl.ds(32 * cp, 32)],
            xin.reshape(16, 192, 128).at[:, pl.ds(32 * cp, 32)],
            in_sem.at[cp],
        )
        for cp in order
    }
    for cp in order:
        loads[cp].start()
    label_load = pltpu.make_async_copy(labels, lab, in_sem.at[6])
    label_load.start()
    inv_load = pltpu.make_async_copy(inv, inv_s, in_sem.at[7])
    inv_load.start()

    barrier = pltpu.get_barrier_semaphore()
    greeted = [(down, 0), (down, 1), (up, 0), (up, 1), sibling] + plane_both + column_both
    for to in greeted:
        pl.semaphore_signal(barrier, inc=1, device_id=to, device_id_type=MESH)

    def turn(parts):
        def body(row, carry):
            for cp in parts:
                c, p = divmod(cp, 2)
                xt[p * 3 + c, row + 1, own] = xin[pl.ds(cp * 32 + row, 16, stride=192), :]
            return carry

        for cp in parts:
            loads[cp].wait()
        lax.fori_loop(0, 32, body, 0, unroll=4)
        for cp in parts:
            c, p = divmod(cp, 2)
            xt[p * 3 + c, 0, own] = xt[p * 3 + c, 32, own]
            xt[p * 3 + c, 33, own] = xt[p * 3 + c, 1, own]
            xt[p * 3 + c, 34, own] = xt[p * 3 + c, 2, own]

    def halo(d, src, dst, to_slab):
        copies = []
        for n in range(PIECES):
            for to in range(2):
                rows = pl.ds(PIECE * n + 1, PIECE)
                from_rows = pl.ds(16 * to + PIECE * n + 1, PIECE)
                copies.append(
                    remote(
                        src(2, from_rows),
                        dst.at[:, rows, own],
                        halo_s.at[d, n, to],
                        halo_r.at[d, n, k],
                        (to_slab, to),
                    )
                )
                if n == 0:
                    copies.append(
                        remote(
                            src(1, pl.ds(16 * to, 1)),
                            dst.at[pl.ds(0, 1), pl.ds(0, 1), own],
                            halo_s.at[d, PIECES, to],
                            halo_r.at[d, PIECES, k],
                            (to_slab, to),
                        )
                    )
        for c in copies:
            c.start()
        return copies

    turn((2, 4))
    pl.semaphore_wait(barrier, len(greeted))
    sends = halo(0, lambda n, rows: xt.at[pl.ds(1, n), rows, own], ha, down)

    turn((1, 3, 5))

    def above(row, carry):
        ex = xt[3, row, own]
        pq[0, row] = xt[4, row, own] + (xt[3, row + 1, own] - ex)
        pq[1, row] = (rf(ex) - ex) + xt[5, row, own]
        return carry

    lax.fori_loop(0, 33, above, 0, unroll=3)
    sends += halo(1, lambda n, rows: pq.at[pl.ds(0, n), rows], hb, up)

    turn((0,))
    swap = remote(xt.at[:, :, own], xt.at[:, :, own], swap_s.at[0], swap_r.at[0], sibling)
    swap.start()
    sends.append(swap)

    label_load.wait()
    inv_load.wait()
    for p in range(2):
        regions = lab[p]
        value = jnp.zeros(regions.shape, F32)
        for r in range(3):
            value = value + jnp.where(regions == r, 1.0, 0.0) * inv_s[r]
        eta[p, 1:33] = value
        eta[p, 0:1] = value[31:32]
        eta[p, 33:40] = value[0:7]
    eta_copy = remote(eta.at[1], eta_in, eta_s.at[0], eta_r.at[0], (up, k))
    eta_copy.start()
    sends.append(eta_copy)

    def curl_x(p, row):
        ey = xt[3 * p + 1, row, own]
        return eta[p, pl.ds(row, 1), :] * (
            (xt[3 * p + 2, row + 1, own] - xt[3 * p + 2, row, own]) - (rf(ey) - ey)
        )

    def late(row, before):
        ea = eta[0, pl.ds(row, 1), :]
        ex, ey, ez = xt[0, row, own], xt[1, row, own], xt[2, row, own]
        now = curl_x(0, row)
        hy = ea * ((rf(ex) - ex) - (xt[5, row, own] - ez))
        hz = ea * ((xt[4, row, own] - ey) - (xt[0, row + 1, own] - ex))
        sq[0, row - 1] = hy - (now - before)
        hx = curl_x(1, row)
        sq[1, row - 1] = (hx - rb(hx)) + hz
        return now

    lax.fori_loop(1, 33, late, curl_x(0, 0))
    for d, to_slab, dst in ((0, down, sa), (1, up, qb)):
        for to in range(2):
            c = remote(
                sq.at[d, pl.ds(16 * to, 16)],
                dst.at[:, own],
                late_s.at[d, to],
                late_r.at[d, k],
                (to_slab, to),
            )
            c.start()
            sends.append(c)

    def plain_first(i, value):
        plain_src[i] = value
        for j, chip in enumerate(plane):
            c = remote(
                plain_src.at[i],
                plain_1.at[i, y * CX + x],
                plain_s.at[i, j],
                plain_r.at[i, j],
                (chip, k),
            )
            c.start()
            sends.append(c)
        plain_1[i, y * CX + x] = value

    def plain_second(i):
        for j in range(len(plane)):
            remote(
                plain_src.at[i], plain_1.at[i, 0], plain_s.at[i, j], plain_r.at[i, j], sibling
            ).wait_recv()
        value = plain_1[i, 0]
        for j in range(1, chips):
            value = value + plain_1[i, j]
        plain_mid[i] = value
        off = len(plane)
        for j, to in enumerate(column_both + [sibling]):
            at = off + j
            from_at = off + j if j == len(column_both) else off + (j // 2) * 2 + k
            c = remote(
                plain_mid.at[i],
                plain_2.at[i, z * 2 + k],
                plain_s.at[i, at],
                plain_r.at[i, from_at],
                to,
            )
            c.start()
            sends.append(c)
        plain_2[i, z * 2 + k] = value

    def plain_end(i):
        for j in range(len(plane), len(plane) + len(column_both) + 1):
            remote(
                plain_mid.at[i], plain_2.at[i, 0], plain_s.at[i, j], plain_r.at[i, j], sibling
            ).wait_recv()
        value = plain_2[i, 0]
        for j in range(1, 2 * CZ):
            value = value + plain_2[i, j]
        return unpack(value * (1.0 / count))

    swap.wait_recv()

    def put(t, at, values):
        hi, lo = (jnp.concatenate(v, axis=1) for v in zip(*(split(v) for v in values)))
        tiles[t, at : at + 32] = hi
        tiles[t, at + 64 : at + 96] = lo
        return hi, lo

    def first_gram(row, total):
        for r in range(0, 6, 2):
            both = jnp.concatenate(
                put((mine + row) * 3 + r // 2, 0, [xt[r + q, mine + row + 1] for q in range(2)]),
                axis=0,
            )
            total = total + lax.dot_general(both, both, NT, preferred_element_type=F32)
        return total

    total = lax.fori_loop(0, 16, first_gram, jnp.zeros((64, 64), F32))
    total = total[:, :32] + total[:, 32:]
    plain_first(0, pack(total[:32] + total[32:]))

    def inside(row, carry):
        at = mine + row
        ea, eb = eta[0, pl.ds(at, 1), :], eta[1, pl.ds(at, 1), :]
        ex, ey, ez = xt[0, at], xt[1, at], xt[2, at]
        fy, fz = xt[4, at], xt[5, at]
        hs[0, row] = ea * ((xt[2, at + 1] - ez) - (rf(ey) - ey))
        hs[1, row] = ea * ((rf(ex) - ex) - (fz - ez))
        hs[2, row] = ea * ((fy - ey) - (xt[0, at + 1] - ex))
        hs[3, row] = eb * ((xt[5, at + 1] - fz) - (rf(fy) - fy))
        return carry

    lax.fori_loop(0, 17, inside, 0)

    def other_block(row, carry):
        for r in range(0, 6, 2):
            put((theirs + row) * 3 + r // 2, 0, [xt[r + q, theirs + row + 1] for q in range(2)])
        return carry

    lax.fori_loop(0, 16, other_block, 0)
    eta_copy.wait_recv()

    def last_z(row):
        at = mine + row
        hz = eta[1, pl.ds(at, 1), :] * ((ha[0, row] - xt[4, at]) - (xt[3, at + 1] - xt[3, at]))
        mz = eta_in[pl.ds(at, 1), :] * (xt[1, at] - hb[0, row])
        return hz, mz

    def image(row, carry):
        hz_old, mz_old = carry
        at = mine + row
        to = mine + row - 1
        hz, mz = last_z(row)
        ex = xt[3, at]
        hy = eta[1, pl.ds(at, 1), :] * ((rf(ex) - ex) - (ha[1, row] - xt[5, at]))
        my = eta_in[pl.ds(at, 1), :] * (hb[1, row] - xt[2, at])
        hyb[row] = hy
        hzm[row] = mz
        ax_, ay_, az_, bx_ = hs[0, row], hs[1, row], hs[2, row], hs[3, row]
        ax[0, to] = 0.25 * ((az_ - hs[2, row - 1]) - (ay_ - rb(ay_)))
        ax[1, to] = 0.25 * ((ax_ - rb(ax_)) - (az_ - mz))
        ax[2, to] = 0.25 * ((ay_ - my) - (ax_ - hs[0, row - 1]))
        ax[3, to] = 0.25 * ((hz - hz_old) - (hy - rb(hy)))
        ax[4, to] = 0.25 * ((bx_ - rb(bx_)) - (hz - az_))
        ax[5, to] = 0.25 * ((hy - ay_) - (bx_ - hs[3, row - 1]))
        axm[row - 1] = 0.25 * ((mz - mz_old) - (my - rb(my)))
        return hz, mz

    def products(row, total):
        at = mine + row - 1
        for r in range(0, 6, 2):
            t = at * 3 + r // 2
            right = jnp.concatenate(put(t, 32, [ax[r + q, at] for q in range(2)]), axis=0)
            total = total + lax.dot_general(tiles[t], right, NT, preferred_element_type=F32)
        return total

    total = jnp.zeros((128, 64), F32)
    carry = None
    swaps = []
    for n in range(PIECES):
        for d, dst in enumerate((ha, hb)):
            for c in range(2):
                arrived = dst.at[:, pl.ds(PIECE * n + 1, PIECE), pl.ds(16 * c, 16)]
                remote(
                    arrived, arrived, halo_s.at[d, n, c], halo_r.at[d, n, c], sibling
                ).wait_recv()
                if n == 0:
                    arrived = dst.at[pl.ds(0, 1), pl.ds(0, 1), pl.ds(16 * c, 16)]
                    remote(
                        arrived, arrived, halo_s.at[d, PIECES, c], halo_r.at[d, PIECES, c], sibling
                    ).wait_recv()
        if n == 0:
            carry = last_z(0)
        carry = lax.fori_loop(PIECE * n + 1, PIECE * n + PIECE + 1, image, carry)
        rows = pl.ds(mine + PIECE * n, PIECE)
        c = remote(ax.at[:, rows], ax.at[:, rows], swap_s.at[n + 1], swap_r.at[n + 1], sibling)
        c.start()
        swaps.append(c)
        if n == 0:
            c = remote(
                axm.at[0], axm.at[16], swap_s.at[PIECES + 1], swap_r.at[PIECES + 1], sibling
            )
            c.start()
            swaps.append(c)
        total = lax.fori_loop(PIECE * n + 1, PIECE * n + PIECE + 1, products, total)
        if n == 1:
            plain_second(0)
    sends += swaps

    total = total[:, :32] + total[:, 32:]
    total = total[:64] + total[64:]
    split_src[0] = pack(total[:32])
    split_src[1] = pack(total[32:])
    slot = (y * CX + x) * 2 + k
    for i, to in enumerate(plane_both + [sibling]):
        half = to[1]
        from_i = i if i == len(plane_both) else (i // 2) * 2 + k
        c = remote(
            split_src.at[half], split_1.at[slot], split_s.at[0, i], split_r.at[0, from_i], to
        )
        c.start()
        sends.append(c)
    split_1[slot] = split_src[k]

    g0 = plain_end(0)
    (inv11,) = eliminate(0.5 * (g0 + g0.T))

    for c in swaps:
        c.wait_recv()
    for r in range(6):
        ax[r, 32] = ax[r, 0]

    def other_image(row, carry):
        for r in range(0, 6, 2):
            put((theirs + row) * 3 + r // 2, 32, [ax[r + q, theirs + row] for q in range(2)])
        return carry

    lax.fori_loop(0, 16, other_image, 0)

    for i in range(len(plane_both) + 1):
        remote(
            split_src.at[0], split_1.at[0], split_s.at[0, i], split_r.at[0, i], sibling
        ).wait_recv()
    value = split_1[0]
    for i in range(1, 2 * chips):
        value = value + split_1[i]
    split_mid[...] = value
    for i, to in enumerate(column_both + [sibling]):
        from_i = i if i == len(column_both) else (i // 2) * 2 + k
        c = remote(split_mid, split_2.at[k, z], split_s.at[1, i], split_r.at[1, from_i], to)
        c.start()
        sends.append(c)
    split_2[k, z] = value

    for d, dst in enumerate((sa, qb)):
        for c in range(2):
            arrived = dst.at[:, pl.ds(16 * c, 16)]
            remote(
                arrived, arrived, late_s.at[d, c], late_r.at[d, c], sibling
            ).wait_recv()

    def third(row, acc):
        at = mine + row
        to = at - 1
        ea, eb = eta[0, pl.ds(at, 1), :], eta[1, pl.ds(at, 1), :]
        em = eta_in[pl.ds(at, 1), :]
        ux, uy, uz = ax[0, to], ax[1, to], ax[2, to]
        vx, vy, vz = ax[3, to], ax[4, to], ax[5, to]
        pz = 0.25 * (sa[row - 1] - hyb[row])
        my = 0.25 * (qb[row - 1] - hzm[row])
        curls = (
            (ea, (ax[2, to + 1] - uz) - (rf(uy) - uy)),
            (ea, (rf(ux) - ux) - (vz - uz)),
            (ea, (vy - uy) - (ax[0, to + 1] - ux)),
            (eb, (ax[5, to + 1] - vz) - (rf(vy) - vy)),
            (eb, (rf(vx) - vx) - (pz - vz)),
            (em, (uy - my) - (axm[row] - axm[row - 1])),
        )
        for i in range(0, 6, 2):
            left, right = [], []
            for e, v in curls[i : i + 2]:
                left.append(jnp.concatenate(split(v), axis=0))
                right.append(jnp.concatenate(split(e * v), axis=0))
            acc = acc + lax.dot_general(
                jnp.concatenate(left, axis=1),
                jnp.concatenate(right, axis=1),
                NT,
                preferred_element_type=F32,
            )
        return acc

    acc = lax.fori_loop(1, 17, third, jnp.zeros((64, 64), F32))
    acc = acc[:, :32] + acc[:, 32:]
    plain_first(1, pack(0.25 * (acc[:32] + acc[32:])))

    for i in range(len(column_both) + 1):
        remote(
            split_mid, split_2.at[0, 0], split_s.at[1, i], split_r.at[1, i], sibling
        ).wait_recv()
    halves = []
    for c in range(2):
        value = split_2[c, 0]
        for i in range(1, CZ):
            value = value + split_2[c, i]
        halves.append(unpack(value * (1.0 / count)))
    g1, g2 = halves
    g1t = g1.T
    g2 = 0.5 * (g2 + g2.T)
    top = jnp.concatenate([0.5 * (g1 + g1t), g2], axis=1)
    low21 = dot32(g1t, inv11, NT)
    inv22, inv21 = eliminate(g2 - dot32(low21, low21, NT), -dot32(low21, inv11, NN))
    inverse = jnp.concatenate(
        [
            jnp.concatenate([inv11, jnp.zeros((32, 32), F32)], axis=1),
            jnp.concatenate([inv21, inv22], axis=1),
        ],
        axis=0,
    )
    coeffs = dot32(dot32(dot32(inv11, top, NN), inverse, NT), inverse, NN)
    ct[...] = coeffs

    plain_second(1)
    own_h, own_l = split(ct[own, :])
    left = jnp.concatenate([own_h, own_l], axis=0)
    left = jnp.concatenate([left, left], axis=1)

    def fresh(row, carry):
        for r in range(0, 6, 2):
            res = lax.dot_general(
                left, tiles[row * 3 + r // 2], NN, preferred_element_type=F32
            )
            res = res[:16] + res[16:]
            for q in range(2):
                p, c = divmod(r + q, 3)
                out[pl.ds((c * 2 + p) * 32 + row, 16, stride=192), :] = res[
                    :, 128 * q : 128 * q + 128
                ]
        return carry

    lax.fori_loop(0, 32, fresh, 0, unroll=2)

    g3 = plain_end(1)
    proj = jnp.concatenate(
        [top, jnp.concatenate([g2, 0.5 * (g3 + g3.T)], axis=1)], axis=0
    )
    ray_out[...] = dot32(inverse, dot32(inverse, proj, NN), NT)
    for c in sends:
        c.wait_send()


def on_device(block, labels, inverse_eps):
    bands, comps, planes, ny, nz = block.shape
    count = comps * planes * CX * CY * CZ * ny * nz
    dma = pltpu.SemaphoreType.DMA
    vmem = pltpu.VMEM
    chips = CX * CY
    hbm = pl.BlockSpec(memory_space=pltpu.HBM)
    next_block, rayleigh = pl.pallas_call(
        functools.partial(kernel, count),
        out_shape=(
            jax.ShapeDtypeStruct((bands * comps * planes * ny, nz), F32),
            jax.ShapeDtypeStruct((64, 64), F32),
        ),
        in_specs=[hbm, hbm, hbm],
        out_specs=(
            pl.BlockSpec(memory_space=pltpu.VMEM),
            pl.BlockSpec(memory_space=pltpu.VMEM),
        ),
        scratch_shapes=[
            vmem((3072, 128), F32),
            vmem((2, 32, 128), jnp.int32),
            pltpu.SMEM((3,), F32),
            vmem((6, 35, 32, 128), F32),
            vmem((2, 33, 16, 128), F32),
            vmem((2, 32, 16, 128), F32),
            vmem((2, 17, 32, 128), F32),
            vmem((2, 17, 32, 128), F32),
            vmem((16, 32, 128), F32),
            vmem((16, 32, 128), F32),
            vmem((2, 40, 128), F32),
            vmem((40, 128), F32),
            vmem((4, 17, 32, 128), F32),
            vmem((17, 32, 128), F32),
            vmem((17, 32, 128), F32),
            vmem((6, 33, 32, 128), F32),
            vmem((17, 32, 128), F32),
            vmem((96, 128, 256), BF16),
            vmem((2, 8, 128), F32),
            vmem((2, chips, 8, 128), F32),
            vmem((2, 8, 128), F32),
            vmem((2, 2 * CZ, 8, 128), F32),
            vmem((2, 8, 128), F32),
            vmem((2 * chips, 8, 128), F32),
            vmem((8, 128), F32),
            vmem((2, CZ, 8, 128), F32),
            vmem((32, 64), F32),
            dma((8,)),
            dma((2, PIECES + 1, 2)),
            dma((2, PIECES + 1, 2)),
            dma((2, 2)),
            dma((2, 2)),
            dma((PIECES + 2,)),
            dma((PIECES + 2,)),
            dma((1,)),
            dma((1,)),
            dma((2, chips - 1 + 2 * CZ - 1)),
            dma((2, chips - 1 + 2 * CZ - 1)),
            dma((2, 2 * chips - 1)),
            dma((2, 2 * chips - 1)),
        ],
        compiler_params=pltpu.CompilerParams(
            collective_id=0, has_side_effects=True, vmem_limit_bytes=56 << 20
        ),
        name="subspace",
    )(block.reshape(bands, comps * planes * ny, nz), labels, inverse_eps)
    return next_block.reshape(block.shape), rayleigh


def solution(mesh):
    in_specs = (P("band", None, "slab", None, None), P("slab", None, None), P())
    out_specs = (P("band", None, "slab", None, None), P())
    return jax.shard_map(
        on_device, mesh=mesh, in_specs=in_specs, out_specs=out_specs, check_vma=False
    )
```

```python
import functools

import jax
import jax.numpy as jnp
from jax import lax
from jax.experimental import pallas as pl
from jax.experimental.pallas import tpu as pltpu
from jax.sharding import PartitionSpec as P

MESH = pl.DeviceIdType.MESH
F32 = jnp.float32
BF16 = jnp.bfloat16
CX, CY, CZ = 4, 4, 8
PIECE = 4
PIECES = 16 // PIECE
NT = (((1,), (1,)), ((), ()))
NN = (((1,), (0,)), ((), ()))


def rf(v):
    return pltpu.roll(v, v.shape[-1] - 1, v.ndim - 1)


def rb(v):
    return pltpu.roll(v, 1, v.ndim - 1)


def split(v):
    hi = v.astype(BF16)
    return hi, (v - hi.astype(F32)).astype(BF16)


def dot32(a, b, dims):
    return lax.dot_general(
        a, b, dims, precision=lax.Precision.HIGHEST, preferred_element_type=F32
    )


def remote(src, dst, send, recv, to):
    return pltpu.make_async_remote_copy(
        src_ref=src, dst_ref=dst, send_sem=send, recv_sem=recv, device_id=to, device_id_type=MESH
    )


def pack(m):
    return jnp.concatenate([m[8 * i : 8 * i + 8] for i in range(4)], axis=1)


def unpack(v):
    return jnp.concatenate([v[:, 32 * i : 32 * i + 32] for i in range(4)], axis=0)


def identity(n):
    rows = lax.broadcasted_iota(jnp.int32, (n, n), 0)
    return (rows == lax.broadcasted_iota(jnp.int32, (n, n), 1)).astype(F32)


def eliminate(matrix, *others):
    n = matrix.shape[0]
    eye = identity(n)
    whole = jnp.concatenate([matrix, eye, *others], axis=1)
    shape = (8, whole.shape[1])
    row_id = lax.broadcasted_iota(jnp.int32, shape, 0)
    parts = [whole[8 * i : 8 * i + 8] for i in range(n // 8)]
    for k in range(0, n, 2):
        home, at = divmod(k, 8)
        f0 = [jnp.broadcast_to(part[:, k : k + 1], shape) for part in parts[home:]]
        f1 = [jnp.broadcast_to(part[:, k + 1 : k + 2], shape) for part in parts[home:]]
        a, b = f0[0][at : at + 1], f0[0][at + 1 : at + 2]
        bt, c = f1[0][at : at + 1], f1[0][at + 1 : at + 2]
        r0, r1 = parts[home][at : at + 1], parts[home][at + 1 : at + 2]
        u0, u1 = c * r0 - bt * r1, a * r1 - b * r0
        scale = 1.0 / (a * c - b * bt)
        t0, t1 = u0 * scale, u1 * scale
        second = u1 * (1.0 / a)
        for i in range(home, n // 8):
            new = parts[i] - (f0[i - home] * t0 + f1[i - home] * t1)
            if i == home:
                kept = jnp.where(row_id == at + 1, second, parts[i])
                new = jnp.where(row_id > at + 1, new, kept)
            parts[i] = new
    whole = jnp.concatenate(parts, axis=0)
    diag = jnp.sum(whole[:, :n] * eye, axis=1, keepdims=True)
    whole = whole * (1.0 / jnp.sqrt(diag))
    return [whole[:, n * i : n * i + n] for i in range(1, 2 + len(others))]


def kernel(
    count,
    block,
    labels,
    inv,
    out,
    ray_out,
    xin,
    lab,
    inv_s,
    xt,
    pq,
    sq,
    hb,
    ha,
    sa,
    qb,
    eta,
    eta_in,
    hs,
    hyb,
    hzm,
    ax,
    axm,
    tiles,
    plain_src,
    plain_1,
    plain_mid,
    plain_2,
    split_src,
    split_1,
    split_mid,
    split_2,
    ct,
    in_sem,
    halo_s,
    halo_r,
    late_s,
    late_r,
    swap_s,
    swap_r,
    eta_s,
    eta_r,
    plain_s,
    plain_r,
    split_s,
    split_r,
):
    slabs = CX * CY * CZ
    chips = CX * CY
    s = lax.axis_index("slab")
    k = lax.axis_index("band")
    x = lax.rem(s, CX)
    y = lax.rem(lax.div(s, CX), CY)
    z = lax.div(s, chips)
    up = lax.rem(s + 1, slabs)
    down = lax.rem(s + slabs - 1, slabs)
    base = s - x - CX * y
    sibling = (s, 1 - k)
    plane = [
        base + CX * lax.rem(y + i, CY) + lax.rem(x + j, CX)
        for i in range(CY)
        for j in range(CX)
        if (i, j) != (0, 0)
    ]
    column = [s - chips * z + chips * lax.rem(z + i, CZ) for i in range(1, CZ)]
    plane_both = [(chip, c) for chip in plane for c in range(2)]
    column_both = [(chip, c) for chip in column for c in range(2)]
    mine = pl.multiple_of(16 * k, 16)
    theirs = pl.multiple_of(16 * (1 - k), 16)
    own = pl.ds(mine, 16)

    order = (2, 4, 1, 3, 5, 0)
    loads = {
        cp: pltpu.make_async_copy(
            block.at[:, pl.ds(32 * cp, 32)],
            xin.reshape(16, 192, 128).at[:, pl.ds(32 * cp, 32)],
            in_sem.at[cp],
        )
        for cp in order
    }
    for cp in order:
        loads[cp].start()
    label_load = pltpu.make_async_copy(labels, lab, in_sem.at[6])
    label_load.start()
    inv_load = pltpu.make_async_copy(inv, inv_s, in_sem.at[7])
    inv_load.start()

    barrier = pltpu.get_barrier_semaphore()
    greeted = [(down, 0), (down, 1), (up, 0), (up, 1), sibling] + plane_both + column_both
    for to in greeted:
        pl.semaphore_signal(barrier, inc=1, device_id=to, device_id_type=MESH)

    def turn(parts):
        def body(row, carry):
            for cp in parts:
                c, p = divmod(cp, 2)
                xt[p * 3 + c, row + 1, own] = xin[pl.ds(cp * 32 + row, 16, stride=192), :]
            return carry

        for cp in parts:
            loads[cp].wait()
        lax.fori_loop(0, 32, body, 0, unroll=4)
        for cp in parts:
            c, p = divmod(cp, 2)
            xt[p * 3 + c, 0, own] = xt[p * 3 + c, 32, own]
            xt[p * 3 + c, 33, own] = xt[p * 3 + c, 1, own]
            xt[p * 3 + c, 34, own] = xt[p * 3 + c, 2, own]

    def halo(d, src, dst, to_slab):
        copies = []
        for n in range(PIECES):
            for to in range(2):
                rows = pl.ds(PIECE * n + 1, PIECE)
                from_rows = pl.ds(16 * to + PIECE * n + 1, PIECE)
                copies.append(
                    remote(
                        src(2, from_rows),
                        dst.at[:, rows, own],
                        halo_s.at[d, n, to],
                        halo_r.at[d, n, k],
                        (to_slab, to),
                    )
                )
                if n == 0:
                    copies.append(
                        remote(
                            src(1, pl.ds(16 * to, 1)),
                            dst.at[pl.ds(0, 1), pl.ds(0, 1), own],
                            halo_s.at[d, PIECES, to],
                            halo_r.at[d, PIECES, k],
                            (to_slab, to),
                        )
                    )
        for c in copies:
            c.start()
        return copies

    turn((2, 4))
    pl.semaphore_wait(barrier, len(greeted))
    sends = halo(0, lambda n, rows: xt.at[pl.ds(1, n), rows, own], ha, down)

    turn((1, 3, 5))

    def above(row, carry):
        ex = xt[3, row, own]
        pq[0, row] = xt[4, row, own] + (xt[3, row + 1, own] - ex)
        pq[1, row] = (rf(ex) - ex) + xt[5, row, own]
        return carry

    lax.fori_loop(0, 33, above, 0, unroll=11)
    sends += halo(1, lambda n, rows: pq.at[pl.ds(0, n), rows], hb, up)

    turn((0,))
    swap = remote(xt.at[:, :, own], xt.at[:, :, own], swap_s.at[0], swap_r.at[0], sibling)
    swap.start()
    sends.append(swap)

    label_load.wait()
    inv_load.wait()
    for p in range(2):
        regions = lab[p]
        value = jnp.zeros(regions.shape, F32)
        for r in range(3):
            value = value + jnp.where(regions == r, 1.0, 0.0) * inv_s[r]
        eta[p, 1:33] = value
        eta[p, 0:1] = value[31:32]
        eta[p, 33:40] = value[0:7]
    eta_copy = remote(eta.at[1], eta_in, eta_s.at[0], eta_r.at[0], (up, k))
    eta_copy.start()
    sends.append(eta_copy)

    def curl_x(p, row):
        ey = xt[3 * p + 1, row, own]
        return eta[p, pl.ds(row, 1), :] * (
            (xt[3 * p + 2, row + 1, own] - xt[3 * p + 2, row, own]) - (rf(ey) - ey)
        )

    def late(row, before):
        ea = eta[0, pl.ds(row, 1), :]
        ex, ey, ez = xt[0, row, own], xt[1, row, own], xt[2, row, own]
        now = curl_x(0, row)
        hy = ea * ((rf(ex) - ex) - (xt[5, row, own] - ez))
        hz = ea * ((xt[4, row, own] - ey) - (xt[0, row + 1, own] - ex))
        sq[0, row - 1] = hy - (now - before)
        hx = curl_x(1, row)
        sq[1, row - 1] = (hx - rb(hx)) + hz
        return now

    lax.fori_loop(1, 33, late, curl_x(0, 0), unroll=4)
    for d, to_slab, dst in ((0, down, sa), (1, up, qb)):
        for to in range(2):
            c = remote(
                sq.at[d, pl.ds(16 * to, 16)],
                dst.at[:, own],
                late_s.at[d, to],
                late_r.at[d, k],
                (to_slab, to),
            )
            c.start()
            sends.append(c)

    around = column_both + [sibling]

    def plain_first(i, value):
        plain_src[i] = value
        for j, to in enumerate(around):
            from_j = j if j == len(column_both) else (j // 2) * 2 + k
            c = remote(
                plain_src.at[i],
                plain_1.at[i, z * 2 + k],
                plain_s.at[i, j],
                plain_r.at[i, from_j],
                to,
            )
            c.start()
            sends.append(c)
        plain_1[i, z * 2 + k] = value

    def plain_second(i):
        for j in range(len(around)):
            remote(
                plain_src.at[i], plain_1.at[i, 0], plain_s.at[i, j], plain_r.at[i, j], sibling
            ).wait_recv()
        value = plain_1[i, 0]
        for j in range(1, 2 * CZ):
            value = value + plain_1[i, j]
        plain_mid[i] = value
        for j, chip in enumerate(plane):
            at = len(around) + j
            c = remote(
                plain_mid.at[i],
                plain_2.at[i, y * CX + x],
                plain_s.at[i, at],
                plain_r.at[i, at],
                (chip, k),
            )
            c.start()
            sends.append(c)
        plain_2[i, y * CX + x] = value

    def plain_end(i):
        for j in range(len(around), len(around) + len(plane)):
            remote(
                plain_mid.at[i], plain_2.at[i, 0], plain_s.at[i, j], plain_r.at[i, j], sibling
            ).wait_recv()
        value = plain_2[i, 0]
        for j in range(1, chips):
            value = value + plain_2[i, j]
        return unpack(value * (1.0 / count))

    swap.wait_recv()

    def put(t, at, values):
        hi, lo = (jnp.concatenate(v, axis=1) for v in zip(*(split(v) for v in values)))
        tiles[t, at : at + 32] = hi
        tiles[t, at + 64 : at + 96] = lo
        return hi, lo

    def first_gram(row, total):
        for r in range(0, 6, 2):
            both = jnp.concatenate(
                put((mine + row) * 3 + r // 2, 0, [xt[r + q, mine + row + 1] for q in range(2)]),
                axis=0,
            )
            total = total + lax.dot_general(both, both, NT, preferred_element_type=F32)
        return total

    total = lax.fori_loop(0, 16, first_gram, jnp.zeros((64, 64), F32), unroll=4)
    total = total[:, :32] + total[:, 32:]
    plain_first(0, pack(total[:32] + total[32:]))

    def inside(row, carry):
        at = mine + row
        ea, eb = eta[0, pl.ds(at, 1), :], eta[1, pl.ds(at, 1), :]
        ex, ey, ez = xt[0, at], xt[1, at], xt[2, at]
        fy, fz = xt[4, at], xt[5, at]
        hs[0, row] = ea * ((xt[2, at + 1] - ez) - (rf(ey) - ey))
        hs[1, row] = ea * ((rf(ex) - ex) - (fz - ez))
        hs[2, row] = ea * ((fy - ey) - (xt[0, at + 1] - ex))
        hs[3, row] = eb * ((xt[5, at + 1] - fz) - (rf(fy) - fy))
        return carry

    inside(0, 0)
    lax.fori_loop(1, 17, inside, 0, unroll=4)

    def other_block(row, carry):
        for r in range(0, 6, 2):
            put((theirs + row) * 3 + r // 2, 0, [xt[r + q, theirs + row + 1] for q in range(2)])
        return carry

    lax.fori_loop(0, 16, other_block, 0, unroll=4)
    eta_copy.wait_recv()

    def last_z(row):
        at = mine + row
        hz = eta[1, pl.ds(at, 1), :] * ((ha[0, row] - xt[4, at]) - (xt[3, at + 1] - xt[3, at]))
        mz = eta_in[pl.ds(at, 1), :] * (xt[1, at] - hb[0, row])
        return hz, mz

    def image(row, carry):
        hz_old, mz_old = carry
        at = mine + row
        to = mine + row - 1
        hz, mz = last_z(row)
        ex = xt[3, at]
        hy = eta[1, pl.ds(at, 1), :] * ((rf(ex) - ex) - (ha[1, row] - xt[5, at]))
        my = eta_in[pl.ds(at, 1), :] * (hb[1, row] - xt[2, at])
        hyb[row] = hy
        hzm[row] = mz
        ax_, ay_, az_, bx_ = hs[0, row], hs[1, row], hs[2, row], hs[3, row]
        ax[0, to] = 0.25 * ((az_ - hs[2, row - 1]) - (ay_ - rb(ay_)))
        ax[1, to] = 0.25 * ((ax_ - rb(ax_)) - (az_ - mz))
        ax[2, to] = 0.25 * ((ay_ - my) - (ax_ - hs[0, row - 1]))
        ax[3, to] = 0.25 * ((hz - hz_old) - (hy - rb(hy)))
        ax[4, to] = 0.25 * ((bx_ - rb(bx_)) - (hz - az_))
        ax[5, to] = 0.25 * ((hy - ay_) - (bx_ - hs[3, row - 1]))
        axm[row - 1] = 0.25 * ((mz - mz_old) - (my - rb(my)))
        return hz, mz

    def products(row, total):
        at = mine + row - 1
        for r in range(0, 6, 2):
            t = at * 3 + r // 2
            right = jnp.concatenate(put(t, 32, [ax[r + q, at] for q in range(2)]), axis=0)
            total = total + lax.dot_general(tiles[t], right, NT, preferred_element_type=F32)
        return total

    total = jnp.zeros((128, 64), F32)
    carry = None
    swaps = []
    for n in range(PIECES):
        for d, dst in enumerate((ha, hb)):
            for c in range(2):
                arrived = dst.at[:, pl.ds(PIECE * n + 1, PIECE), pl.ds(16 * c, 16)]
                remote(
                    arrived, arrived, halo_s.at[d, n, c], halo_r.at[d, n, c], sibling
                ).wait_recv()
                if n == 0:
                    arrived = dst.at[pl.ds(0, 1), pl.ds(0, 1), pl.ds(16 * c, 16)]
                    remote(
                        arrived, arrived, halo_s.at[d, PIECES, c], halo_r.at[d, PIECES, c], sibling
                    ).wait_recv()
        if n == 0:
            carry = last_z(0)
        carry = lax.fori_loop(PIECE * n + 1, PIECE * n + PIECE + 1, image, carry, unroll=4)
        rows = pl.ds(mine + PIECE * n, PIECE)
        c = remote(ax.at[:, rows], ax.at[:, rows], swap_s.at[n + 1], swap_r.at[n + 1], sibling)
        c.start()
        swaps.append(c)
        if n == 0:
            c = remote(
                axm.at[0], axm.at[16], swap_s.at[PIECES + 1], swap_r.at[PIECES + 1], sibling
            )
            c.start()
            swaps.append(c)
        total = lax.fori_loop(PIECE * n + 1, PIECE * n + PIECE + 1, products, total, unroll=4)
    sends += swaps

    total = total[:, :32] + total[:, 32:]
    total = total[:64] + total[64:]
    split_src[0] = pack(total[:32])
    split_src[1] = pack(total[32:])
    for i, to in enumerate(around):
        from_i = i if i == len(column_both) else (i // 2) * 2 + k
        c = remote(
            split_src.at[to[1]],
            split_1.at[z * 2 + k],
            split_s.at[0, i],
            split_r.at[0, from_i],
            to,
        )
        c.start()
        sends.append(c)
    split_1[z * 2 + k] = split_src[k]
    plain_second(0)

    for c in swaps:
        c.wait_recv()
    for r in range(6):
        ax[r, 32] = ax[r, 0]

    def other_image(row, carry):
        for r in range(0, 6, 2):
            put((theirs + row) * 3 + r // 2, 32, [ax[r + q, theirs + row] for q in range(2)])
        return carry

    lax.fori_loop(0, 16, other_image, 0, unroll=4)

    for i in range(len(around)):
        remote(
            split_src.at[0], split_1.at[0], split_s.at[0, i], split_r.at[0, i], sibling
        ).wait_recv()
    value = split_1[0]
    for i in range(1, 2 * CZ):
        value = value + split_1[i]
    split_mid[...] = value
    for i, to in enumerate(plane_both + [sibling]):
        from_i = i if i == len(plane_both) else (i // 2) * 2 + k
        c = remote(
            split_mid, split_2.at[k, y * CX + x], split_s.at[1, i], split_r.at[1, from_i], to
        )
        c.start()
        sends.append(c)
    split_2[k, y * CX + x] = value

    for d, dst in enumerate((sa, qb)):
        for c in range(2):
            arrived = dst.at[:, pl.ds(16 * c, 16)]
            remote(
                arrived, arrived, late_s.at[d, c], late_r.at[d, c], sibling
            ).wait_recv()

    def third(row, acc):
        at = mine + row
        to = at - 1
        ea, eb = eta[0, pl.ds(at, 1), :], eta[1, pl.ds(at, 1), :]
        em = eta_in[pl.ds(at, 1), :]
        ux, uy, uz = ax[0, to], ax[1, to], ax[2, to]
        vx, vy, vz = ax[3, to], ax[4, to], ax[5, to]
        pz = 0.25 * (sa[row - 1] - hyb[row])
        my = 0.25 * (qb[row - 1] - hzm[row])
        curls = (
            (ea, (ax[2, to + 1] - uz) - (rf(uy) - uy)),
            (ea, (rf(ux) - ux) - (vz - uz)),
            (ea, (vy - uy) - (ax[0, to + 1] - ux)),
            (eb, (ax[5, to + 1] - vz) - (rf(vy) - vy)),
            (eb, (rf(vx) - vx) - (pz - vz)),
            (em, (uy - my) - (axm[row] - axm[row - 1])),
        )
        for i in range(0, 6, 2):
            left, right = [], []
            for e, v in curls[i : i + 2]:
                left.append(jnp.concatenate(split(v), axis=0))
                right.append(jnp.concatenate(split(e * v), axis=0))
            acc = acc + lax.dot_general(
                jnp.concatenate(left, axis=1),
                jnp.concatenate(right, axis=1),
                NT,
                preferred_element_type=F32,
            )
        return acc

    acc = lax.fori_loop(1, 17, third, jnp.zeros((64, 64), F32), unroll=4)
    acc = acc[:, :32] + acc[:, 32:]
    plain_first(1, pack(0.25 * (acc[:32] + acc[32:])))

    g0 = plain_end(0)
    (inv11,) = eliminate(0.5 * (g0 + g0.T))

    for i in range(len(plane_both) + 1):
        remote(
            split_mid, split_2.at[0, 0], split_s.at[1, i], split_r.at[1, i], sibling
        ).wait_recv()
    halves = []
    for c in range(2):
        value = split_2[c, 0]
        for i in range(1, chips):
            value = value + split_2[c, i]
        halves.append(unpack(value * (1.0 / count)))
    plain_second(1)
    g1, g2 = halves
    g1t = g1.T
    g2 = 0.5 * (g2 + g2.T)
    top = jnp.concatenate([0.5 * (g1 + g1t), g2], axis=1)
    low21 = dot32(g1t, inv11, NT)
    inv22, inv21 = eliminate(g2 - dot32(low21, low21, NT), -dot32(low21, inv11, NN))
    inverse = jnp.concatenate(
        [
            jnp.concatenate([inv11, jnp.zeros((32, 32), F32)], axis=1),
            jnp.concatenate([inv21, inv22], axis=1),
        ],
        axis=0,
    )
    coeffs = dot32(dot32(dot32(inv11, top, NN), inverse, NT), inverse, NN)
    ct[...] = coeffs

    own_h, own_l = split(ct[own, :])
    left = jnp.concatenate([own_h, own_l], axis=0)
    left = jnp.concatenate([left, left], axis=1)

    def fresh(row, carry):
        for r in range(0, 6, 2):
            res = lax.dot_general(
                left, tiles[row * 3 + r // 2], NN, preferred_element_type=F32
            )
            res = res[:16] + res[16:]
            for q in range(2):
                p, c = divmod(r + q, 3)
                out[pl.ds((c * 2 + p) * 32 + row, 16, stride=192), :] = res[
                    :, 128 * q : 128 * q + 128
                ]
        return carry

    lax.fori_loop(0, 32, fresh, 0, unroll=8)

    g3 = plain_end(1)
    proj = jnp.concatenate(
        [top, jnp.concatenate([g2, 0.5 * (g3 + g3.T)], axis=1)], axis=0
    )
    ray_out[...] = dot32(inverse, dot32(inverse, proj, NN), NT)
    for c in sends:
        c.wait_send()


def on_device(block, labels, inverse_eps):
    bands, comps, planes, ny, nz = block.shape
    count = comps * planes * CX * CY * CZ * ny * nz
    dma = pltpu.SemaphoreType.DMA
    vmem = pltpu.VMEM
    chips = CX * CY
    hbm = pl.BlockSpec(memory_space=pltpu.HBM)
    next_block, rayleigh = pl.pallas_call(
        functools.partial(kernel, count),
        out_shape=(
            jax.ShapeDtypeStruct((bands * comps * planes * ny, nz), F32),
            jax.ShapeDtypeStruct((64, 64), F32),
        ),
        in_specs=[hbm, hbm, hbm],
        out_specs=(
            pl.BlockSpec(memory_space=pltpu.VMEM),
            pl.BlockSpec(memory_space=pltpu.VMEM),
        ),
        scratch_shapes=[
            vmem((3072, 128), F32),
            vmem((2, 32, 128), jnp.int32),
            pltpu.SMEM((3,), F32),
            vmem((6, 35, 32, 128), F32),
            vmem((2, 33, 16, 128), F32),
            vmem((2, 32, 16, 128), F32),
            vmem((2, 17, 32, 128), F32),
            vmem((2, 17, 32, 128), F32),
            vmem((16, 32, 128), F32),
            vmem((16, 32, 128), F32),
            vmem((2, 40, 128), F32),
            vmem((40, 128), F32),
            vmem((4, 17, 32, 128), F32),
            vmem((17, 32, 128), F32),
            vmem((17, 32, 128), F32),
            vmem((6, 33, 32, 128), F32),
            vmem((17, 32, 128), F32),
            vmem((96, 128, 256), BF16),
            vmem((2, 8, 128), F32),
            vmem((2, 2 * CZ, 8, 128), F32),
            vmem((2, 8, 128), F32),
            vmem((2, chips, 8, 128), F32),
            vmem((2, 8, 128), F32),
            vmem((2 * CZ, 8, 128), F32),
            vmem((8, 128), F32),
            vmem((2, chips, 8, 128), F32),
            vmem((32, 64), F32),
            dma((8,)),
            dma((2, PIECES + 1, 2)),
            dma((2, PIECES + 1, 2)),
            dma((2, 2)),
            dma((2, 2)),
            dma((PIECES + 2,)),
            dma((PIECES + 2,)),
            dma((1,)),
            dma((1,)),
            dma((2, chips - 1 + 2 * CZ - 1)),
            dma((2, chips - 1 + 2 * CZ - 1)),
            dma((2, 2 * chips - 1)),
            dma((2, 2 * chips - 1)),
        ],
        compiler_params=pltpu.CompilerParams(
            collective_id=0, has_side_effects=True, vmem_limit_bytes=32 << 20
        ),
        name="subspace",
    )(
        *(
            pltpu.with_memory_space_constraint(a, pltpu.HBM)
            for a in (block.reshape(bands, comps * planes * ny, nz), labels, inverse_eps)
        )
    )
    return next_block.reshape(block.shape), rayleigh


def solution(mesh):
    in_specs = (P("band", None, "slab", None, None), P("slab", None, None), P())
    out_specs = (P("band", None, "slab", None, None), P())
    return jax.shard_map(
        on_device, mesh=mesh, in_specs=in_specs, out_specs=out_specs, check_vma=False
    )
```

```python
import functools

import jax
import jax.numpy as jnp
from jax import lax
from jax.experimental import pallas as pl
from jax.experimental.pallas import tpu as pltpu
from jax.sharding import PartitionSpec as P

MESH = pl.DeviceIdType.MESH
F32 = jnp.float32
BF16 = jnp.bfloat16
CX, CY, CZ = 4, 4, 8
PIECE = 4
PIECES = 16 // PIECE
LATE = ((0, 12), (12, 16))
NT = (((1,), (1,)), ((), ()))
NN = (((1,), (0,)), ((), ()))


def rf(v):
    return pltpu.roll(v, v.shape[-1] - 1, v.ndim - 1)


def rb(v):
    return pltpu.roll(v, 1, v.ndim - 1)


def split(v):
    hi = v.astype(BF16)
    return hi, (v - hi.astype(F32)).astype(BF16)


def dot32(a, b, dims):
    return lax.dot_general(
        a, b, dims, precision=lax.Precision.HIGHEST, preferred_element_type=F32
    )


def remote(src, dst, send, recv, to):
    return pltpu.make_async_remote_copy(
        src_ref=src, dst_ref=dst, send_sem=send, recv_sem=recv, device_id=to, device_id_type=MESH
    )


def pack(m):
    return jnp.concatenate([m[8 * i : 8 * i + 8] for i in range(4)], axis=1)


def unpack(v):
    return jnp.concatenate([v[:, 32 * i : 32 * i + 32] for i in range(4)], axis=0)


def identity(n):
    rows = lax.broadcasted_iota(jnp.int32, (n, n), 0)
    return (rows == lax.broadcasted_iota(jnp.int32, (n, n), 1)).astype(F32)


def eliminate(matrix, *others):
    n = matrix.shape[0]
    eye = identity(n)
    whole = jnp.concatenate([matrix, eye, *others], axis=1)
    shape = (8, whole.shape[1])
    row_id = lax.broadcasted_iota(jnp.int32, shape, 0)
    parts = [whole[8 * i : 8 * i + 8] for i in range(n // 8)]
    for k in range(0, n, 2):
        home, at = divmod(k, 8)
        f0 = [jnp.broadcast_to(part[:, k : k + 1], shape) for part in parts[home:]]
        f1 = [jnp.broadcast_to(part[:, k + 1 : k + 2], shape) for part in parts[home:]]
        a, b = f0[0][at : at + 1], f0[0][at + 1 : at + 2]
        bt, c = f1[0][at : at + 1], f1[0][at + 1 : at + 2]
        r0, r1 = parts[home][at : at + 1], parts[home][at + 1 : at + 2]
        u0, u1 = c * r0 - bt * r1, a * r1 - b * r0
        scale = 1.0 / (a * c - b * bt)
        t0, t1 = u0 * scale, u1 * scale
        second = u1 * (1.0 / a)
        for i in range(home, n // 8):
            new = parts[i] - (f0[i - home] * t0 + f1[i - home] * t1)
            if i == home:
                kept = jnp.where(row_id == at + 1, second, parts[i])
                new = jnp.where(row_id > at + 1, new, kept)
            parts[i] = new
    whole = jnp.concatenate(parts, axis=0)
    diag = jnp.sum(whole[:, :n] * eye, axis=1, keepdims=True)
    whole = whole * (1.0 / jnp.sqrt(diag))
    return [whole[:, n * i : n * i + n] for i in range(1, 2 + len(others))]


def kernel(
    count,
    block,
    labels,
    inv,
    out,
    ray_out,
    xin,
    lab,
    inv_s,
    xt,
    pq,
    sq,
    hb,
    ha,
    sa,
    qb,
    eta,
    eta_in,
    hs,
    hyb,
    hzm,
    ax,
    axm,
    tiles,
    plain_src,
    plain_1,
    plain_mid,
    plain_2,
    split_src,
    split_1,
    split_mid,
    split_2,
    ct,
    in_sem,
    halo_s,
    halo_r,
    late_s,
    late_r,
    swap_s,
    swap_r,
    eta_s,
    eta_r,
    sum_s,
    sum_r,
):
    slabs = CX * CY * CZ
    chips = CX * CY
    s = lax.axis_index("slab")
    k = lax.axis_index("band")
    x = lax.rem(s, CX)
    y = lax.rem(lax.div(s, CX), CY)
    z = lax.div(s, chips)
    up = lax.rem(s + 1, slabs)
    down = lax.rem(s + slabs - 1, slabs)
    base = s - x - CX * y
    sibling = (s, 1 - k)
    plane = [
        base + CX * lax.rem(y + i, CY) + lax.rem(x + j, CX)
        for i, j in sorted(
            ((i, j) for i in range(CY) for j in range(CX) if (i, j) != (0, 0)),
            key=lambda o: -(min(o[0], CY - o[0]) + min(o[1], CX - o[1])),
        )
    ]
    column = [
        s - chips * z + chips * lax.rem(z + i, CZ)
        for i in sorted(range(1, CZ), key=lambda o: -min(o, CZ - o))
    ]
    plane_both = [(chip, c) for chip in plane for c in range(2)] + [sibling]
    column_both = [(chip, c) for chip in column for c in range(2)] + [sibling]
    plane_own = [(chip, k) for chip in plane]
    mine = pl.multiple_of(16 * k, 16)
    theirs = pl.multiple_of(16 * (1 - k), 16)
    own = pl.ds(mine, 16)

    order = (2, 4, 1, 3, 5, 0)
    loads = {
        cp: pltpu.make_async_copy(
            block.at[:, pl.ds(32 * cp, 32)],
            xin.reshape(16, 192, 128).at[:, pl.ds(32 * cp, 32)],
            in_sem.at[cp],
        )
        for cp in order
    }
    for cp in order:
        loads[cp].start()
    label_load = pltpu.make_async_copy(labels, lab, in_sem.at[6])
    label_load.start()
    inv_load = pltpu.make_async_copy(inv, inv_s, in_sem.at[7])
    inv_load.start()

    barrier = pltpu.get_barrier_semaphore()
    greeted = [(down, 0), (down, 1), (up, 0), (up, 1)] + plane_both + column_both[:-1]
    for to in greeted:
        pl.semaphore_signal(barrier, inc=1, device_id=to, device_id_type=MESH)

    turned = set()

    def turn(cp, rows):
        c, p = divmod(cp, 2)
        r = p * 3 + c
        for row in rows:
            if (cp, row) not in turned:
                turned.add((cp, row))
                value = xin[pl.ds(cp * 32 + row, 16, stride=192), :]
                xt[r, row + 1, own] = value
                if row == 31:
                    xt[r, 0, own] = value
                if row < 2:
                    xt[r, row + 33, own] = value

    def piece(n):
        return [16 * to + PIECE * n + i for to in range(2) for i in range(PIECE)]

    def halo(d, n, src, step, dst, to_slab):
        copies = []
        for to in range(2):
            if n == 0:
                copies.append(
                    remote(
                        src(1, pl.ds(step * to, 1)),
                        dst.at[pl.ds(0, 1), pl.ds(0, 1), own],
                        halo_s.at[d, PIECES, to],
                        halo_r.at[d, PIECES],
                        (to_slab, to),
                    )
                )
            copies.append(
                remote(
                    src(2, pl.ds(step * to + PIECE * n + 1, PIECE)),
                    dst.at[:, pl.ds(PIECE * n + 1, PIECE), own],
                    halo_s.at[d, n, to],
                    halo_r.at[d, n],
                    (to_slab, to),
                )
            )
        for c in copies:
            c.start()
        return copies

    sends = []
    for n in range(PIECES):
        if n == 0:
            loads[2].wait()
            turn(2, (31, 15))
            loads[4].wait()
        turn(2, piece(n))
        turn(4, piece(n))
        if n == 0:
            pl.semaphore_wait(barrier, len(greeted))
        sends += halo(0, n, lambda m, rows: xt.at[pl.ds(1, m), rows, own], 16, ha, down)
        if n == 0:
            loads[1].wait()
            turn(1, range(32))
            loads[3].wait()
            turn(3, (31, 15))
            for to in range(2):
                row = 16 * to
                pq[0, 17 * to] = xt[4, row, own] + (xt[3, row + 1, own] - xt[3, row, own])
            loads[5].wait()
        turn(3, piece(n))
        turn(5, piece(n))
        for row in piece(n):
            ex = xt[3, row + 1, own]
            at = row + 1 + row // 16
            pq[0, at] = xt[4, row + 1, own] + (xt[3, row + 2, own] - ex)
            pq[1, at] = (rf(ex) - ex) + xt[5, row + 1, own]
        sends += halo(1, n, lambda m, rows: pq.at[pl.ds(0, m), rows], 17, hb, up)

    loads[0].wait()
    turn(0, range(32))
    swap = remote(xt.at[:, :, own], xt.at[:, :, own], swap_s.at[0], swap_r.at[0], sibling)
    swap.start()
    sends.append(swap)

    label_load.wait()
    inv_load.wait()
    for p in range(2):
        regions = lab[p]
        value = jnp.zeros(regions.shape, F32)
        for r in range(3):
            value = value + jnp.where(regions == r, 1.0, 0.0) * inv_s[r]
        eta[p, 1:33] = value
        eta[p, 0:1] = value[31:32]
        eta[p, 33:40] = value[0:7]
    eta_copy = remote(eta.at[1], eta_in, eta_s.at[0], eta_r.at[0], (up, k))
    eta_copy.start()
    sends.append(eta_copy)

    def curl_x(p, row):
        ey = xt[3 * p + 1, row, own]
        return eta[p, pl.ds(row, 1), :] * (
            (xt[3 * p + 2, row + 1, own] - xt[3 * p + 2, row, own]) - (rf(ey) - ey)
        )

    def late(row, before):
        ea = eta[0, pl.ds(row, 1), :]
        ex, ey, ez = xt[0, row, own], xt[1, row, own], xt[2, row, own]
        now = curl_x(0, row)
        hy = ea * ((rf(ex) - ex) - (xt[5, row, own] - ez))
        hz = ea * ((xt[4, row, own] - ey) - (xt[0, row + 1, own] - ex))
        sq[0, row - 1] = hy - (now - before)
        hx = curl_x(1, row)
        sq[1, row - 1] = (hx - rb(hx)) + hz
        return now

    lax.fori_loop(1, 33, late, curl_x(0, 0), unroll=4)
    for n, (lo, hi) in enumerate(LATE):
        for d, to_slab, dst in ((0, down, sa), (1, up, qb)):
            for to in range(2):
                c = remote(
                    sq.at[d, pl.ds(16 * to + lo, hi - lo)],
                    dst.at[pl.ds(lo, hi - lo), own],
                    late_s.at[d, n, to],
                    late_r.at[d, n],
                    (to_slab, to),
                )
                c.start()
                sends.append(c)

    def scatter(src, dst, send, recv, group):
        for to in group:
            remote(src(to[1]), dst, send, recv, to).start()

    def gathered(src, send, recv, group):
        part = src.at[pl.ds(0, len(group))]
        remote(part, part, send, recv, sibling).wait_recv()

    def total_of(ref):
        value = ref[0]
        for i in range(1, ref.shape[0]):
            value = value + ref[i]
        return value

    def plain_first(i, value):
        plain_src[i] = value
        at = z * 2 + k
        scatter(
            lambda _: plain_src.at[i], plain_1.at[i, at], sum_s.at[i, 0], sum_r.at[i, 0], column_both
        )
        plain_1[i, at] = value

    def plain_second(i):
        gathered(plain_1.at[i], sum_s.at[i, 0], sum_r.at[i, 0], column_both)
        value = total_of(plain_1.at[i])
        plain_mid[i] = value
        at = y * CX + x
        scatter(
            lambda _: plain_mid.at[i], plain_2.at[i, at], sum_s.at[i, 1], sum_r.at[i, 1], plane_own
        )
        plain_2[i, at] = value

    def plain_end(i):
        gathered(plain_2.at[i], sum_s.at[i, 1], sum_r.at[i, 1], plane_own)
        return unpack(total_of(plain_2.at[i]) * (1.0 / count))

    def sent(i, ref, phase, group):
        part = ref.at[pl.ds(0, len(group))]
        remote(part, part, sum_s.at[i, phase], sum_r.at[i, phase], sibling).wait_send()

    swap.wait_recv()

    def put(t, at, values):
        hi, lo = (jnp.concatenate(v, axis=1) for v in zip(*(split(v) for v in values)))
        tiles[t, at : at + 32] = hi
        tiles[t, at + 64 : at + 96] = lo
        return hi, lo

    def first_gram(row, total):
        for r in range(0, 6, 2):
            both = jnp.concatenate(
                put((mine + row) * 3 + r // 2, 0, [xt[r + q, mine + row + 1] for q in range(2)]),
                axis=0,
            )
            total = total + lax.dot_general(both, both, NT, preferred_element_type=F32)
        return total

    total = lax.fori_loop(0, 16, first_gram, jnp.zeros((64, 64), F32), unroll=4)
    total = total[:, :32] + total[:, 32:]
    plain_first(0, pack(total[:32] + total[32:]))

    def inside(row, carry):
        at = mine + row
        ea, eb = eta[0, pl.ds(at, 1), :], eta[1, pl.ds(at, 1), :]
        ex, ey, ez = xt[0, at], xt[1, at], xt[2, at]
        fy, fz = xt[4, at], xt[5, at]
        hs[0, row] = ea * ((xt[2, at + 1] - ez) - (rf(ey) - ey))
        hs[1, row] = ea * ((rf(ex) - ex) - (fz - ez))
        hs[2, row] = ea * ((fy - ey) - (xt[0, at + 1] - ex))
        hs[3, row] = eb * ((xt[5, at + 1] - fz) - (rf(fy) - fy))
        return carry

    inside(0, 0)
    lax.fori_loop(1, 17, inside, 0, unroll=4)

    def other_block(row, carry):
        for r in range(0, 6, 2):
            put((theirs + row) * 3 + r // 2, 0, [xt[r + q, theirs + row + 1] for q in range(2)])
        return carry

    lax.fori_loop(0, 16, other_block, 0, unroll=4)
    eta_copy.wait_recv()

    def last_z(row):
        at = mine + row
        hz = eta[1, pl.ds(at, 1), :] * ((ha[0, row] - xt[4, at]) - (xt[3, at + 1] - xt[3, at]))
        mz = eta_in[pl.ds(at, 1), :] * (xt[1, at] - hb[0, row])
        return hz, mz

    def image(row, carry):
        hz_old, mz_old = carry
        at = mine + row
        to = mine + row - 1
        hz, mz = last_z(row)
        ex = xt[3, at]
        hy = eta[1, pl.ds(at, 1), :] * ((rf(ex) - ex) - (ha[1, row] - xt[5, at]))
        my = eta_in[pl.ds(at, 1), :] * (hb[1, row] - xt[2, at])
        hyb[row] = hy
        hzm[row] = mz
        ax_, ay_, az_, bx_ = hs[0, row], hs[1, row], hs[2, row], hs[3, row]
        ax[0, to] = 0.25 * ((az_ - hs[2, row - 1]) - (ay_ - rb(ay_)))
        ax[1, to] = 0.25 * ((ax_ - rb(ax_)) - (az_ - mz))
        ax[2, to] = 0.25 * ((ay_ - my) - (ax_ - hs[0, row - 1]))
        ax[3, to] = 0.25 * ((hz - hz_old) - (hy - rb(hy)))
        ax[4, to] = 0.25 * ((bx_ - rb(bx_)) - (hz - az_))
        ax[5, to] = 0.25 * ((hy - ay_) - (bx_ - hs[3, row - 1]))
        axm[row - 1] = 0.25 * ((mz - mz_old) - (my - rb(my)))
        return hz, mz

    def products(row, total):
        at = mine + row - 1
        for r in range(0, 6, 2):
            t = at * 3 + r // 2
            right = jnp.concatenate(put(t, 32, [ax[r + q, at] for q in range(2)]), axis=0)
            total = total + lax.dot_general(tiles[t], right, NT, preferred_element_type=F32)
        return total

    total = jnp.zeros((128, 64), F32)
    carry = None
    swaps = []
    for n in range(PIECES):
        for d, dst in enumerate((ha, hb)):
            arrived = [(dst.at[:, pl.ds(PIECE * n + 1, PIECE)], n)]
            if n == 0:
                arrived.append((dst.at[pl.ds(0, 1), pl.ds(0, 1)], PIECES))
            for ref, i in arrived:
                remote(ref, ref, halo_s.at[d, i, 0], halo_r.at[d, i], sibling).wait_recv()
        if n == 0:
            carry = last_z(0)
        carry = lax.fori_loop(PIECE * n + 1, PIECE * n + PIECE + 1, image, carry, unroll=4)
        rows = pl.ds(mine + PIECE * n, PIECE)
        c = remote(ax.at[:, rows], ax.at[:, rows], swap_s.at[n + 1], swap_r.at[n + 1], sibling)
        c.start()
        swaps.append(c)
        if n == 0:
            c = remote(
                axm.at[0], axm.at[16], swap_s.at[PIECES + 1], swap_r.at[PIECES + 1], sibling
            )
            c.start()
            swaps.append(c)
        total = lax.fori_loop(PIECE * n + 1, PIECE * n + PIECE + 1, products, total, unroll=4)

    total = total[:, :32] + total[:, 32:]
    total = total[:64] + total[64:]
    split_src[0] = pack(total[:32])
    split_src[1] = pack(total[32:])
    at = z * 2 + k
    scatter(
        lambda c: split_src.at[c], split_1.at[at], sum_s.at[2, 0], sum_r.at[2, 0], column_both
    )
    split_1[at] = split_src[k]
    plain_second(0)

    for c in swaps:
        c.wait_recv()
    sends += swaps
    for r in range(6):
        ax[r, 32] = ax[r, 0]

    def other_image(row, carry):
        for r in range(0, 6, 2):
            put((theirs + row) * 3 + r // 2, 32, [ax[r + q, theirs + row] for q in range(2)])
        return carry

    lax.fori_loop(0, 16, other_image, 0, unroll=4)

    def third(row, acc):
        at = mine + row
        to = at - 1
        ea, eb = eta[0, pl.ds(at, 1), :], eta[1, pl.ds(at, 1), :]
        em = eta_in[pl.ds(at, 1), :]
        ux, uy, uz = ax[0, to], ax[1, to], ax[2, to]
        vx, vy, vz = ax[3, to], ax[4, to], ax[5, to]
        pz = 0.25 * (sa[row - 1] - hyb[row])
        my = 0.25 * (qb[row - 1] - hzm[row])
        curls = (
            (ea, (ax[2, to + 1] - uz) - (rf(uy) - uy)),
            (ea, (rf(ux) - ux) - (vz - uz)),
            (ea, (vy - uy) - (ax[0, to + 1] - ux)),
            (eb, (ax[5, to + 1] - vz) - (rf(vy) - vy)),
            (eb, (rf(vx) - vx) - (pz - vz)),
            (em, (uy - my) - (axm[row] - axm[row - 1])),
        )
        for i in range(0, 6, 2):
            left, right = [], []
            for e, v in curls[i : i + 2]:
                left.append(jnp.concatenate(split(v), axis=0))
                right.append(jnp.concatenate(split(e * v), axis=0))
            acc = acc + lax.dot_general(
                jnp.concatenate(left, axis=1),
                jnp.concatenate(right, axis=1),
                NT,
                preferred_element_type=F32,
            )
        return acc

    acc = jnp.zeros((64, 64), F32)
    for n, (lo, hi) in enumerate(LATE):
        if n == len(LATE) - 1:
            for c in sends:
                c.wait_send()
            gathered(split_1, sum_s.at[2, 0], sum_r.at[2, 0], column_both)
            value = total_of(split_1)
            split_mid[...] = value
            at = y * CX + x
            scatter(
                lambda _: split_mid, split_2.at[k, at], sum_s.at[2, 1], sum_r.at[2, 1], plane_both
            )
            split_2[k, at] = value
        for d, dst in enumerate((sa, qb)):
            ref = dst.at[pl.ds(lo, hi - lo)]
            remote(ref, ref, late_s.at[d, n, 0], late_r.at[d, n], sibling).wait_recv()
        acc = lax.fori_loop(lo + 1, hi + 1, third, acc, unroll=4)
    acc = acc[:, :32] + acc[:, 32:]
    plain_first(1, pack(0.25 * (acc[:32] + acc[32:])))

    g0 = plain_end(0)
    (inv11,) = eliminate(0.5 * (g0 + g0.T))

    part = split_2.reshape(2 * chips, 8, 128).at[pl.ds(0, len(plane_both))]
    remote(part, part, sum_s.at[2, 1], sum_r.at[2, 1], sibling).wait_recv()
    halves = [unpack(total_of(split_2.at[c]) * (1.0 / count)) for c in range(2)]
    plain_second(1)
    g1, g2 = halves
    g1t = g1.T
    g2 = 0.5 * (g2 + g2.T)
    top = jnp.concatenate([0.5 * (g1 + g1t), g2], axis=1)
    low21 = dot32(g1t, inv11, NT)
    inv22, inv21 = eliminate(g2 - dot32(low21, low21, NT), -dot32(low21, inv11, NN))
    inverse = jnp.concatenate(
        [
            jnp.concatenate([inv11, jnp.zeros((32, 32), F32)], axis=1),
            jnp.concatenate([inv21, inv22], axis=1),
        ],
        axis=0,
    )
    coeffs = dot32(dot32(dot32(inv11, top, NN), inverse, NT), inverse, NN)
    ct[...] = coeffs

    own_h, own_l = split(ct[own, :])
    left = jnp.concatenate([own_h, own_l], axis=0)
    left = jnp.concatenate([left, left], axis=1)

    def fresh(row, carry):
        for r in range(0, 6, 2):
            res = lax.dot_general(
                left, tiles[row * 3 + r // 2], NN, preferred_element_type=F32
            )
            res = res[:16] + res[16:]
            for q in range(2):
                p, c = divmod(r + q, 3)
                out[pl.ds((c * 2 + p) * 32 + row, 16, stride=192), :] = res[
                    :, 128 * q : 128 * q + 128
                ]
        return carry

    lax.fori_loop(0, 32, fresh, 0, unroll=8)

    sent(0, plain_1.at[0], 0, column_both)
    sent(0, plain_2.at[0], 1, plane_own)
    sent(1, plain_1.at[1], 0, column_both)
    sent(1, plain_2.at[1], 1, plane_own)
    sent(2, split_1, 0, column_both)
    sent(2, split_2.reshape(2 * chips, 8, 128), 1, plane_both)
    g3 = plain_end(1)
    proj = jnp.concatenate(
        [top, jnp.concatenate([g2, 0.5 * (g3 + g3.T)], axis=1)], axis=0
    )
    ray_out[...] = dot32(inverse, dot32(inverse, proj, NN), NT)


def finish(block, ray, block_out, ray_out, sem):
    copies = [
        pltpu.make_async_copy(block, block_out, sem.at[0]),
        pltpu.make_async_copy(ray, ray_out, sem.at[1]),
    ]
    for c in copies:
        c.start()
    for c in copies:
        c.wait()


def on_device(block, labels, inverse_eps):
    bands, comps, planes, ny, nz = block.shape
    count = comps * planes * CX * CY * CZ * ny * nz
    dma = pltpu.SemaphoreType.DMA
    vmem = pltpu.VMEM
    chips = CX * CY
    hbm = pl.BlockSpec(memory_space=pltpu.HBM)
    next_block, rayleigh = pl.pallas_call(
        functools.partial(kernel, count),
        out_shape=(
            jax.ShapeDtypeStruct((bands * comps * planes * ny, nz), F32),
            jax.ShapeDtypeStruct((64, 64), F32),
        ),
        in_specs=[hbm, hbm, hbm],
        out_specs=(
            pl.BlockSpec(memory_space=pltpu.VMEM),
            pl.BlockSpec(memory_space=pltpu.VMEM),
        ),
        scratch_shapes=[
            vmem((3072, 128), F32),
            vmem((2, 32, 128), jnp.int32),
            pltpu.SMEM((3,), F32),
            vmem((6, 35, 32, 128), F32),
            vmem((2, 34, 16, 128), F32),
            vmem((2, 32, 16, 128), F32),
            vmem((2, 17, 32, 128), F32),
            vmem((2, 17, 32, 128), F32),
            vmem((16, 32, 128), F32),
            vmem((16, 32, 128), F32),
            vmem((2, 40, 128), F32),
            vmem((40, 128), F32),
            vmem((4, 17, 32, 128), F32),
            vmem((17, 32, 128), F32),
            vmem((17, 32, 128), F32),
            vmem((6, 33, 32, 128), F32),
            vmem((17, 32, 128), F32),
            vmem((96, 128, 256), BF16),
            vmem((2, 8, 128), F32),
            vmem((2, 2 * CZ, 8, 128), F32),
            vmem((2, 8, 128), F32),
            vmem((2, chips, 8, 128), F32),
            vmem((2, 8, 128), F32),
            vmem((2 * CZ, 8, 128), F32),
            vmem((8, 128), F32),
            vmem((2, chips, 8, 128), F32),
            vmem((32, 64), F32),
            dma((8,)),
            dma((2, PIECES + 1, 2)),
            dma((2, PIECES + 1)),
            dma((2, len(LATE), 2)),
            dma((2, len(LATE))),
            dma((PIECES + 2,)),
            dma((PIECES + 2,)),
            dma((1,)),
            dma((1,)),
            dma((3, 2)),
            dma((3, 2)),
        ],
        compiler_params=pltpu.CompilerParams(
            collective_id=0, has_side_effects=True, vmem_limit_bytes=32 << 20
        ),
        name="subspace",
    )(
        *(
            pltpu.with_memory_space_constraint(a, pltpu.HBM)
            for a in (block.reshape(bands, comps * planes * ny, nz), labels, inverse_eps)
        )
    )
    next_block, rayleigh = pl.pallas_call(
        finish,
        out_shape=(
            jax.ShapeDtypeStruct(next_block.shape, F32),
            jax.ShapeDtypeStruct(rayleigh.shape, F32),
        ),
        in_specs=[pl.BlockSpec(memory_space=pltpu.VMEM)] * 2,
        out_specs=(hbm, hbm),
        scratch_shapes=[dma((2,))],
        name="finish",
    )(next_block, rayleigh)
    return next_block.reshape(block.shape), rayleigh


def solution(mesh):
    in_specs = (P("band", None, "slab", None, None), P("slab", None, None), P())
    out_specs = (P("band", None, "slab", None, None), P())
    return jax.shard_map(
        on_device, mesh=mesh, in_specs=in_specs, out_specs=out_specs, check_vma=False
    )
```

```python
import functools

import jax
import jax.numpy as jnp
from jax import lax
from jax.experimental import pallas as pl
from jax.experimental.pallas import tpu as pltpu
from jax.sharding import PartitionSpec as P

MESH = pl.DeviceIdType.MESH
F32 = jnp.float32
BF16 = jnp.bfloat16
CX, CY, CZ = 4, 4, 8
PIECE = 4
PIECES = 16 // PIECE
LATE = ((0, 12), (12, 16))
NT = (((1,), (1,)), ((), ()))
NN = (((1,), (0,)), ((), ()))


def rf(v):
    return pltpu.roll(v, v.shape[-1] - 1, v.ndim - 1)


def rb(v):
    return pltpu.roll(v, 1, v.ndim - 1)


def split(v):
    hi = v.astype(BF16)
    return hi, (v - hi.astype(F32)).astype(BF16)


def dot32(a, b, dims):
    return lax.dot_general(
        a, b, dims, precision=lax.Precision.HIGHEST, preferred_element_type=F32
    )


def remote(src, dst, send, recv, to):
    return pltpu.make_async_remote_copy(
        src_ref=src, dst_ref=dst, send_sem=send, recv_sem=recv, device_id=to, device_id_type=MESH
    )


def pack(m):
    return jnp.concatenate([m[8 * i : 8 * i + 8] for i in range(4)], axis=1)


def unpack(v):
    return jnp.concatenate([v[:, 32 * i : 32 * i + 32] for i in range(4)], axis=0)


def identity(n):
    rows = lax.broadcasted_iota(jnp.int32, (n, n), 0)
    return (rows == lax.broadcasted_iota(jnp.int32, (n, n), 1)).astype(F32)


def eliminate(matrix, *others):
    n = matrix.shape[0]
    eye = identity(n)
    whole = jnp.concatenate([matrix, eye, *others], axis=1)
    shape = (8, whole.shape[1])
    row_id = lax.broadcasted_iota(jnp.int32, shape, 0)
    parts = [whole[8 * i : 8 * i + 8] for i in range(n // 8)]
    for k in range(0, n, 2):
        home, at = divmod(k, 8)
        f0 = [jnp.broadcast_to(part[:, k : k + 1], shape) for part in parts[home:]]
        f1 = [jnp.broadcast_to(part[:, k + 1 : k + 2], shape) for part in parts[home:]]
        a, b = f0[0][at : at + 1], f0[0][at + 1 : at + 2]
        bt, c = f1[0][at : at + 1], f1[0][at + 1 : at + 2]
        r0, r1 = parts[home][at : at + 1], parts[home][at + 1 : at + 2]
        u0, u1 = c * r0 - bt * r1, a * r1 - b * r0
        scale = 1.0 / (a * c - b * bt)
        t0, t1 = u0 * scale, u1 * scale
        second = u1 * (1.0 / a)
        for i in range(home, n // 8):
            new = parts[i] - (f0[i - home] * t0 + f1[i - home] * t1)
            if i == home:
                kept = jnp.where(row_id == at + 1, second, parts[i])
                new = jnp.where(row_id > at + 1, new, kept)
            parts[i] = new
    whole = jnp.concatenate(parts, axis=0)
    diag = jnp.sum(whole[:, :n] * eye, axis=1, keepdims=True)
    whole = whole * (1.0 / jnp.sqrt(diag))
    return [whole[:, n * i : n * i + n] for i in range(1, 2 + len(others))]


def kernel(
    count,
    block,
    labels,
    inv,
    out,
    ray_out,
    xin,
    lab,
    inv_s,
    xt,
    pq,
    sq,
    hb,
    ha,
    sa,
    qb,
    eta,
    eta_in,
    hs,
    hyb,
    hzm,
    ax,
    axm,
    tiles,
    plain_src,
    plain_1,
    plain_mid,
    plain_2,
    split_src,
    split_1,
    split_mid,
    split_2,
    ct,
    in_sem,
    halo_s,
    halo_r,
    late_s,
    late_r,
    swap_s,
    swap_r,
    eta_s,
    eta_r,
    sum_s,
    sum_r,
):
    slabs = CX * CY * CZ
    chips = CX * CY
    s = lax.axis_index("slab")
    k = lax.axis_index("band")
    x = lax.rem(s, CX)
    y = lax.rem(lax.div(s, CX), CY)
    z = lax.div(s, chips)
    up = lax.rem(s + 1, slabs)
    down = lax.rem(s + slabs - 1, slabs)
    base = s - x - CX * y
    sibling = (s, 1 - k)
    plane = [
        base + CX * lax.rem(y + i, CY) + lax.rem(x + j, CX)
        for i, j in sorted(
            ((i, j) for i in range(CY) for j in range(CX) if (i, j) != (0, 0)),
            key=lambda o: -(min(o[0], CY - o[0]) + min(o[1], CX - o[1])),
        )
    ]
    column = [
        s - chips * z + chips * lax.rem(z + i, CZ)
        for i in sorted(range(1, CZ), key=lambda o: -min(o, CZ - o))
    ]
    plane_both = [(chip, c) for chip in plane for c in range(2)] + [sibling]
    column_both = [(chip, c) for chip in column for c in range(2)] + [sibling]
    plane_own = [(chip, k) for chip in plane]
    mine = pl.multiple_of(16 * k, 16)
    theirs = pl.multiple_of(16 * (1 - k), 16)
    own = pl.ds(mine, 16)

    order = (2, 4, 1, 3, 5, 0)
    loads = {
        cp: pltpu.make_async_copy(
            block.at[:, pl.ds(32 * cp, 32)],
            xin.reshape(16, 192, 128).at[:, pl.ds(32 * cp, 32)],
            in_sem.at[cp],
        )
        for cp in order
    }
    for cp in order:
        loads[cp].start()
    label_load = pltpu.make_async_copy(labels, lab, in_sem.at[6])
    label_load.start()
    inv_load = pltpu.make_async_copy(inv, inv_s, in_sem.at[7])
    inv_load.start()

    barrier = pltpu.get_barrier_semaphore()
    greeted = [(down, 0), (down, 1), (up, 0), (up, 1)] + plane_both + column_both[:-1]
    for to in greeted:
        pl.semaphore_signal(barrier, inc=1, device_id=to, device_id_type=MESH)

    turned = set()

    def turn(cp, rows):
        c, p = divmod(cp, 2)
        r = p * 3 + c
        for row in rows:
            if (cp, row) not in turned:
                turned.add((cp, row))
                value = xin[pl.ds(cp * 32 + row, 16, stride=192), :]
                xt[r, row + 1, own] = value
                if row == 31:
                    xt[r, 0, own] = value
                if row < 2:
                    xt[r, row + 33, own] = value

    def piece(n):
        return [16 * to + PIECE * n + i for to in range(2) for i in range(PIECE)]

    def halo(d, n, src, step, dst, to_slab):
        copies = []
        for to in range(2):
            if n == 0:
                copies.append(
                    remote(
                        src(1, pl.ds(step * to, 1)),
                        dst.at[pl.ds(0, 1), pl.ds(0, 1), own],
                        halo_s.at[d, PIECES, to],
                        halo_r.at[d, PIECES],
                        (to_slab, to),
                    )
                )
            copies.append(
                remote(
                    src(2, pl.ds(step * to + PIECE * n + 1, PIECE)),
                    dst.at[:, pl.ds(PIECE * n + 1, PIECE), own],
                    halo_s.at[d, n, to],
                    halo_r.at[d, n],
                    (to_slab, to),
                )
            )
        for c in copies:
            c.start()
        return copies

    sends = []
    for n in range(PIECES):
        if n == 0:
            loads[2].wait()
            turn(2, (31, 15))
            loads[4].wait()
        turn(2, piece(n))
        turn(4, piece(n))
        if n == 0:
            pl.semaphore_wait(barrier, len(greeted))
        sends += halo(0, n, lambda m, rows: xt.at[pl.ds(1, m), rows, own], 16, ha, down)
        if n == 0:
            loads[1].wait()
            turn(1, range(32))
            loads[3].wait()
            turn(3, (31, 15))
            for to in range(2):
                row = 16 * to
                pq[0, 17 * to] = xt[4, row, own] + (xt[3, row + 1, own] - xt[3, row, own])
            loads[5].wait()
        turn(3, piece(n))
        turn(5, piece(n))
        for row in piece(n):
            ex = xt[3, row + 1, own]
            at = row + 1 + row // 16
            pq[0, at] = xt[4, row + 1, own] + (xt[3, row + 2, own] - ex)
            pq[1, at] = (rf(ex) - ex) + xt[5, row + 1, own]
        sends += halo(1, n, lambda m, rows: pq.at[pl.ds(0, m), rows], 17, hb, up)

    loads[0].wait()
    turn(0, range(32))
    swap = remote(xt.at[:, :, own], xt.at[:, :, own], swap_s.at[0], swap_r.at[0], sibling)
    swap.start()
    sends.append(swap)

    label_load.wait()
    inv_load.wait()
    for p in range(2):
        regions = lab[p]
        value = jnp.zeros(regions.shape, F32)
        for r in range(3):
            value = value + jnp.where(regions == r, 1.0, 0.0) * inv_s[r]
        eta[p, 1:33] = value
        eta[p, 0:1] = value[31:32]
        eta[p, 33:40] = value[0:7]
    eta_copy = remote(eta.at[1], eta_in, eta_s.at[0], eta_r.at[0], (up, k))
    eta_copy.start()
    sends.append(eta_copy)

    def curl_x(p, row):
        ey = xt[3 * p + 1, row, own]
        return eta[p, pl.ds(row, 1), :] * (
            (xt[3 * p + 2, row + 1, own] - xt[3 * p + 2, row, own]) - (rf(ey) - ey)
        )

    def late(row, before):
        ea = eta[0, pl.ds(row, 1), :]
        ex, ey, ez = xt[0, row, own], xt[1, row, own], xt[2, row, own]
        now = curl_x(0, row)
        hy = ea * ((rf(ex) - ex) - (xt[5, row, own] - ez))
        hz = ea * ((xt[4, row, own] - ey) - (xt[0, row + 1, own] - ex))
        sq[0, row - 1] = hy - (now - before)
        hx = curl_x(1, row)
        sq[1, row - 1] = (hx - rb(hx)) + hz
        return now

    lax.fori_loop(1, 33, late, curl_x(0, 0), unroll=4)
    for n, (lo, hi) in enumerate(LATE):
        for d, to_slab, dst in ((0, down, sa), (1, up, qb)):
            for to in range(2):
                c = remote(
                    sq.at[d, pl.ds(16 * to + lo, hi - lo)],
                    dst.at[pl.ds(lo, hi - lo), own],
                    late_s.at[d, n, to],
                    late_r.at[d, n],
                    (to_slab, to),
                )
                c.start()
                sends.append(c)

    def scatter(src, dst, send, recv, group):
        for to in group:
            remote(src(to[1]), dst, send, recv, to).start()

    def gathered(src, send, recv, group):
        part = src.at[pl.ds(0, len(group))]
        remote(part, part, send, recv, sibling).wait_recv()

    def total_of(ref):
        value = ref[0]
        for i in range(1, ref.shape[0]):
            value = value + ref[i]
        return value

    def plain_first(i, value):
        plain_src[i] = value
        at = z * 2 + k
        scatter(
            lambda _: plain_src.at[i], plain_1.at[i, at], sum_s.at[i, 0], sum_r.at[i, 0], column_both
        )
        plain_1[i, at] = value

    def plain_second(i):
        gathered(plain_1.at[i], sum_s.at[i, 0], sum_r.at[i, 0], column_both)
        value = total_of(plain_1.at[i])
        plain_mid[i] = value
        at = y * CX + x
        scatter(
            lambda _: plain_mid.at[i], plain_2.at[i, at], sum_s.at[i, 1], sum_r.at[i, 1], plane_own
        )
        plain_2[i, at] = value

    def plain_end(i):
        gathered(plain_2.at[i], sum_s.at[i, 1], sum_r.at[i, 1], plane_own)
        return unpack(total_of(plain_2.at[i]) * (1.0 / count))

    def sent(i, ref, phase, group):
        part = ref.at[pl.ds(0, len(group))]
        remote(part, part, sum_s.at[i, phase], sum_r.at[i, phase], sibling).wait_send()

    swap.wait_recv()

    def put(t, at, values):
        hi, lo = (jnp.concatenate(v, axis=1) for v in zip(*(split(v) for v in values)))
        tiles[t, at : at + 32] = hi
        tiles[t, at + 64 : at + 96] = lo
        return hi, lo

    def first_gram(row, total):
        for r in range(0, 6, 2):
            both = jnp.concatenate(
                put((mine + row) * 3 + r // 2, 0, [xt[r + q, mine + row + 1] for q in range(2)]),
                axis=0,
            )
            total = total + lax.dot_general(both, both, NT, preferred_element_type=F32)
        return total

    total = lax.fori_loop(0, 16, first_gram, jnp.zeros((64, 64), F32), unroll=4)
    total = total[:, :32] + total[:, 32:]
    plain_first(0, pack(total[:32] + total[32:]))

    def inside(row, carry):
        at = mine + row
        ea, eb = eta[0, pl.ds(at, 1), :], eta[1, pl.ds(at, 1), :]
        ex, ey, ez = xt[0, at], xt[1, at], xt[2, at]
        fy, fz = xt[4, at], xt[5, at]
        hs[0, row] = ea * ((xt[2, at + 1] - ez) - (rf(ey) - ey))
        hs[1, row] = ea * ((rf(ex) - ex) - (fz - ez))
        hs[2, row] = ea * ((fy - ey) - (xt[0, at + 1] - ex))
        hs[3, row] = eb * ((xt[5, at + 1] - fz) - (rf(fy) - fy))
        return carry

    inside(0, 0)
    lax.fori_loop(1, 17, inside, 0, unroll=4)

    def other_block(row, carry):
        for r in range(0, 6, 2):
            put((theirs + row) * 3 + r // 2, 0, [xt[r + q, theirs + row + 1] for q in range(2)])
        return carry

    lax.fori_loop(0, 16, other_block, 0, unroll=4)
    eta_copy.wait_recv()

    def last_z(row):
        at = mine + row
        hz = eta[1, pl.ds(at, 1), :] * ((ha[0, row] - xt[4, at]) - (xt[3, at + 1] - xt[3, at]))
        mz = eta_in[pl.ds(at, 1), :] * (xt[1, at] - hb[0, row])
        return hz, mz

    def image(row, carry):
        hz_old, mz_old = carry
        at = mine + row
        to = mine + row - 1
        hz, mz = last_z(row)
        ex = xt[3, at]
        hy = eta[1, pl.ds(at, 1), :] * ((rf(ex) - ex) - (ha[1, row] - xt[5, at]))
        my = eta_in[pl.ds(at, 1), :] * (hb[1, row] - xt[2, at])
        hyb[row] = hy
        hzm[row] = mz
        ax_, ay_, az_, bx_ = hs[0, row], hs[1, row], hs[2, row], hs[3, row]
        ax[0, to] = 0.25 * ((az_ - hs[2, row - 1]) - (ay_ - rb(ay_)))
        ax[1, to] = 0.25 * ((ax_ - rb(ax_)) - (az_ - mz))
        ax[2, to] = 0.25 * ((ay_ - my) - (ax_ - hs[0, row - 1]))
        ax[3, to] = 0.25 * ((hz - hz_old) - (hy - rb(hy)))
        ax[4, to] = 0.25 * ((bx_ - rb(bx_)) - (hz - az_))
        ax[5, to] = 0.25 * ((hy - ay_) - (bx_ - hs[3, row - 1]))
        axm[row - 1] = 0.25 * ((mz - mz_old) - (my - rb(my)))
        return hz, mz

    def products(row, total):
        at = mine + row - 1
        for r in range(0, 6, 2):
            t = at * 3 + r // 2
            right = jnp.concatenate(put(t, 32, [ax[r + q, at] for q in range(2)]), axis=0)
            total = total + lax.dot_general(tiles[t], right, NT, preferred_element_type=F32)
        return total

    total = jnp.zeros((128, 64), F32)
    carry = None
    swaps = []
    for n in range(PIECES):
        for d, dst in enumerate((ha, hb)):
            arrived = [(dst.at[:, pl.ds(PIECE * n + 1, PIECE)], n)]
            if n == 0:
                arrived.append((dst.at[pl.ds(0, 1), pl.ds(0, 1)], PIECES))
            for ref, i in arrived:
                remote(ref, ref, halo_s.at[d, i, 0], halo_r.at[d, i], sibling).wait_recv()
        if n == 0:
            carry = last_z(0)
        carry = lax.fori_loop(PIECE * n + 1, PIECE * n + PIECE + 1, image, carry, unroll=4)
        rows = pl.ds(mine + PIECE * n, PIECE)
        c = remote(ax.at[:, rows], ax.at[:, rows], swap_s.at[n + 1], swap_r.at[n + 1], sibling)
        c.start()
        swaps.append(c)
        if n == 0:
            c = remote(
                axm.at[0], axm.at[16], swap_s.at[PIECES + 1], swap_r.at[PIECES + 1], sibling
            )
            c.start()
            swaps.append(c)
        total = lax.fori_loop(PIECE * n + 1, PIECE * n + PIECE + 1, products, total, unroll=4)

    total = total[:, :32] + total[:, 32:]
    total = total[:64] + total[64:]
    split_src[0] = pack(total[:32])
    split_src[1] = pack(total[32:])
    at = z * 2 + k
    scatter(
        lambda c: split_src.at[c], split_1.at[at], sum_s.at[2, 0], sum_r.at[2, 0], column_both
    )
    split_1[at] = split_src[k]
    plain_second(0)

    for c in swaps:
        c.wait_recv()
    sends += swaps
    for r in range(6):
        ax[r, 32] = ax[r, 0]

    def other_image(row, carry):
        for r in range(0, 6, 2):
            put((theirs + row) * 3 + r // 2, 32, [ax[r + q, theirs + row] for q in range(2)])
        return carry

    lax.fori_loop(0, 16, other_image, 0, unroll=4)

    def third(row, acc):
        at = mine + row
        to = at - 1
        ea, eb = eta[0, pl.ds(at, 1), :], eta[1, pl.ds(at, 1), :]
        em = eta_in[pl.ds(at, 1), :]
        ux, uy, uz = ax[0, to], ax[1, to], ax[2, to]
        vx, vy, vz = ax[3, to], ax[4, to], ax[5, to]
        pz = 0.25 * (sa[row - 1] - hyb[row])
        my = 0.25 * (qb[row - 1] - hzm[row])
        curls = (
            (ea, (ax[2, to + 1] - uz) - (rf(uy) - uy)),
            (ea, (rf(ux) - ux) - (vz - uz)),
            (ea, (vy - uy) - (ax[0, to + 1] - ux)),
            (eb, (ax[5, to + 1] - vz) - (rf(vy) - vy)),
            (eb, (rf(vx) - vx) - (pz - vz)),
            (em, (uy - my) - (axm[row] - axm[row - 1])),
        )
        for i in range(0, 6, 2):
            left, right = [], []
            for e, v in curls[i : i + 2]:
                left.append(jnp.concatenate(split(v), axis=0))
                right.append(jnp.concatenate(split(e * v), axis=0))
            acc = acc + lax.dot_general(
                jnp.concatenate(left, axis=1),
                jnp.concatenate(right, axis=1),
                NT,
                preferred_element_type=F32,
            )
        return acc

    acc = jnp.zeros((64, 64), F32)
    for n, (lo, hi) in enumerate(LATE):
        for d, dst in enumerate((sa, qb)):
            ref = dst.at[pl.ds(lo, hi - lo)]
            remote(ref, ref, late_s.at[d, n, 0], late_r.at[d, n], sibling).wait_recv()
        acc = lax.fori_loop(lo + 1, hi + 1, third, acc, unroll=4)
    acc = acc[:, :32] + acc[:, 32:]
    plain_first(1, pack(0.25 * (acc[:32] + acc[32:])))

    gathered(split_1, sum_s.at[2, 0], sum_r.at[2, 0], column_both)
    value = total_of(split_1)
    split_mid[...] = value
    at = y * CX + x
    scatter(lambda _: split_mid, split_2.at[k, at], sum_s.at[2, 1], sum_r.at[2, 1], plane_both)
    split_2[k, at] = value
    for c in sends:
        c.wait_send()

    g0 = plain_end(0)
    (inv11,) = eliminate(0.5 * (g0 + g0.T))
    plain_second(1)

    part = split_2.reshape(2 * chips, 8, 128).at[pl.ds(0, len(plane_both))]
    remote(part, part, sum_s.at[2, 1], sum_r.at[2, 1], sibling).wait_recv()
    halves = [unpack(total_of(split_2.at[c]) * (1.0 / count)) for c in range(2)]
    g1, g2 = halves
    g1t = g1.T
    g2 = 0.5 * (g2 + g2.T)
    top = jnp.concatenate([0.5 * (g1 + g1t), g2], axis=1)
    low21 = dot32(g1t, inv11, NT)
    inv22, inv21 = eliminate(g2 - dot32(low21, low21, NT), -dot32(low21, inv11, NN))
    inverse = jnp.concatenate(
        [
            jnp.concatenate([inv11, jnp.zeros((32, 32), F32)], axis=1),
            jnp.concatenate([inv21, inv22], axis=1),
        ],
        axis=0,
    )
    coeffs = dot32(dot32(dot32(inv11, top, NN), inverse, NT), inverse, NN)
    ct[...] = coeffs

    own_h, own_l = split(ct[own, :])
    left = jnp.concatenate([own_h, own_l], axis=0)
    left = jnp.concatenate([left, left], axis=1)

    def fresh(row, carry):
        for r in range(0, 6, 2):
            res = lax.dot_general(
                left, tiles[row * 3 + r // 2], NN, preferred_element_type=F32
            )
            res = res[:16] + res[16:]
            for q in range(2):
                p, c = divmod(r + q, 3)
                out[pl.ds((c * 2 + p) * 32 + row, 16, stride=192), :] = res[
                    :, 128 * q : 128 * q + 128
                ]
        return carry

    lax.fori_loop(0, 32, fresh, 0, unroll=8)

    sent(0, plain_1.at[0], 0, column_both)
    sent(0, plain_2.at[0], 1, plane_own)
    sent(1, plain_1.at[1], 0, column_both)
    sent(1, plain_2.at[1], 1, plane_own)
    sent(2, split_1, 0, column_both)
    sent(2, split_2.reshape(2 * chips, 8, 128), 1, plane_both)
    g3 = plain_end(1)
    proj = jnp.concatenate(
        [top, jnp.concatenate([g2, 0.5 * (g3 + g3.T)], axis=1)], axis=0
    )
    ray_out[...] = dot32(inverse, dot32(inverse, proj, NN), NT)


def finish(block, ray, block_out, ray_out, sem):
    copies = [
        pltpu.make_async_copy(block, block_out, sem.at[0]),
        pltpu.make_async_copy(ray, ray_out, sem.at[1]),
    ]
    for c in copies:
        c.start()
    for c in copies:
        c.wait()


def on_device(block, labels, inverse_eps):
    bands, comps, planes, ny, nz = block.shape
    count = comps * planes * CX * CY * CZ * ny * nz
    dma = pltpu.SemaphoreType.DMA
    vmem = pltpu.VMEM
    chips = CX * CY
    hbm = pl.BlockSpec(memory_space=pltpu.HBM)
    next_block, rayleigh = pl.pallas_call(
        functools.partial(kernel, count),
        out_shape=(
            jax.ShapeDtypeStruct((bands * comps * planes * ny, nz), F32),
            jax.ShapeDtypeStruct((64, 64), F32),
        ),
        in_specs=[hbm, hbm, hbm],
        out_specs=(
            pl.BlockSpec(memory_space=pltpu.VMEM),
            pl.BlockSpec(memory_space=pltpu.VMEM),
        ),
        scratch_shapes=[
            vmem((3072, 128), F32),
            vmem((2, 32, 128), jnp.int32),
            pltpu.SMEM((3,), F32),
            vmem((6, 35, 32, 128), F32),
            vmem((2, 34, 16, 128), F32),
            vmem((2, 32, 16, 128), F32),
            vmem((2, 17, 32, 128), F32),
            vmem((2, 17, 32, 128), F32),
            vmem((16, 32, 128), F32),
            vmem((16, 32, 128), F32),
            vmem((2, 40, 128), F32),
            vmem((40, 128), F32),
            vmem((4, 17, 32, 128), F32),
            vmem((17, 32, 128), F32),
            vmem((17, 32, 128), F32),
            vmem((6, 33, 32, 128), F32),
            vmem((17, 32, 128), F32),
            vmem((96, 128, 256), BF16),
            vmem((2, 8, 128), F32),
            vmem((2, 2 * CZ, 8, 128), F32),
            vmem((2, 8, 128), F32),
            vmem((2, chips, 8, 128), F32),
            vmem((2, 8, 128), F32),
            vmem((2 * CZ, 8, 128), F32),
            vmem((8, 128), F32),
            vmem((2, chips, 8, 128), F32),
            vmem((32, 64), F32),
            dma((8,)),
            dma((2, PIECES + 1, 2)),
            dma((2, PIECES + 1)),
            dma((2, len(LATE), 2)),
            dma((2, len(LATE))),
            dma((PIECES + 2,)),
            dma((PIECES + 2,)),
            dma((1,)),
            dma((1,)),
            dma((3, 2)),
            dma((3, 2)),
        ],
        compiler_params=pltpu.CompilerParams(
            collective_id=0, has_side_effects=True, vmem_limit_bytes=32 << 20
        ),
        name="subspace",
    )(
        *(
            pltpu.with_memory_space_constraint(a, pltpu.HBM)
            for a in (block.reshape(bands, comps * planes * ny, nz), labels, inverse_eps)
        )
    )
    next_block, rayleigh = pl.pallas_call(
        finish,
        out_shape=(
            jax.ShapeDtypeStruct(next_block.shape, F32),
            jax.ShapeDtypeStruct(rayleigh.shape, F32),
        ),
        in_specs=[pl.BlockSpec(memory_space=pl.ANY)] * 2,
        out_specs=(hbm, hbm),
        scratch_shapes=[dma((2,))],
        compiler_params=pltpu.CompilerParams(vmem_limit_bytes=1 << 20),
        name="finish",
    )(next_block, rayleigh)
    return next_block.reshape(block.shape), rayleigh


def solution(mesh):
    in_specs = (P("band", None, "slab", None, None), P("slab", None, None), P())
    out_specs = (P("band", None, "slab", None, None), P())
    return jax.shard_map(
        on_device, mesh=mesh, in_specs=in_specs, out_specs=out_specs, check_vma=False
    )
```

```python
import functools

import jax
import jax.numpy as jnp
from jax import lax
from jax.experimental import pallas as pl
from jax.experimental.pallas import tpu as pltpu
from jax.sharding import PartitionSpec as P

MESH = pl.DeviceIdType.MESH
F32 = jnp.float32
BF16 = jnp.bfloat16
CX, CY, CZ = 4, 4, 8
PIECE = 4
PIECES = 16 // PIECE
LATE = ((0, 12), (12, 16))
NT = (((1,), (1,)), ((), ()))
NN = (((1,), (0,)), ((), ()))


def rf(v):
    return pltpu.roll(v, v.shape[-1] - 1, v.ndim - 1)


def rb(v):
    return pltpu.roll(v, 1, v.ndim - 1)


def split(v):
    hi = v.astype(BF16)
    return hi, (v - hi.astype(F32)).astype(BF16)


def dot32(a, b, dims):
    return lax.dot_general(
        a, b, dims, precision=lax.Precision.HIGHEST, preferred_element_type=F32
    )


def remote(src, dst, send, recv, to):
    return pltpu.make_async_remote_copy(
        src_ref=src, dst_ref=dst, send_sem=send, recv_sem=recv, device_id=to, device_id_type=MESH
    )


def pack(m):
    return jnp.concatenate([m[8 * i : 8 * i + 8] for i in range(4)], axis=1)


def unpack(v):
    return jnp.concatenate([v[:, 32 * i : 32 * i + 32] for i in range(4)], axis=0)


def identity(n):
    rows = lax.broadcasted_iota(jnp.int32, (n, n), 0)
    return (rows == lax.broadcasted_iota(jnp.int32, (n, n), 1)).astype(F32)


def eliminate(matrix, *others):
    n = matrix.shape[0]
    eye = identity(n)
    whole = jnp.concatenate([matrix, eye, *others], axis=1)
    shape = (8, whole.shape[1])
    row_id = lax.broadcasted_iota(jnp.int32, shape, 0)
    parts = [whole[8 * i : 8 * i + 8] for i in range(n // 8)]

    def wide(column, home):
        return [jnp.broadcast_to(part[:, column : column + 1], shape) for part in parts[home:]]

    f0, f1 = wide(0, 0), wide(1, 0)
    for k in range(0, n, 2):
        home, at = divmod(k, 8)
        ahead = [wide(k + 2 + j, home) for j in range(2)] if k + 2 < n else []
        a, b = f0[0][at : at + 1], f0[0][at + 1 : at + 2]
        bt, c = f1[0][at : at + 1], f1[0][at + 1 : at + 2]
        scale = 1.0 / (a * c - b * bt)

        def pivots(part):
            r0, r1 = part[at : at + 1], part[at + 1 : at + 2]
            u0, u1 = c * r0 - bt * r1, a * r1 - b * r0
            return u0 * scale, u1 * scale, u1

        t0, t1, u1 = pivots(parts[home])
        second = u1 * (1.0 / a)
        coming = []
        for columns in ahead:
            s0, s1, _ = pivots(columns[0])
            coming.append([v - (p * s0 + q * s1) for v, p, q in zip(columns, f0, f1)])
        for i in range(home, n // 8):
            new = parts[i] - (f0[i - home] * t0 + f1[i - home] * t1)
            if i == home:
                kept = jnp.where(row_id == at + 1, second, parts[i])
                new = jnp.where(row_id > at + 1, new, kept)
            parts[i] = new
        if ahead:
            f0, f1 = (columns[(k + 2) // 8 - home :] for columns in coming)
    whole = jnp.concatenate(parts, axis=0)
    diag = jnp.sum(whole[:, :n] * eye, axis=1, keepdims=True)
    whole = whole * (1.0 / jnp.sqrt(diag))
    return [whole[:, n * i : n * i + n] for i in range(1, 2 + len(others))]


def kernel(
    count,
    block,
    labels,
    inv,
    out,
    ray_out,
    xin,
    lab,
    inv_s,
    xt,
    pq,
    sq,
    hb,
    ha,
    sa,
    qb,
    eta,
    eta_in,
    hs,
    hyb,
    hzm,
    ax,
    axm,
    tiles,
    plain_src,
    plain_1,
    plain_mid,
    plain_2,
    split_src,
    split_1,
    split_mid,
    split_2,
    ct,
    in_sem,
    halo_s,
    halo_r,
    late_s,
    late_r,
    swap_s,
    swap_r,
    eta_s,
    eta_r,
    sum_s,
    sum_r,
):
    slabs = CX * CY * CZ
    chips = CX * CY
    s = lax.axis_index("slab")
    k = lax.axis_index("band")
    x = lax.rem(s, CX)
    y = lax.rem(lax.div(s, CX), CY)
    z = lax.div(s, chips)
    up = lax.rem(s + 1, slabs)
    down = lax.rem(s + slabs - 1, slabs)
    base = s - x - CX * y
    sibling = (s, 1 - k)
    plane = [
        base + CX * lax.rem(y + i, CY) + lax.rem(x + j, CX)
        for i, j in sorted(
            ((i, j) for i in range(CY) for j in range(CX) if (i, j) != (0, 0)),
            key=lambda o: -(min(o[0], CY - o[0]) + min(o[1], CX - o[1])),
        )
    ]
    column = [
        s - chips * z + chips * lax.rem(z + i, CZ)
        for i in sorted(range(1, CZ), key=lambda o: -min(o, CZ - o))
    ]
    plane_both = [(chip, c) for chip in plane for c in range(2)] + [sibling]
    column_both = [(chip, c) for chip in column for c in range(2)] + [sibling]
    plane_own = [(chip, k) for chip in plane]
    mine = pl.multiple_of(16 * k, 16)
    theirs = pl.multiple_of(16 * (1 - k), 16)
    own = pl.ds(mine, 16)

    order = (2, 4, 1, 3, 5, 0)
    loads = {
        cp: pltpu.make_async_copy(
            block.at[:, pl.ds(32 * cp, 32)],
            xin.reshape(16, 192, 128).at[:, pl.ds(32 * cp, 32)],
            in_sem.at[cp],
        )
        for cp in order
    }
    for cp in order:
        loads[cp].start()
    label_load = pltpu.make_async_copy(labels, lab, in_sem.at[6])
    label_load.start()
    inv_load = pltpu.make_async_copy(inv, inv_s, in_sem.at[7])
    inv_load.start()

    barrier = pltpu.get_barrier_semaphore()
    greeted = [(down, 0), (down, 1), (up, 0), (up, 1)] + plane_both + column_both[:-1]
    for to in greeted:
        pl.semaphore_signal(barrier, inc=1, device_id=to, device_id_type=MESH)

    turned = set()

    def turn(cp, rows):
        c, p = divmod(cp, 2)
        r = p * 3 + c
        for row in rows:
            if (cp, row) not in turned:
                turned.add((cp, row))
                value = xin[pl.ds(cp * 32 + row, 16, stride=192), :]
                xt[r, row + 1, own] = value
                if row == 31:
                    xt[r, 0, own] = value
                if row < 2:
                    xt[r, row + 33, own] = value

    def piece(n):
        return [16 * to + PIECE * n + i for to in range(2) for i in range(PIECE)]

    def halo(d, n, src, step, dst, to_slab):
        copies = []
        for to in range(2):
            if n == 0:
                copies.append(
                    remote(
                        src(1, pl.ds(step * to, 1)),
                        dst.at[pl.ds(0, 1), pl.ds(0, 1), own],
                        halo_s.at[d, PIECES, to],
                        halo_r.at[d, PIECES],
                        (to_slab, to),
                    )
                )
            copies.append(
                remote(
                    src(2, pl.ds(step * to + PIECE * n + 1, PIECE)),
                    dst.at[:, pl.ds(PIECE * n + 1, PIECE), own],
                    halo_s.at[d, n, to],
                    halo_r.at[d, n],
                    (to_slab, to),
                )
            )
        for c in copies:
            c.start()
        return copies

    sends = []
    for n in range(PIECES):
        if n == 0:
            loads[2].wait()
            turn(2, (31, 15))
            loads[4].wait()
        turn(2, piece(n))
        turn(4, piece(n))
        if n == 0:
            pl.semaphore_wait(barrier, len(greeted))
        sends += halo(0, n, lambda m, rows: xt.at[pl.ds(1, m), rows, own], 16, ha, down)
        if n == 0:
            loads[1].wait()
            turn(1, (31, 15, 0, 16))
            loads[3].wait()
            turn(3, (31, 15))
            for to in range(2):
                row = 16 * to
                pq[0, 17 * to] = xt[4, row, own] + (xt[3, row + 1, own] - xt[3, row, own])
            loads[5].wait()
        turn(1, piece(n) + [(row + 1) % 32 for row in piece(n)])
        turn(3, piece(n))
        turn(5, piece(n))
        for row in piece(n):
            ex = xt[3, row + 1, own]
            at = row + 1 + row // 16
            pq[0, at] = xt[4, row + 1, own] + (xt[3, row + 2, own] - ex)
            pq[1, at] = (rf(ex) - ex) + xt[5, row + 1, own]
        sends += halo(1, n, lambda m, rows: pq.at[pl.ds(0, m), rows], 17, hb, up)

    loads[0].wait()
    turn(0, range(32))
    swap = remote(xt.at[:, :, own], xt.at[:, :, own], swap_s.at[0], swap_r.at[0], sibling)
    swap.start()
    sends.append(swap)

    label_load.wait()
    inv_load.wait()
    for p in range(2):
        regions = lab[p]
        value = jnp.zeros(regions.shape, F32)
        for r in range(3):
            value = value + jnp.where(regions == r, 1.0, 0.0) * inv_s[r]
        eta[p, 1:33] = value
        eta[p, 0:1] = value[31:32]
        eta[p, 33:40] = value[0:7]
    eta_copy = remote(eta.at[1], eta_in, eta_s.at[0], eta_r.at[0], (up, k))
    eta_copy.start()
    sends.append(eta_copy)

    def curl_x(p, row):
        ey = xt[3 * p + 1, row, own]
        return eta[p, pl.ds(row, 1), :] * (
            (xt[3 * p + 2, row + 1, own] - xt[3 * p + 2, row, own]) - (rf(ey) - ey)
        )

    def late(row, before):
        ea = eta[0, pl.ds(row, 1), :]
        ex, ey, ez = xt[0, row, own], xt[1, row, own], xt[2, row, own]
        now = curl_x(0, row)
        hy = ea * ((rf(ex) - ex) - (xt[5, row, own] - ez))
        hz = ea * ((xt[4, row, own] - ey) - (xt[0, row + 1, own] - ex))
        sq[0, row - 1] = hy - (now - before)
        hx = curl_x(1, row)
        sq[1, row - 1] = (hx - rb(hx)) + hz
        return now

    lax.fori_loop(1, 33, late, curl_x(0, 0), unroll=4)

    def send_late(n):
        lo, hi = LATE[n]
        for d, to_slab, dst in ((0, down, sa), (1, up, qb)):
            for to in range(2):
                c = remote(
                    sq.at[d, pl.ds(16 * to + lo, hi - lo)],
                    dst.at[pl.ds(lo, hi - lo), own],
                    late_s.at[d, n, to],
                    late_r.at[d, n],
                    (to_slab, to),
                )
                c.start()
                sends.append(c)

    def scatter(src, dst, send, recv, group):
        for to in group:
            remote(src(to[1]), dst, send, recv, to).start()

    def gathered(src, send, recv, group):
        part = src.at[pl.ds(0, len(group))]
        remote(part, part, send, recv, sibling).wait_recv()

    def total_of(ref):
        value = ref[0]
        for i in range(1, ref.shape[0]):
            value = value + ref[i]
        return value

    def plain_first(i, value):
        plain_src[i] = value
        at = z * 2 + k
        scatter(
            lambda _: plain_src.at[i], plain_1.at[i, at], sum_s.at[i, 0], sum_r.at[i, 0], column_both
        )
        plain_1[i, at] = value

    def plain_second(i):
        gathered(plain_1.at[i], sum_s.at[i, 0], sum_r.at[i, 0], column_both)
        value = total_of(plain_1.at[i])
        plain_mid[i] = value
        at = y * CX + x
        scatter(
            lambda _: plain_mid.at[i], plain_2.at[i, at], sum_s.at[i, 1], sum_r.at[i, 1], plane_own
        )
        plain_2[i, at] = value

    def plain_end(i):
        gathered(plain_2.at[i], sum_s.at[i, 1], sum_r.at[i, 1], plane_own)
        return unpack(total_of(plain_2.at[i]) * (1.0 / count))

    def sent(i, ref, phase, group):
        part = ref.at[pl.ds(0, len(group))]
        remote(part, part, sum_s.at[i, phase], sum_r.at[i, phase], sibling).wait_send()

    for n in range(len(LATE)):
        send_late(n)

    swap.wait_recv()

    def put(t, at, values):
        hi, lo = (jnp.concatenate(v, axis=1) for v in zip(*(split(v) for v in values)))
        tiles[t, at : at + 32] = hi
        tiles[t, at + 64 : at + 96] = lo
        return hi, lo

    def first_gram(row, total):
        for r in range(0, 6, 2):
            both = jnp.concatenate(
                put((mine + row) * 3 + r // 2, 0, [xt[r + q, mine + row + 1] for q in range(2)]),
                axis=0,
            )
            total = total + lax.dot_general(both, both, NT, preferred_element_type=F32)
        return total

    total = lax.fori_loop(0, 16, first_gram, jnp.zeros((64, 64), F32), unroll=4)
    total = total[:, :32] + total[:, 32:]
    plain_first(0, pack(total[:32] + total[32:]))

    def inside(row, carry):
        at = mine + row
        ea, eb = eta[0, pl.ds(at, 1), :], eta[1, pl.ds(at, 1), :]
        ex, ey, ez = xt[0, at], xt[1, at], xt[2, at]
        fy, fz = xt[4, at], xt[5, at]
        hs[0, row] = ea * ((xt[2, at + 1] - ez) - (rf(ey) - ey))
        hs[1, row] = ea * ((rf(ex) - ex) - (fz - ez))
        hs[2, row] = ea * ((fy - ey) - (xt[0, at + 1] - ex))
        hs[3, row] = eb * ((xt[5, at + 1] - fz) - (rf(fy) - fy))
        return carry

    inside(0, 0)
    lax.fori_loop(1, 17, inside, 0, unroll=4)

    def other_block(row, carry):
        for r in range(0, 6, 2):
            put((theirs + row) * 3 + r // 2, 0, [xt[r + q, theirs + row + 1] for q in range(2)])
        return carry

    lax.fori_loop(0, 16, other_block, 0, unroll=4)
    eta_copy.wait_recv()

    def last_z(row):
        at = mine + row
        hz = eta[1, pl.ds(at, 1), :] * ((ha[0, row] - xt[4, at]) - (xt[3, at + 1] - xt[3, at]))
        mz = eta_in[pl.ds(at, 1), :] * (xt[1, at] - hb[0, row])
        return hz, mz

    def image(row, carry):
        hz_old, mz_old = carry
        at = mine + row
        to = mine + row - 1
        hz, mz = last_z(row)
        ex = xt[3, at]
        hy = eta[1, pl.ds(at, 1), :] * ((rf(ex) - ex) - (ha[1, row] - xt[5, at]))
        my = eta_in[pl.ds(at, 1), :] * (hb[1, row] - xt[2, at])
        hyb[row] = hy
        hzm[row] = mz
        ax_, ay_, az_, bx_ = hs[0, row], hs[1, row], hs[2, row], hs[3, row]
        ax[0, to] = 0.25 * ((az_ - hs[2, row - 1]) - (ay_ - rb(ay_)))
        ax[1, to] = 0.25 * ((ax_ - rb(ax_)) - (az_ - mz))
        ax[2, to] = 0.25 * ((ay_ - my) - (ax_ - hs[0, row - 1]))
        ax[3, to] = 0.25 * ((hz - hz_old) - (hy - rb(hy)))
        ax[4, to] = 0.25 * ((bx_ - rb(bx_)) - (hz - az_))
        ax[5, to] = 0.25 * ((hy - ay_) - (bx_ - hs[3, row - 1]))
        axm[row - 1] = 0.25 * ((mz - mz_old) - (my - rb(my)))
        return hz, mz

    def products(row, total):
        at = mine + row - 1
        for r in range(0, 6, 2):
            t = at * 3 + r // 2
            right = jnp.concatenate(put(t, 32, [ax[r + q, at] for q in range(2)]), axis=0)
            total = total + lax.dot_general(tiles[t], right, NT, preferred_element_type=F32)
        return total

    total = jnp.zeros((128, 64), F32)
    carry = None
    swaps = []
    for n in range(PIECES):
        for d, dst in enumerate((ha, hb)):
            arrived = [(dst.at[:, pl.ds(PIECE * n + 1, PIECE)], n)]
            if n == 0:
                arrived.append((dst.at[pl.ds(0, 1), pl.ds(0, 1)], PIECES))
            for ref, i in arrived:
                remote(ref, ref, halo_s.at[d, i, 0], halo_r.at[d, i], sibling).wait_recv()
        if n == 0:
            carry = last_z(0)
        carry = lax.fori_loop(PIECE * n + 1, PIECE * n + PIECE + 1, image, carry, unroll=4)
        rows = pl.ds(mine + PIECE * n, PIECE)
        c = remote(ax.at[:, rows], ax.at[:, rows], swap_s.at[n + 1], swap_r.at[n + 1], sibling)
        c.start()
        swaps.append(c)
        if n == 0:
            c = remote(
                axm.at[0], axm.at[16], swap_s.at[PIECES + 1], swap_r.at[PIECES + 1], sibling
            )
            c.start()
            swaps.append(c)
        total = lax.fori_loop(PIECE * n + 1, PIECE * n + PIECE + 1, products, total, unroll=4)

    total = total[:, :32] + total[:, 32:]
    total = total[:64] + total[64:]
    split_src[0] = pack(total[:32])
    split_src[1] = pack(total[32:])
    at = z * 2 + k
    scatter(
        lambda c: split_src.at[c], split_1.at[at], sum_s.at[2, 0], sum_r.at[2, 0], column_both
    )
    split_1[at] = split_src[k]

    for c in swaps:
        c.wait_recv()
    sends += swaps
    for r in range(6):
        ax[r, 32] = ax[r, 0]

    def other_image(row, carry):
        for r in range(0, 6, 2):
            put((theirs + row) * 3 + r // 2, 32, [ax[r + q, theirs + row] for q in range(2)])
        return carry

    lax.fori_loop(0, 16, other_image, 0, unroll=4)

    def third(row, acc):
        at = mine + row
        to = at - 1
        ea, eb = eta[0, pl.ds(at, 1), :], eta[1, pl.ds(at, 1), :]
        em = eta_in[pl.ds(at, 1), :]
        ux, uy, uz = ax[0, to], ax[1, to], ax[2, to]
        vx, vy, vz = ax[3, to], ax[4, to], ax[5, to]
        pz = 0.25 * (sa[row - 1] - hyb[row])
        my = 0.25 * (qb[row - 1] - hzm[row])
        curls = (
            (ea, (ax[2, to + 1] - uz) - (rf(uy) - uy)),
            (ea, (rf(ux) - ux) - (vz - uz)),
            (ea, (vy - uy) - (ax[0, to + 1] - ux)),
            (eb, (ax[5, to + 1] - vz) - (rf(vy) - vy)),
            (eb, (rf(vx) - vx) - (pz - vz)),
            (em, (uy - my) - (axm[row] - axm[row - 1])),
        )
        for i in range(0, 6, 2):
            left, right = [], []
            for e, v in curls[i : i + 2]:
                left.append(jnp.concatenate(split(v), axis=0))
                right.append(jnp.concatenate(split(e * v), axis=0))
            acc = acc + lax.dot_general(
                jnp.concatenate(left, axis=1),
                jnp.concatenate(right, axis=1),
                NT,
                preferred_element_type=F32,
            )
        return acc

    acc = jnp.zeros((64, 64), F32)
    for n, (lo, hi) in enumerate(LATE):
        for d, dst in enumerate((sa, qb)):
            ref = dst.at[pl.ds(lo, hi - lo)]
            remote(ref, ref, late_s.at[d, n, 0], late_r.at[d, n], sibling).wait_recv()
        acc = lax.fori_loop(lo + 1, hi + 1, third, acc, unroll=4)
    acc = acc[:, :32] + acc[:, 32:]
    plain_first(1, pack(0.25 * (acc[:32] + acc[32:])))

    plain_second(0)

    gathered(split_1, sum_s.at[2, 0], sum_r.at[2, 0], column_both)
    value = total_of(split_1)
    split_mid[...] = value
    at = y * CX + x
    scatter(lambda _: split_mid, split_2.at[k, at], sum_s.at[2, 1], sum_r.at[2, 1], plane_both)
    split_2[k, at] = value
    for c in sends:
        c.wait_send()

    g0 = plain_end(0)
    (inv11,) = eliminate(0.5 * (g0 + g0.T))
    plain_second(1)

    part = split_2.reshape(2 * chips, 8, 128).at[pl.ds(0, len(plane_both))]
    remote(part, part, sum_s.at[2, 1], sum_r.at[2, 1], sibling).wait_recv()
    halves = [unpack(total_of(split_2.at[c]) * (1.0 / count)) for c in range(2)]
    g1, g2 = halves
    g1t = g1.T
    g2 = 0.5 * (g2 + g2.T)
    top = jnp.concatenate([0.5 * (g1 + g1t), g2], axis=1)
    low21 = dot32(g1t, inv11, NT)
    inv22, inv21 = eliminate(g2 - dot32(low21, low21, NT), -dot32(low21, inv11, NN))
    inverse = jnp.concatenate(
        [
            jnp.concatenate([inv11, jnp.zeros((32, 32), F32)], axis=1),
            jnp.concatenate([inv21, inv22], axis=1),
        ],
        axis=0,
    )
    coeffs = dot32(dot32(dot32(inv11, top, NN), inverse, NT), inverse, NN)
    ct[...] = coeffs

    own_h, own_l = split(ct[own, :])
    left = jnp.concatenate([own_h, own_l], axis=0)
    left = jnp.concatenate([left, left], axis=1)

    def fresh(row, carry):
        for r in range(0, 6, 2):
            res = lax.dot_general(
                left, tiles[row * 3 + r // 2], NN, preferred_element_type=F32
            )
            res = res[:16] + res[16:]
            for q in range(2):
                p, c = divmod(r + q, 3)
                out[pl.ds((c * 2 + p) * 32 + row, 16, stride=192), :] = res[
                    :, 128 * q : 128 * q + 128
                ]
        return carry

    lax.fori_loop(0, 32, fresh, 0, unroll=16)

    sent(0, plain_1.at[0], 0, column_both)
    sent(0, plain_2.at[0], 1, plane_own)
    sent(1, plain_1.at[1], 0, column_both)
    sent(1, plain_2.at[1], 1, plane_own)
    sent(2, split_1, 0, column_both)
    sent(2, split_2.reshape(2 * chips, 8, 128), 1, plane_both)
    g3 = plain_end(1)
    proj = jnp.concatenate(
        [top, jnp.concatenate([g2, 0.5 * (g3 + g3.T)], axis=1)], axis=0
    )
    ray_out[...] = dot32(inverse, dot32(inverse, proj, NN), NT)


def finish(block, ray, block_out, ray_out, sem):
    copies = [
        pltpu.make_async_copy(block, block_out, sem.at[0]),
        pltpu.make_async_copy(ray, ray_out, sem.at[1]),
    ]
    for c in copies:
        c.start()
    for c in copies:
        c.wait()


def on_device(block, labels, inverse_eps):
    bands, comps, planes, ny, nz = block.shape
    count = comps * planes * CX * CY * CZ * ny * nz
    dma = pltpu.SemaphoreType.DMA
    vmem = pltpu.VMEM
    chips = CX * CY
    hbm = pl.BlockSpec(memory_space=pltpu.HBM)
    next_block, rayleigh = pl.pallas_call(
        functools.partial(kernel, count),
        out_shape=(
            jax.ShapeDtypeStruct((bands * comps * planes * ny, nz), F32),
            jax.ShapeDtypeStruct((64, 64), F32),
        ),
        in_specs=[hbm, hbm, hbm],
        out_specs=(
            pl.BlockSpec(memory_space=pltpu.VMEM),
            pl.BlockSpec(memory_space=pltpu.VMEM),
        ),
        scratch_shapes=[
            vmem((3072, 128), F32),
            vmem((2, 32, 128), jnp.int32),
            pltpu.SMEM((3,), F32),
            vmem((6, 35, 32, 128), F32),
            vmem((2, 34, 16, 128), F32),
            vmem((2, 32, 16, 128), F32),
            vmem((2, 17, 32, 128), F32),
            vmem((2, 17, 32, 128), F32),
            vmem((16, 32, 128), F32),
            vmem((16, 32, 128), F32),
            vmem((2, 40, 128), F32),
            vmem((40, 128), F32),
            vmem((4, 17, 32, 128), F32),
            vmem((17, 32, 128), F32),
            vmem((17, 32, 128), F32),
            vmem((6, 33, 32, 128), F32),
            vmem((17, 32, 128), F32),
            vmem((96, 128, 256), BF16),
            vmem((2, 8, 128), F32),
            vmem((2, 2 * CZ, 8, 128), F32),
            vmem((2, 8, 128), F32),
            vmem((2, chips, 8, 128), F32),
            vmem((2, 8, 128), F32),
            vmem((2 * CZ, 8, 128), F32),
            vmem((8, 128), F32),
            vmem((2, chips, 8, 128), F32),
            vmem((32, 64), F32),
            dma((8,)),
            dma((2, PIECES + 1, 2)),
            dma((2, PIECES + 1)),
            dma((2, len(LATE), 2)),
            dma((2, len(LATE))),
            dma((PIECES + 2,)),
            dma((PIECES + 2,)),
            dma((1,)),
            dma((1,)),
            dma((3, 2)),
            dma((3, 2)),
        ],
        compiler_params=pltpu.CompilerParams(
            collective_id=0, has_side_effects=True, vmem_limit_bytes=32 << 20
        ),
        name="subspace",
    )(
        *(
            pltpu.with_memory_space_constraint(a, pltpu.HBM)
            for a in (block.reshape(bands, comps * planes * ny, nz), labels, inverse_eps)
        )
    )
    next_block, rayleigh = pl.pallas_call(
        finish,
        out_shape=(
            jax.ShapeDtypeStruct(next_block.shape, F32),
            jax.ShapeDtypeStruct(rayleigh.shape, F32),
        ),
        in_specs=[pl.BlockSpec(memory_space=pl.ANY)] * 2,
        out_specs=(hbm, hbm),
        scratch_shapes=[dma((2,))],
        compiler_params=pltpu.CompilerParams(vmem_limit_bytes=1 << 20),
        name="finish",
    )(next_block, rayleigh)
    return next_block.reshape(block.shape), rayleigh


def solution(mesh):
    in_specs = (P("band", None, "slab", None, None), P("slab", None, None), P())
    out_specs = (P("band", None, "slab", None, None), P())
    return jax.shard_map(
        on_device, mesh=mesh, in_specs=in_specs, out_specs=out_specs, check_vma=False
    )
```

```python
import functools

import jax
import jax.numpy as jnp
from jax import lax
from jax.experimental import pallas as pl
from jax.experimental.pallas import tpu as pltpu
from jax.sharding import PartitionSpec as P

MESH = pl.DeviceIdType.MESH
F32 = jnp.float32
BF16 = jnp.bfloat16
CX, CY, CZ = 4, 4, 8
PIECE = 8
PIECES = 16 // PIECE
LATE = ((0, 12), (12, 16))
NT = (((1,), (1,)), ((), ()))
NN = (((1,), (0,)), ((), ()))


def rf(v):
    return pltpu.roll(v, v.shape[-1] - 1, v.ndim - 1)


def rb(v):
    return pltpu.roll(v, 1, v.ndim - 1)


def split(v):
    hi = v.astype(BF16)
    return hi, (v - hi.astype(F32)).astype(BF16)


def dot32(a, b, dims):
    return lax.dot_general(
        a, b, dims, precision=lax.Precision.HIGHEST, preferred_element_type=F32
    )


def remote(src, dst, send, recv, to):
    return pltpu.make_async_remote_copy(
        src_ref=src, dst_ref=dst, send_sem=send, recv_sem=recv, device_id=to, device_id_type=MESH
    )


def pack(m):
    return jnp.concatenate([m[8 * i : 8 * i + 8] for i in range(4)], axis=1)


def unpack(v):
    return jnp.concatenate([v[:, 32 * i : 32 * i + 32] for i in range(4)], axis=0)


def symmetric(m):
    return 0.5 * (m + m.T)


def identity(n):
    rows = lax.broadcasted_iota(jnp.int32, (n, n), 0)
    return (rows == lax.broadcasted_iota(jnp.int32, (n, n), 1)).astype(F32)


def eliminate(matrix, *others):
    n = matrix.shape[0]
    eye = identity(n)
    whole = jnp.concatenate([matrix, eye, *others], axis=1)
    shape = (8, whole.shape[1])
    row_id = lax.broadcasted_iota(jnp.int32, shape, 0)
    parts = [whole[8 * i : 8 * i + 8] for i in range(n // 8)]

    def wide(column, home):
        return [jnp.broadcast_to(part[:, column : column + 1], shape) for part in parts[home:]]

    f0, f1 = wide(0, 0), wide(1, 0)
    for k in range(0, n, 2):
        home, at = divmod(k, 8)
        ahead = [wide(k + 2 + j, home) for j in range(2)] if k + 2 < n else []
        a, b = f0[0][at : at + 1], f0[0][at + 1 : at + 2]
        bt, c = f1[0][at : at + 1], f1[0][at + 1 : at + 2]
        scale = 1.0 / (a * c - b * bt)

        def pivots(part):
            r0, r1 = part[at : at + 1], part[at + 1 : at + 2]
            u0, u1 = c * r0 - bt * r1, a * r1 - b * r0
            return u0 * scale, u1 * scale, u1

        t0, t1, u1 = pivots(parts[home])
        second = u1 * (1.0 / a)
        coming = []
        for columns in ahead:
            s0, s1, _ = pivots(columns[0])
            coming.append([v - (p * s0 + q * s1) for v, p, q in zip(columns, f0, f1)])
        for i in range(home, n // 8):
            new = parts[i] - (f0[i - home] * t0 + f1[i - home] * t1)
            if i == home:
                kept = jnp.where(row_id == at + 1, second, parts[i])
                new = jnp.where(row_id > at + 1, new, kept)
            parts[i] = new
        if ahead:
            f0, f1 = (columns[(k + 2) // 8 - home :] for columns in coming)
    whole = jnp.concatenate(parts, axis=0)
    diag = jnp.sum(whole[:, :n] * eye, axis=1, keepdims=True)
    whole = whole * (1.0 / jnp.sqrt(diag))
    return [whole[:, n * i : n * i + n] for i in range(1, 2 + len(others))]


def kernel(
    count,
    block,
    labels,
    inv,
    out,
    ray_out,
    xin,
    lab,
    inv_s,
    xt,
    pq,
    sq,
    hb,
    ha,
    sa,
    qb,
    eta,
    eta_in,
    hs,
    hyb,
    hzm,
    ax,
    axm,
    tiles,
    plain_src,
    plain_1,
    plain_mid,
    plain_2,
    split_src,
    split_1,
    split_mid,
    split_2,
    ct,
    in_sem,
    halo_s,
    halo_r,
    late_s,
    late_r,
    swap_s,
    swap_r,
    eta_s,
    eta_r,
    sum_s,
    sum_r,
):
    slabs = CX * CY * CZ
    chips = CX * CY
    s = lax.axis_index("slab")
    k = lax.axis_index("band")
    x = lax.rem(s, CX)
    y = lax.rem(lax.div(s, CX), CY)
    z = lax.div(s, chips)
    up = lax.rem(s + 1, slabs)
    down = lax.rem(s + slabs - 1, slabs)
    base = s - x - CX * y
    sibling = (s, 1 - k)
    plane = [
        base + CX * lax.rem(y + i, CY) + lax.rem(x + j, CX)
        for i, j in sorted(
            ((i, j) for i in range(CY) for j in range(CX) if (i, j) != (0, 0)),
            key=lambda o: -(min(o[0], CY - o[0]) + min(o[1], CX - o[1])),
        )
    ]
    column = [
        s - chips * z + chips * lax.rem(z + i, CZ)
        for i in sorted(range(1, CZ), key=lambda o: -min(o, CZ - o))
    ]
    plane_both = [(chip, c) for chip in plane for c in range(2)] + [sibling]
    column_both = [(chip, c) for chip in column for c in range(2)] + [sibling]
    plane_own = [(chip, k) for chip in plane]
    mine = pl.multiple_of(16 * k, 16)
    theirs = pl.multiple_of(16 * (1 - k), 16)
    own = pl.ds(mine, 16)

    order = (2, 4, 1, 3, 5, 0)
    loads = {
        cp: pltpu.make_async_copy(
            block.at[:, pl.ds(32 * cp, 32)],
            xin.reshape(16, 192, 128).at[:, pl.ds(32 * cp, 32)],
            in_sem.at[cp],
        )
        for cp in order
    }
    for cp in order:
        loads[cp].start()
    label_load = pltpu.make_async_copy(labels, lab, in_sem.at[6])
    label_load.start()
    inv_load = pltpu.make_async_copy(inv, inv_s, in_sem.at[7])
    inv_load.start()

    barrier = pltpu.get_barrier_semaphore()
    greeted = [(down, 0), (down, 1), (up, 0), (up, 1)] + plane_both + column_both[:-1]
    for to in greeted:
        pl.semaphore_signal(barrier, inc=1, device_id=to, device_id_type=MESH)

    turned = set()

    def turn(cp, rows):
        c, p = divmod(cp, 2)
        r = p * 3 + c
        for row in rows:
            if (cp, row) not in turned:
                turned.add((cp, row))
                value = xin[pl.ds(cp * 32 + row, 16, stride=192), :]
                xt[r, row + 1, own] = value
                if row == 31:
                    xt[r, 0, own] = value
                if row < 2:
                    xt[r, row + 33, own] = value

    def piece(n):
        return [16 * to + PIECE * n + i for to in range(2) for i in range(PIECE)]

    def halo(d, n, src, step, dst, to_slab):
        copies = []
        for to in range(2):
            if n == 0:
                copies.append(
                    remote(
                        src(1, pl.ds(step * to, 1)),
                        dst.at[pl.ds(0, 1), pl.ds(0, 1), own],
                        halo_s.at[d, PIECES, to],
                        halo_r.at[d, PIECES],
                        (to_slab, to),
                    )
                )
            copies.append(
                remote(
                    src(2, pl.ds(step * to + PIECE * n + 1, PIECE)),
                    dst.at[:, pl.ds(PIECE * n + 1, PIECE), own],
                    halo_s.at[d, n, to],
                    halo_r.at[d, n],
                    (to_slab, to),
                )
            )
        for c in copies:
            c.start()
        return copies

    sends = []
    for n in range(PIECES):
        if n == 0:
            loads[2].wait()
            turn(2, (31, 15))
            loads[4].wait()
        turn(2, piece(n))
        turn(4, piece(n))
        if n == 0:
            pl.semaphore_wait(barrier, len(greeted))
        sends += halo(0, n, lambda m, rows: xt.at[pl.ds(1, m), rows, own], 16, ha, down)
        if n == 0:
            loads[1].wait()
            turn(1, (31, 15, 0, 16))
            loads[3].wait()
            turn(3, (31, 15))
            for to in range(2):
                row = 16 * to
                pq[0, 17 * to] = xt[4, row, own] + (xt[3, row + 1, own] - xt[3, row, own])
            loads[5].wait()
        turn(1, piece(n) + [(row + 1) % 32 for row in piece(n)])
        turn(3, piece(n))
        turn(5, piece(n))
        for row in piece(n):
            ex = xt[3, row + 1, own]
            at = row + 1 + row // 16
            pq[0, at] = xt[4, row + 1, own] + (xt[3, row + 2, own] - ex)
            pq[1, at] = (rf(ex) - ex) + xt[5, row + 1, own]
        sends += halo(1, n, lambda m, rows: pq.at[pl.ds(0, m), rows], 17, hb, up)

    loads[0].wait()
    turn(0, range(32))
    swap = remote(xt.at[:, :, own], xt.at[:, :, own], swap_s.at[0], swap_r.at[0], sibling)
    swap.start()
    sends.append(swap)

    label_load.wait()
    inv_load.wait()
    for p in range(2):
        regions = lab[p]
        value = jnp.zeros(regions.shape, F32)
        for r in range(3):
            value = value + jnp.where(regions == r, 1.0, 0.0) * inv_s[r]
        eta[p, 1:33] = value
        eta[p, 0:1] = value[31:32]
        eta[p, 33:40] = value[0:7]
    eta_copy = remote(eta.at[1], eta_in, eta_s.at[0], eta_r.at[0], (up, k))
    eta_copy.start()
    sends.append(eta_copy)

    def curl_x(p, row):
        ey = xt[3 * p + 1, row, own]
        return eta[p, pl.ds(row, 1), :] * (
            (xt[3 * p + 2, row + 1, own] - xt[3 * p + 2, row, own]) - (rf(ey) - ey)
        )

    def late(row, before):
        ea = eta[0, pl.ds(row, 1), :]
        ex, ey, ez = xt[0, row, own], xt[1, row, own], xt[2, row, own]
        now = curl_x(0, row)
        hy = ea * ((rf(ex) - ex) - (xt[5, row, own] - ez))
        hz = ea * ((xt[4, row, own] - ey) - (xt[0, row + 1, own] - ex))
        sq[0, row - 1] = hy - (now - before)
        hx = curl_x(1, row)
        sq[1, row - 1] = (hx - rb(hx)) + hz
        return now

    lax.fori_loop(1, 33, late, curl_x(0, 0), unroll=4)

    def send_late(n):
        lo, hi = LATE[n]
        for d, to_slab, dst in ((0, down, sa), (1, up, qb)):
            for to in range(2):
                c = remote(
                    sq.at[d, pl.ds(16 * to + lo, hi - lo)],
                    dst.at[pl.ds(lo, hi - lo), own],
                    late_s.at[d, n, to],
                    late_r.at[d, n],
                    (to_slab, to),
                )
                c.start()
                sends.append(c)

    def scatter(src, dst, send, recv, group):
        for to in group:
            remote(src(to[1]), dst, send, recv, to).start()

    def gathered(src, send, recv, group):
        part = src.at[pl.ds(0, len(group))]
        remote(part, part, send, recv, sibling).wait_recv()

    def total_of(ref):
        values = [ref[i] for i in range(ref.shape[0])]
        while len(values) > 1:
            values = [a + b for a, b in zip(values[::2], values[1::2])]
        return values[0]

    def plain_first(i, value):
        plain_src[i] = value
        at = z * 2 + k
        scatter(
            lambda _: plain_src.at[i], plain_1.at[i, at], sum_s.at[i, 0], sum_r.at[i, 0], column_both
        )
        plain_1[i, at] = value

    def plain_second(i):
        gathered(plain_1.at[i], sum_s.at[i, 0], sum_r.at[i, 0], column_both)
        value = total_of(plain_1.at[i])
        plain_mid[i] = value
        at = y * CX + x
        scatter(
            lambda _: plain_mid.at[i], plain_2.at[i, at], sum_s.at[i, 1], sum_r.at[i, 1], plane_own
        )
        plain_2[i, at] = value

    def plain_end(i):
        gathered(plain_2.at[i], sum_s.at[i, 1], sum_r.at[i, 1], plane_own)
        return unpack(total_of(plain_2.at[i]) * (1.0 / count))

    def sent(i, ref, phase, group):
        part = ref.at[pl.ds(0, len(group))]
        remote(part, part, sum_s.at[i, phase], sum_r.at[i, phase], sibling).wait_send()

    for n in range(len(LATE)):
        send_late(n)

    swap.wait_recv()

    def put(t, at, values):
        hi, lo = (jnp.concatenate(v, axis=1) for v in zip(*(split(v) for v in values)))
        tiles[t, at : at + 32] = hi
        tiles[t, at + 64 : at + 96] = lo
        return hi, lo

    def first_gram(row, total):
        for r in range(0, 6, 2):
            both = jnp.concatenate(
                put((mine + row) * 3 + r // 2, 0, [xt[r + q, mine + row + 1] for q in range(2)]),
                axis=0,
            )
            total = total + lax.dot_general(both, both, NT, preferred_element_type=F32)
        return total

    total = lax.fori_loop(0, 16, first_gram, jnp.zeros((64, 64), F32), unroll=4)
    total = total[:, :32] + total[:, 32:]
    plain_first(0, pack(symmetric(total[:32] + total[32:])))

    def inside(row, carry):
        at = mine + row
        ea, eb = eta[0, pl.ds(at, 1), :], eta[1, pl.ds(at, 1), :]
        ex, ey, ez = xt[0, at], xt[1, at], xt[2, at]
        fy, fz = xt[4, at], xt[5, at]
        hs[0, row] = ea * ((xt[2, at + 1] - ez) - (rf(ey) - ey))
        hs[1, row] = ea * ((rf(ex) - ex) - (fz - ez))
        hs[2, row] = ea * ((fy - ey) - (xt[0, at + 1] - ex))
        hs[3, row] = eb * ((xt[5, at + 1] - fz) - (rf(fy) - fy))
        return carry

    inside(0, 0)
    lax.fori_loop(1, 17, inside, 0, unroll=4)

    def other_block(row, carry):
        for r in range(0, 6, 2):
            put((theirs + row) * 3 + r // 2, 0, [xt[r + q, theirs + row + 1] for q in range(2)])
        return carry

    lax.fori_loop(0, 16, other_block, 0, unroll=4)
    eta_copy.wait_recv()

    def last_z(row):
        at = mine + row
        hz = eta[1, pl.ds(at, 1), :] * ((ha[0, row] - xt[4, at]) - (xt[3, at + 1] - xt[3, at]))
        mz = eta_in[pl.ds(at, 1), :] * (xt[1, at] - hb[0, row])
        return hz, mz

    def image(row, carry):
        hz_old, mz_old = carry
        at = mine + row
        to = mine + row - 1
        hz, mz = last_z(row)
        ex = xt[3, at]
        hy = eta[1, pl.ds(at, 1), :] * ((rf(ex) - ex) - (ha[1, row] - xt[5, at]))
        my = eta_in[pl.ds(at, 1), :] * (hb[1, row] - xt[2, at])
        hyb[row] = hy
        hzm[row] = mz
        ax_, ay_, az_, bx_ = hs[0, row], hs[1, row], hs[2, row], hs[3, row]
        ax[0, to] = 0.25 * ((az_ - hs[2, row - 1]) - (ay_ - rb(ay_)))
        ax[1, to] = 0.25 * ((ax_ - rb(ax_)) - (az_ - mz))
        ax[2, to] = 0.25 * ((ay_ - my) - (ax_ - hs[0, row - 1]))
        ax[3, to] = 0.25 * ((hz - hz_old) - (hy - rb(hy)))
        ax[4, to] = 0.25 * ((bx_ - rb(bx_)) - (hz - az_))
        ax[5, to] = 0.25 * ((hy - ay_) - (bx_ - hs[3, row - 1]))
        axm[row - 1] = 0.25 * ((mz - mz_old) - (my - rb(my)))
        return hz, mz

    def products(row, total):
        at = mine + row - 1
        for r in range(0, 6, 2):
            t = at * 3 + r // 2
            right = jnp.concatenate(put(t, 32, [ax[r + q, at] for q in range(2)]), axis=0)
            total = total + lax.dot_general(tiles[t], right, NT, preferred_element_type=F32)
        return total

    total = jnp.zeros((128, 64), F32)
    carry = None
    swaps = []
    for n in range(PIECES):
        for d, dst in enumerate((ha, hb)):
            arrived = [(dst.at[:, pl.ds(PIECE * n + 1, PIECE)], n)]
            if n == 0:
                arrived.append((dst.at[pl.ds(0, 1), pl.ds(0, 1)], PIECES))
            for ref, i in arrived:
                remote(ref, ref, halo_s.at[d, i, 0], halo_r.at[d, i], sibling).wait_recv()
        if n == 0:
            carry = last_z(0)
        carry = lax.fori_loop(PIECE * n + 1, PIECE * n + PIECE + 1, image, carry, unroll=4)
        rows = pl.ds(mine + PIECE * n, PIECE)
        c = remote(ax.at[:, rows], ax.at[:, rows], swap_s.at[n + 1], swap_r.at[n + 1], sibling)
        c.start()
        swaps.append(c)
        if n == 0:
            c = remote(
                axm.at[0], axm.at[16], swap_s.at[PIECES + 1], swap_r.at[PIECES + 1], sibling
            )
            c.start()
            swaps.append(c)
        total = lax.fori_loop(PIECE * n + 1, PIECE * n + PIECE + 1, products, total, unroll=4)

    total = total[:, :32] + total[:, 32:]
    total = total[:64] + total[64:]
    split_src[0:8] = pack(total[:32])
    split_src[8:16] = pack(symmetric(total[32:]))
    at = z * 2 + k
    scatter(lambda _: split_src, split_1.at[at], sum_s.at[2, 0], sum_r.at[2, 0], column_both)
    split_1[at] = split_src[...]

    for c in swaps:
        c.wait_recv()
    sends += swaps
    for r in range(6):
        ax[r, 32] = ax[r, 0]

    def other_image(row, carry):
        for r in range(0, 6, 2):
            put((theirs + row) * 3 + r // 2, 32, [ax[r + q, theirs + row] for q in range(2)])
        return carry

    lax.fori_loop(0, 16, other_image, 0, unroll=4)

    def third(row, acc):
        at = mine + row
        to = at - 1
        ea, eb = eta[0, pl.ds(at, 1), :], eta[1, pl.ds(at, 1), :]
        em = eta_in[pl.ds(at, 1), :]
        ux, uy, uz = ax[0, to], ax[1, to], ax[2, to]
        vx, vy, vz = ax[3, to], ax[4, to], ax[5, to]
        pz = 0.25 * (sa[row - 1] - hyb[row])
        my = 0.25 * (qb[row - 1] - hzm[row])
        curls = (
            (ea, (ax[2, to + 1] - uz) - (rf(uy) - uy)),
            (ea, (rf(ux) - ux) - (vz - uz)),
            (ea, (vy - uy) - (ax[0, to + 1] - ux)),
            (eb, (ax[5, to + 1] - vz) - (rf(vy) - vy)),
            (eb, (rf(vx) - vx) - (pz - vz)),
            (em, (uy - my) - (axm[row] - axm[row - 1])),
        )
        for i in range(0, 6, 2):
            left, right = [], []
            for e, v in curls[i : i + 2]:
                left.append(jnp.concatenate(split(v), axis=0))
                right.append(jnp.concatenate(split(e * v), axis=0))
            acc = acc + lax.dot_general(
                jnp.concatenate(left, axis=1),
                jnp.concatenate(right, axis=1),
                NT,
                preferred_element_type=F32,
            )
        return acc

    acc = jnp.zeros((64, 64), F32)
    for n, (lo, hi) in enumerate(LATE):
        for d, dst in enumerate((sa, qb)):
            ref = dst.at[pl.ds(lo, hi - lo)]
            remote(ref, ref, late_s.at[d, n, 0], late_r.at[d, n], sibling).wait_recv()
        acc = lax.fori_loop(lo + 1, hi + 1, third, acc, unroll=4)
    acc = acc[:, :32] + acc[:, 32:]
    plain_first(1, pack(0.25 * symmetric(acc[:32] + acc[32:])))

    plain_second(0)

    gathered(split_1, sum_s.at[2, 0], sum_r.at[2, 0], column_both)
    value = total_of(split_1)
    split_mid[...] = value
    at = y * CX + x
    scatter(lambda _: split_mid, split_2.at[at], sum_s.at[2, 1], sum_r.at[2, 1], plane_own)
    split_2[at] = value
    for c in sends:
        c.wait_send()

    g0 = plain_end(0)
    (inv11,) = eliminate(g0)
    plain_second(1)

    gathered(split_2, sum_s.at[2, 1], sum_r.at[2, 1], plane_own)
    value = total_of(split_2) * (1.0 / count)
    halves = [unpack(value[8 * c : 8 * c + 8]) for c in range(2)]
    g1, g2 = halves
    g1t = g1.T
    top = jnp.concatenate([0.5 * (g1 + g1t), g2], axis=1)
    low21 = dot32(g1t, inv11, NT)
    inv22, inv21 = eliminate(g2 - dot32(low21, low21, NT), -dot32(low21, inv11, NN))
    inverse = jnp.concatenate(
        [
            jnp.concatenate([inv11, jnp.zeros((32, 32), F32)], axis=1),
            jnp.concatenate([inv21, inv22], axis=1),
        ],
        axis=0,
    )
    coeffs = dot32(dot32(dot32(inv11, top, NN), inverse, NT), inverse, NN)
    ct[...] = coeffs

    own_h, own_l = split(ct[own, :])
    left = jnp.concatenate([own_h, own_l], axis=0)
    left = jnp.concatenate([left, left], axis=1)

    def fresh(row, carry):
        for r in range(0, 6, 2):
            res = lax.dot_general(
                left, tiles[row * 3 + r // 2], NN, preferred_element_type=F32
            )
            res = res[:16] + res[16:]
            for q in range(2):
                p, c = divmod(r + q, 3)
                out[pl.ds((c * 2 + p) * 32 + row, 16, stride=192), :] = res[
                    :, 128 * q : 128 * q + 128
                ]
        return carry

    lax.fori_loop(0, 32, fresh, 0, unroll=32)

    sent(0, plain_1.at[0], 0, column_both)
    sent(0, plain_2.at[0], 1, plane_own)
    sent(1, plain_1.at[1], 0, column_both)
    sent(1, plain_2.at[1], 1, plane_own)
    sent(2, split_1, 0, column_both)
    sent(2, split_2, 1, plane_own)
    g3 = plain_end(1)
    proj = jnp.concatenate(
        [top, jnp.concatenate([g2, g3], axis=1)], axis=0
    )
    ray_out[...] = dot32(inverse, dot32(inverse, proj, NN), NT)


def finish(block, ray, block_out, ray_out, sem):
    copies = [
        pltpu.make_async_copy(block, block_out, sem.at[0]),
        pltpu.make_async_copy(ray, ray_out, sem.at[1]),
    ]
    for c in copies:
        c.start()
    for c in copies:
        c.wait()


def on_device(block, labels, inverse_eps):
    bands, comps, planes, ny, nz = block.shape
    count = comps * planes * CX * CY * CZ * ny * nz
    dma = pltpu.SemaphoreType.DMA
    vmem = pltpu.VMEM
    chips = CX * CY
    hbm = pl.BlockSpec(memory_space=pltpu.HBM)
    next_block, rayleigh = pl.pallas_call(
        functools.partial(kernel, count),
        out_shape=(
            jax.ShapeDtypeStruct((bands * comps * planes * ny, nz), F32),
            jax.ShapeDtypeStruct((64, 64), F32),
        ),
        in_specs=[hbm, hbm, hbm],
        out_specs=(
            pl.BlockSpec(memory_space=pltpu.VMEM),
            pl.BlockSpec(memory_space=pltpu.VMEM),
        ),
        scratch_shapes=[
            vmem((3072, 128), F32),
            vmem((2, 32, 128), jnp.int32),
            pltpu.SMEM((3,), F32),
            vmem((6, 35, 32, 128), F32),
            vmem((2, 34, 16, 128), F32),
            vmem((2, 32, 16, 128), F32),
            vmem((2, 17, 32, 128), F32),
            vmem((2, 17, 32, 128), F32),
            vmem((16, 32, 128), F32),
            vmem((16, 32, 128), F32),
            vmem((2, 40, 128), F32),
            vmem((40, 128), F32),
            vmem((4, 17, 32, 128), F32),
            vmem((17, 32, 128), F32),
            vmem((17, 32, 128), F32),
            vmem((6, 33, 32, 128), F32),
            vmem((17, 32, 128), F32),
            vmem((96, 128, 256), BF16),
            vmem((2, 8, 128), F32),
            vmem((2, 2 * CZ, 8, 128), F32),
            vmem((2, 8, 128), F32),
            vmem((2, chips, 8, 128), F32),
            vmem((16, 128), F32),
            vmem((2 * CZ, 16, 128), F32),
            vmem((16, 128), F32),
            vmem((chips, 16, 128), F32),
            vmem((32, 64), F32),
            dma((8,)),
            dma((2, PIECES + 1, 2)),
            dma((2, PIECES + 1)),
            dma((2, len(LATE), 2)),
            dma((2, len(LATE))),
            dma((PIECES + 2,)),
            dma((PIECES + 2,)),
            dma((1,)),
            dma((1,)),
            dma((3, 2)),
            dma((3, 2)),
        ],
        compiler_params=pltpu.CompilerParams(
            collective_id=0, has_side_effects=True, vmem_limit_bytes=32 << 20
        ),
        name="subspace",
    )(
        *(
            pltpu.with_memory_space_constraint(a, pltpu.HBM)
            for a in (block.reshape(bands, comps * planes * ny, nz), labels, inverse_eps)
        )
    )
    next_block, rayleigh = pl.pallas_call(
        finish,
        out_shape=(
            jax.ShapeDtypeStruct(next_block.shape, F32),
            jax.ShapeDtypeStruct(rayleigh.shape, F32),
        ),
        in_specs=[pl.BlockSpec(memory_space=pl.ANY)] * 2,
        out_specs=(hbm, hbm),
        scratch_shapes=[dma((2,))],
        compiler_params=pltpu.CompilerParams(vmem_limit_bytes=1 << 20),
        name="finish",
    )(next_block, rayleigh)
    return next_block.reshape(block.shape), rayleigh


def solution(mesh):
    in_specs = (P("band", None, "slab", None, None), P("slab", None, None), P())
    out_specs = (P("band", None, "slab", None, None), P())
    return jax.shard_map(
        on_device, mesh=mesh, in_specs=in_specs, out_specs=out_specs, check_vma=False
    )
```

```python
import functools

import jax
import jax.numpy as jnp
from jax import lax
from jax.experimental import pallas as pl
from jax.experimental.pallas import tpu as pltpu
from jax.sharding import PartitionSpec as P

MESH = pl.DeviceIdType.MESH
F32 = jnp.float32
BF16 = jnp.bfloat16
CX, CY, CZ = 4, 4, 8
PIECE = 8
PIECES = 16 // PIECE
LATE = ((0, 12), (12, 16))
NT = (((1,), (1,)), ((), ()))
NN = (((1,), (0,)), ((), ()))


def rf(v):
    return pltpu.roll(v, v.shape[-1] - 1, v.ndim - 1)


def rb(v):
    return pltpu.roll(v, 1, v.ndim - 1)


def split(v):
    hi = v.astype(BF16)
    return hi, (v - hi.astype(F32)).astype(BF16)


def dot32(a, b, dims):
    return lax.dot_general(
        a, b, dims, precision=lax.Precision.HIGHEST, preferred_element_type=F32
    )


def remote(src, dst, send, recv, to):
    return pltpu.make_async_remote_copy(
        src_ref=src, dst_ref=dst, send_sem=send, recv_sem=recv, device_id=to, device_id_type=MESH
    )


def pack(m):
    return jnp.concatenate([m[8 * i : 8 * i + 8] for i in range(4)], axis=1)


def unpack(v):
    return jnp.concatenate([v[:, 32 * i : 32 * i + 32] for i in range(4)], axis=0)


def symmetric(m):
    return 0.5 * (m + m.T)


def identity(n):
    rows = lax.broadcasted_iota(jnp.int32, (n, n), 0)
    return (rows == lax.broadcasted_iota(jnp.int32, (n, n), 1)).astype(F32)


def eliminate(matrix, *others):
    n = matrix.shape[0]
    eye = identity(n)
    marked = matrix * eye
    row_scale = 1.0 / jnp.sqrt(jnp.sum(marked, axis=1, keepdims=True))
    column_scale = 1.0 / jnp.sqrt(jnp.sum(marked, axis=0, keepdims=True))
    whole = jnp.concatenate([matrix * column_scale, eye, *others], axis=1) * row_scale
    shape = (8, whole.shape[1])
    row_id = lax.broadcasted_iota(jnp.int32, shape, 0)
    parts = [whole[8 * i : 8 * i + 8] for i in range(n // 8)]

    def wide(column, home):
        return [jnp.broadcast_to(part[:, column : column + 1], shape) for part in parts[home:]]

    f0, f1 = wide(0, 0), wide(1, 0)
    for k in range(0, n, 2):
        home, at = divmod(k, 8)
        ahead = [wide(k + 2 + j, home) for j in range(2)] if k + 2 < n else []
        a, b = f0[0][at : at + 1], f0[0][at + 1 : at + 2]
        bt, c = f1[0][at : at + 1], f1[0][at + 1 : at + 2]
        scale = 1.0 / (a * c - b * bt)

        def pivots(part):
            r0, r1 = part[at : at + 1], part[at + 1 : at + 2]
            u0, u1 = c * r0 - bt * r1, a * r1 - b * r0
            return u0 * scale, u1 * scale, u1

        t0, t1, u1 = pivots(parts[home])
        second = u1 * (1.0 / a)
        coming = []
        for columns in ahead:
            s0, s1, _ = pivots(columns[0])
            coming.append([v - (p * s0 + q * s1) for v, p, q in zip(columns, f0, f1)])
        for i in range(home, n // 8):
            new = parts[i] - (f0[i - home] * t0 + f1[i - home] * t1)
            if i == home:
                kept = jnp.where(row_id == at + 1, second, parts[i])
                new = jnp.where(row_id > at + 1, new, kept)
            parts[i] = new
        if ahead:
            f0, f1 = (columns[(k + 2) // 8 - home :] for columns in coming)
    whole = jnp.concatenate(parts, axis=0)
    diag = jnp.sum(whole[:, :n] * eye, axis=1, keepdims=True)
    whole = whole * (1.0 / jnp.sqrt(diag))
    return [whole[:, n * i : n * i + n] for i in range(1, 2 + len(others))]


def kernel(
    count,
    block,
    labels,
    inv,
    out,
    ray_out,
    xin,
    lab,
    inv_s,
    xt,
    pq,
    sq,
    hb,
    ha,
    sa,
    qb,
    eta,
    eta_in,
    hs,
    hyb,
    hzm,
    ax,
    axm,
    tiles,
    plain_src,
    plain_1,
    plain_mid,
    plain_2,
    split_src,
    split_1,
    split_mid,
    split_2,
    ct,
    in_sem,
    halo_s,
    halo_r,
    late_s,
    late_r,
    swap_s,
    swap_r,
    eta_s,
    eta_r,
    sum_s,
    sum_r,
):
    slabs = CX * CY * CZ
    chips = CX * CY
    s = lax.axis_index("slab")
    k = lax.axis_index("band")
    x = lax.rem(s, CX)
    y = lax.rem(lax.div(s, CX), CY)
    z = lax.div(s, chips)
    up = lax.rem(s + 1, slabs)
    down = lax.rem(s + slabs - 1, slabs)
    base = s - x - CX * y
    sibling = (s, 1 - k)
    plane = [
        base + CX * lax.rem(y + i, CY) + lax.rem(x + j, CX)
        for i, j in sorted(
            ((i, j) for i in range(CY) for j in range(CX) if (i, j) != (0, 0)),
            key=lambda o: -(min(o[0], CY - o[0]) + min(o[1], CX - o[1])),
        )
    ]
    column = [
        s - chips * z + chips * lax.rem(z + i, CZ)
        for i in sorted(range(1, CZ), key=lambda o: -min(o, CZ - o))
    ]
    plane_both = [(chip, c) for chip in plane for c in range(2)] + [sibling]
    column_both = [(chip, c) for chip in column for c in range(2)] + [sibling]
    plane_own = [(chip, k) for chip in plane]
    mine = pl.multiple_of(16 * k, 16)
    theirs = pl.multiple_of(16 * (1 - k), 16)
    own = pl.ds(mine, 16)

    order = (2, 4, 1, 3, 5, 0)
    loads = {
        cp: pltpu.make_async_copy(
            block.at[:, pl.ds(32 * cp, 32)],
            xin.reshape(16, 192, 128).at[:, pl.ds(32 * cp, 32)],
            in_sem.at[cp],
        )
        for cp in order
    }
    for cp in order:
        loads[cp].start()
    label_load = pltpu.make_async_copy(labels, lab, in_sem.at[6])
    label_load.start()
    inv_load = pltpu.make_async_copy(inv, inv_s, in_sem.at[7])
    inv_load.start()

    barrier = pltpu.get_barrier_semaphore()
    greeted = [(down, 0), (down, 1), (up, 0), (up, 1)] + plane_both + column_both[:-1]
    for to in greeted:
        pl.semaphore_signal(barrier, inc=1, device_id=to, device_id_type=MESH)

    turned = set()

    def turn(cp, rows):
        c, p = divmod(cp, 2)
        r = p * 3 + c
        for row in rows:
            if (cp, row) not in turned:
                turned.add((cp, row))
                value = xin[pl.ds(cp * 32 + row, 16, stride=192), :]
                xt[r, row + 1, own] = value
                if row == 31:
                    xt[r, 0, own] = value
                if row < 2:
                    xt[r, row + 33, own] = value

    def piece(n):
        return [16 * to + PIECE * n + i for to in range(2) for i in range(PIECE)]

    def halo(d, n, src, step, dst, to_slab):
        copies = []
        for to in range(2):
            if n == 0:
                copies.append(
                    remote(
                        src(1, pl.ds(step * to, 1)),
                        dst.at[pl.ds(0, 1), pl.ds(0, 1), own],
                        halo_s.at[d, PIECES, to],
                        halo_r.at[d, PIECES],
                        (to_slab, to),
                    )
                )
            copies.append(
                remote(
                    src(2, pl.ds(step * to + PIECE * n + 1, PIECE)),
                    dst.at[:, pl.ds(PIECE * n + 1, PIECE), own],
                    halo_s.at[d, n, to],
                    halo_r.at[d, n],
                    (to_slab, to),
                )
            )
        for c in copies:
            c.start()
        return copies

    sends = []
    for n in range(PIECES):
        if n == 0:
            loads[2].wait()
            turn(2, (31, 15))
            loads[4].wait()
        turn(2, piece(n))
        turn(4, piece(n))
        if n == 0:
            pl.semaphore_wait(barrier, len(greeted))
        sends += halo(0, n, lambda m, rows: xt.at[pl.ds(1, m), rows, own], 16, ha, down)
        if n == 0:
            loads[1].wait()
            turn(1, (31, 15, 0, 16))
            loads[3].wait()
            turn(3, (31, 15))
            for to in range(2):
                row = 16 * to
                pq[0, 17 * to] = xt[4, row, own] + (xt[3, row + 1, own] - xt[3, row, own])
            loads[5].wait()
        turn(1, piece(n) + [(row + 1) % 32 for row in piece(n)])
        turn(3, piece(n))
        turn(5, piece(n))
        for row in piece(n):
            ex = xt[3, row + 1, own]
            at = row + 1 + row // 16
            pq[0, at] = xt[4, row + 1, own] + (xt[3, row + 2, own] - ex)
            pq[1, at] = (rf(ex) - ex) + xt[5, row + 1, own]
        sends += halo(1, n, lambda m, rows: pq.at[pl.ds(0, m), rows], 17, hb, up)

    loads[0].wait()
    turn(0, range(32))
    swap = remote(xt.at[:, :, own], xt.at[:, :, own], swap_s.at[0], swap_r.at[0], sibling)
    swap.start()
    sends.append(swap)

    label_load.wait()
    inv_load.wait()
    for p in range(2):
        regions = lab[p]
        value = jnp.zeros(regions.shape, F32)
        for r in range(3):
            value = value + jnp.where(regions == r, 1.0, 0.0) * inv_s[r]
        eta[p, 1:33] = value
        eta[p, 0:1] = value[31:32]
        eta[p, 33:40] = value[0:7]
    eta_copy = remote(eta.at[1], eta_in, eta_s.at[0], eta_r.at[0], (up, k))
    eta_copy.start()
    sends.append(eta_copy)

    def curl_x(p, row):
        ey = xt[3 * p + 1, row, own]
        return eta[p, pl.ds(row, 1), :] * (
            (xt[3 * p + 2, row + 1, own] - xt[3 * p + 2, row, own]) - (rf(ey) - ey)
        )

    def late(row, before):
        ea = eta[0, pl.ds(row, 1), :]
        ex, ey, ez = xt[0, row, own], xt[1, row, own], xt[2, row, own]
        now = curl_x(0, row)
        hy = ea * ((rf(ex) - ex) - (xt[5, row, own] - ez))
        hz = ea * ((xt[4, row, own] - ey) - (xt[0, row + 1, own] - ex))
        sq[0, row - 1] = hy - (now - before)
        hx = curl_x(1, row)
        sq[1, row - 1] = (hx - rb(hx)) + hz
        return now

    lax.fori_loop(1, 33, late, curl_x(0, 0), unroll=4)

    def send_late(n):
        lo, hi = LATE[n]
        for d, to_slab, dst in ((0, down, sa), (1, up, qb)):
            for to in range(2):
                c = remote(
                    sq.at[d, pl.ds(16 * to + lo, hi - lo)],
                    dst.at[pl.ds(lo, hi - lo), own],
                    late_s.at[d, n, to],
                    late_r.at[d, n],
                    (to_slab, to),
                )
                c.start()
                sends.append(c)

    def scatter(src, dst, send, recv, group):
        for to in group:
            remote(src(to[1]), dst, send, recv, to).start()

    def gathered(src, send, recv, group):
        part = src.at[pl.ds(0, len(group))]
        remote(part, part, send, recv, sibling).wait_recv()

    def total_of(ref):
        values = [ref[i] for i in range(ref.shape[0])]
        while len(values) > 1:
            values = [a + b for a, b in zip(values[::2], values[1::2])]
        return values[0]

    def plain_first(i, value):
        plain_src[i] = value
        at = z * 2 + k
        scatter(
            lambda _: plain_src.at[i], plain_1.at[i, at], sum_s.at[i, 0], sum_r.at[i, 0], column_both
        )
        plain_1[i, at] = value

    def plain_second(i):
        gathered(plain_1.at[i], sum_s.at[i, 0], sum_r.at[i, 0], column_both)
        value = total_of(plain_1.at[i])
        plain_mid[i] = value
        at = y * CX + x
        scatter(
            lambda _: plain_mid.at[i], plain_2.at[i, at], sum_s.at[i, 1], sum_r.at[i, 1], plane_own
        )
        plain_2[i, at] = value

    def plain_end(i):
        gathered(plain_2.at[i], sum_s.at[i, 1], sum_r.at[i, 1], plane_own)
        return unpack(total_of(plain_2.at[i]) * (1.0 / count))

    def sent(i, ref, phase, group):
        part = ref.at[pl.ds(0, len(group))]
        remote(part, part, sum_s.at[i, phase], sum_r.at[i, phase], sibling).wait_send()

    for n in range(len(LATE)):
        send_late(n)

    swap.wait_recv()

    def put(t, at, values):
        hi, lo = (jnp.concatenate(v, axis=1) for v in zip(*(split(v) for v in values)))
        tiles[t, at : at + 32] = hi
        tiles[t, at + 64 : at + 96] = lo
        return hi, lo

    def first_gram(row, total):
        for r in range(0, 6, 2):
            both = jnp.concatenate(
                put((mine + row) * 3 + r // 2, 0, [xt[r + q, mine + row + 1] for q in range(2)]),
                axis=0,
            )
            total = total + lax.dot_general(both, both, NT, preferred_element_type=F32)
        return total

    total = lax.fori_loop(0, 16, first_gram, jnp.zeros((64, 64), F32), unroll=4)
    total = total[:, :32] + total[:, 32:]
    plain_first(0, pack(symmetric(total[:32] + total[32:])))

    def inside(row, carry):
        at = mine + row
        ea, eb = eta[0, pl.ds(at, 1), :], eta[1, pl.ds(at, 1), :]
        ex, ey, ez = xt[0, at], xt[1, at], xt[2, at]
        fy, fz = xt[4, at], xt[5, at]
        hs[0, row] = ea * ((xt[2, at + 1] - ez) - (rf(ey) - ey))
        hs[1, row] = ea * ((rf(ex) - ex) - (fz - ez))
        hs[2, row] = ea * ((fy - ey) - (xt[0, at + 1] - ex))
        hs[3, row] = eb * ((xt[5, at + 1] - fz) - (rf(fy) - fy))
        return carry

    inside(0, 0)
    lax.fori_loop(1, 17, inside, 0, unroll=4)

    def other_block(row, carry):
        for r in range(0, 6, 2):
            put((theirs + row) * 3 + r // 2, 0, [xt[r + q, theirs + row + 1] for q in range(2)])
        return carry

    lax.fori_loop(0, 16, other_block, 0, unroll=4)
    eta_copy.wait_recv()

    def last_z(row):
        at = mine + row
        hz = eta[1, pl.ds(at, 1), :] * ((ha[0, row] - xt[4, at]) - (xt[3, at + 1] - xt[3, at]))
        mz = eta_in[pl.ds(at, 1), :] * (xt[1, at] - hb[0, row])
        return hz, mz

    def image(row, carry):
        hz_old, mz_old = carry
        at = mine + row
        to = mine + row - 1
        hz, mz = last_z(row)
        ex = xt[3, at]
        hy = eta[1, pl.ds(at, 1), :] * ((rf(ex) - ex) - (ha[1, row] - xt[5, at]))
        my = eta_in[pl.ds(at, 1), :] * (hb[1, row] - xt[2, at])
        hyb[row] = hy
        hzm[row] = mz
        ax_, ay_, az_, bx_ = hs[0, row], hs[1, row], hs[2, row], hs[3, row]
        ax[0, to] = 0.25 * ((az_ - hs[2, row - 1]) - (ay_ - rb(ay_)))
        ax[1, to] = 0.25 * ((ax_ - rb(ax_)) - (az_ - mz))
        ax[2, to] = 0.25 * ((ay_ - my) - (ax_ - hs[0, row - 1]))
        ax[3, to] = 0.25 * ((hz - hz_old) - (hy - rb(hy)))
        ax[4, to] = 0.25 * ((bx_ - rb(bx_)) - (hz - az_))
        ax[5, to] = 0.25 * ((hy - ay_) - (bx_ - hs[3, row - 1]))
        axm[row - 1] = 0.25 * ((mz - mz_old) - (my - rb(my)))
        return hz, mz

    def products(row, total):
        at = mine + row - 1
        for r in range(0, 6, 2):
            t = at * 3 + r // 2
            right = jnp.concatenate(put(t, 32, [ax[r + q, at] for q in range(2)]), axis=0)
            total = total + lax.dot_general(tiles[t], right, NT, preferred_element_type=F32)
        return total

    total = jnp.zeros((128, 64), F32)
    carry = None
    swaps = []
    for n in range(PIECES):
        for d, dst in enumerate((ha, hb)):
            arrived = [(dst.at[:, pl.ds(PIECE * n + 1, PIECE)], n)]
            if n == 0:
                arrived.append((dst.at[pl.ds(0, 1), pl.ds(0, 1)], PIECES))
            for ref, i in arrived:
                remote(ref, ref, halo_s.at[d, i, 0], halo_r.at[d, i], sibling).wait_recv()
        if n == 0:
            carry = last_z(0)
        carry = lax.fori_loop(PIECE * n + 1, PIECE * n + PIECE + 1, image, carry, unroll=4)
        rows = pl.ds(mine + PIECE * n, PIECE)
        c = remote(ax.at[:, rows], ax.at[:, rows], swap_s.at[n + 1], swap_r.at[n + 1], sibling)
        c.start()
        swaps.append(c)
        if n == 0:
            c = remote(
                axm.at[0], axm.at[16], swap_s.at[PIECES + 1], swap_r.at[PIECES + 1], sibling
            )
            c.start()
            swaps.append(c)
        total = lax.fori_loop(PIECE * n + 1, PIECE * n + PIECE + 1, products, total, unroll=4)

    total = total[:, :32] + total[:, 32:]
    total = total[:64] + total[64:]
    split_src[0:8] = pack(total[:32])
    split_src[8:16] = pack(symmetric(total[32:]))
    at = z * 2 + k
    scatter(lambda _: split_src, split_1.at[at], sum_s.at[2, 0], sum_r.at[2, 0], column_both)
    split_1[at] = split_src[...]

    for c in swaps:
        c.wait_recv()
    sends += swaps
    for r in range(6):
        ax[r, 32] = ax[r, 0]

    def other_image(row, carry):
        for r in range(0, 6, 2):
            put((theirs + row) * 3 + r // 2, 32, [ax[r + q, theirs + row] for q in range(2)])
        return carry

    lax.fori_loop(0, 16, other_image, 0, unroll=4)

    def third(row, acc):
        at = mine + row
        to = at - 1
        ea, eb = eta[0, pl.ds(at, 1), :], eta[1, pl.ds(at, 1), :]
        em = eta_in[pl.ds(at, 1), :]
        ux, uy, uz = ax[0, to], ax[1, to], ax[2, to]
        vx, vy, vz = ax[3, to], ax[4, to], ax[5, to]
        pz = 0.25 * (sa[row - 1] - hyb[row])
        my = 0.25 * (qb[row - 1] - hzm[row])
        curls = (
            (ea, (ax[2, to + 1] - uz) - (rf(uy) - uy)),
            (ea, (rf(ux) - ux) - (vz - uz)),
            (ea, (vy - uy) - (ax[0, to + 1] - ux)),
            (eb, (ax[5, to + 1] - vz) - (rf(vy) - vy)),
            (eb, (rf(vx) - vx) - (pz - vz)),
            (em, (uy - my) - (axm[row] - axm[row - 1])),
        )
        for i in range(0, 6, 2):
            left, right = [], []
            for e, v in curls[i : i + 2]:
                left.append(jnp.concatenate(split(v), axis=0))
                right.append(jnp.concatenate(split(e * v), axis=0))
            acc = acc + lax.dot_general(
                jnp.concatenate(left, axis=1),
                jnp.concatenate(right, axis=1),
                NT,
                preferred_element_type=F32,
            )
        return acc

    acc = jnp.zeros((64, 64), F32)
    for n, (lo, hi) in enumerate(LATE):
        for d, dst in enumerate((sa, qb)):
            ref = dst.at[pl.ds(lo, hi - lo)]
            remote(ref, ref, late_s.at[d, n, 0], late_r.at[d, n], sibling).wait_recv()
        acc = lax.fori_loop(lo + 1, hi + 1, third, acc, unroll=4)
    acc = acc[:, :32] + acc[:, 32:]
    plain_first(1, pack(0.25 * symmetric(acc[:32] + acc[32:])))

    plain_second(0)

    gathered(split_1, sum_s.at[2, 0], sum_r.at[2, 0], column_both)
    value = total_of(split_1)
    split_mid[...] = value
    at = y * CX + x
    scatter(lambda _: split_mid, split_2.at[at], sum_s.at[2, 1], sum_r.at[2, 1], plane_own)
    split_2[at] = value
    for c in sends:
        c.wait_send()

    g0 = plain_end(0)
    (inv11,) = eliminate(g0)
    plain_second(1)

    gathered(split_2, sum_s.at[2, 1], sum_r.at[2, 1], plane_own)
    value = total_of(split_2) * (1.0 / count)
    halves = [unpack(value[8 * c : 8 * c + 8]) for c in range(2)]
    g1, g2 = halves
    g1t = g1.T
    top = jnp.concatenate([0.5 * (g1 + g1t), g2], axis=1)
    low21 = dot32(g1t, inv11, NT)
    inv22, inv21 = eliminate(g2 - dot32(low21, low21, NT), -dot32(low21, inv11, NN))
    inverse = jnp.concatenate(
        [
            jnp.concatenate([inv11, jnp.zeros((32, 32), F32)], axis=1),
            jnp.concatenate([inv21, inv22], axis=1),
        ],
        axis=0,
    )
    coeffs = dot32(dot32(dot32(inv11, top, NN), inverse, NT), inverse, NN)
    ct[...] = coeffs

    own_h, own_l = split(ct[own, :])
    left = jnp.concatenate([own_h, own_l], axis=0)
    left = jnp.concatenate([left, left], axis=1)

    def fresh(row, carry):
        for r in range(0, 6, 2):
            res = lax.dot_general(
                left, tiles[row * 3 + r // 2], NN, preferred_element_type=F32
            )
            res = res[:16] + res[16:]
            for q in range(2):
                p, c = divmod(r + q, 3)
                out[pl.ds((c * 2 + p) * 32 + row, 16, stride=192), :] = res[
                    :, 128 * q : 128 * q + 128
                ]
        return carry

    lax.fori_loop(0, 32, fresh, 0, unroll=32)

    sent(0, plain_1.at[0], 0, column_both)
    sent(0, plain_2.at[0], 1, plane_own)
    sent(1, plain_1.at[1], 0, column_both)
    sent(1, plain_2.at[1], 1, plane_own)
    sent(2, split_1, 0, column_both)
    sent(2, split_2, 1, plane_own)
    g3 = plain_end(1)
    proj = jnp.concatenate(
        [top, jnp.concatenate([g2, g3], axis=1)], axis=0
    )
    ray_out[...] = dot32(inverse, dot32(inverse, proj, NN), NT)


def finish(block, ray, block_out, ray_out, sem):
    copies = [
        pltpu.make_async_copy(block, block_out, sem.at[0]),
        pltpu.make_async_copy(ray, ray_out, sem.at[1]),
    ]
    for c in copies:
        c.start()
    for c in copies:
        c.wait()


def on_device(block, labels, inverse_eps):
    bands, comps, planes, ny, nz = block.shape
    count = comps * planes * CX * CY * CZ * ny * nz
    dma = pltpu.SemaphoreType.DMA
    vmem = pltpu.VMEM
    chips = CX * CY
    hbm = pl.BlockSpec(memory_space=pltpu.HBM)
    next_block, rayleigh = pl.pallas_call(
        functools.partial(kernel, count),
        out_shape=(
            jax.ShapeDtypeStruct((bands * comps * planes * ny, nz), F32),
            jax.ShapeDtypeStruct((64, 64), F32),
        ),
        in_specs=[hbm, hbm, hbm],
        out_specs=(
            pl.BlockSpec(memory_space=pltpu.VMEM),
            pl.BlockSpec(memory_space=pltpu.VMEM),
        ),
        scratch_shapes=[
            vmem((3072, 128), F32),
            vmem((2, 32, 128), jnp.int32),
            pltpu.SMEM((3,), F32),
            vmem((6, 35, 32, 128), F32),
            vmem((2, 34, 16, 128), F32),
            vmem((2, 32, 16, 128), F32),
            vmem((2, 17, 32, 128), F32),
            vmem((2, 17, 32, 128), F32),
            vmem((16, 32, 128), F32),
            vmem((16, 32, 128), F32),
            vmem((2, 40, 128), F32),
            vmem((40, 128), F32),
            vmem((4, 17, 32, 128), F32),
            vmem((17, 32, 128), F32),
            vmem((17, 32, 128), F32),
            vmem((6, 33, 32, 128), F32),
            vmem((17, 32, 128), F32),
            vmem((96, 128, 256), BF16),
            vmem((2, 8, 128), F32),
            vmem((2, 2 * CZ, 8, 128), F32),
            vmem((2, 8, 128), F32),
            vmem((2, chips, 8, 128), F32),
            vmem((16, 128), F32),
            vmem((2 * CZ, 16, 128), F32),
            vmem((16, 128), F32),
            vmem((chips, 16, 128), F32),
            vmem((32, 64), F32),
            dma((8,)),
            dma((2, PIECES + 1, 2)),
            dma((2, PIECES + 1)),
            dma((2, len(LATE), 2)),
            dma((2, len(LATE))),
            dma((PIECES + 2,)),
            dma((PIECES + 2,)),
            dma((1,)),
            dma((1,)),
            dma((3, 2)),
            dma((3, 2)),
        ],
        compiler_params=pltpu.CompilerParams(
            collective_id=0, has_side_effects=True, vmem_limit_bytes=32 << 20
        ),
        name="subspace",
    )(
        *(
            pltpu.with_memory_space_constraint(a, pltpu.HBM)
            for a in (block.reshape(bands, comps * planes * ny, nz), labels, inverse_eps)
        )
    )
    next_block, rayleigh = pl.pallas_call(
        finish,
        out_shape=(
            jax.ShapeDtypeStruct(next_block.shape, F32),
            jax.ShapeDtypeStruct(rayleigh.shape, F32),
        ),
        in_specs=[pl.BlockSpec(memory_space=pl.ANY)] * 2,
        out_specs=(hbm, hbm),
        scratch_shapes=[dma((2,))],
        compiler_params=pltpu.CompilerParams(vmem_limit_bytes=1 << 20),
        name="finish",
    )(next_block, rayleigh)
    return next_block.reshape(block.shape), rayleigh


def solution(mesh):
    in_specs = (P("band", None, "slab", None, None), P("slab", None, None), P())
    out_specs = (P("band", None, "slab", None, None), P())
    return jax.shard_map(
        on_device, mesh=mesh, in_specs=in_specs, out_specs=out_specs, check_vma=False
    )
```

```python
import functools

import jax
import jax.numpy as jnp
from jax import lax
from jax.experimental import pallas as pl
from jax.experimental.pallas import tpu as pltpu
from jax.sharding import PartitionSpec as P

MESH = pl.DeviceIdType.MESH
F32 = jnp.float32
BF16 = jnp.bfloat16
CX, CY, CZ = 4, 4, 8
PIECE = 8
PIECES = 16 // PIECE
LATE = ((0, 12), (12, 16))
NT = (((1,), (1,)), ((), ()))
NN = (((1,), (0,)), ((), ()))


def rf(v):
    return pltpu.roll(v, v.shape[-1] - 1, v.ndim - 1)


def rb(v):
    return pltpu.roll(v, 1, v.ndim - 1)


def split(v):
    hi = v.astype(BF16)
    return hi, (v - hi.astype(F32)).astype(BF16)


def dot32(a, b, dims):
    return lax.dot_general(
        a, b, dims, precision=lax.Precision.HIGHEST, preferred_element_type=F32
    )


def remote(src, dst, send, recv, to):
    return pltpu.make_async_remote_copy(
        src_ref=src, dst_ref=dst, send_sem=send, recv_sem=recv, device_id=to, device_id_type=MESH
    )


def pack(m):
    return jnp.concatenate([m[8 * i : 8 * i + 8] for i in range(4)], axis=1)


def unpack(v):
    return jnp.concatenate([v[:, 32 * i : 32 * i + 32] for i in range(4)], axis=0)


def symmetric(m):
    return 0.5 * (m + m.T)


def identity(n):
    rows = lax.broadcasted_iota(jnp.int32, (n, n), 0)
    return (rows == lax.broadcasted_iota(jnp.int32, (n, n), 1)).astype(F32)


def eliminate(matrix, *others):
    n = matrix.shape[0]
    eye = identity(n)
    marked = matrix * eye
    row_scale = 1.0 / jnp.sqrt(jnp.sum(marked, axis=1, keepdims=True))
    column_scale = 1.0 / jnp.sqrt(jnp.sum(marked, axis=0, keepdims=True))
    whole = jnp.concatenate([matrix * column_scale, eye, *others], axis=1) * row_scale
    shape = (8, whole.shape[1])
    row_id = lax.broadcasted_iota(jnp.int32, shape, 0)
    parts = [whole[8 * i : 8 * i + 8] for i in range(n // 8)]

    def wide(column, home):
        return [jnp.broadcast_to(part[:, column : column + 1], shape) for part in parts[home:]]

    f0, f1 = wide(0, 0), wide(1, 0)
    for k in range(0, n, 2):
        home, at = divmod(k, 8)
        ahead = [wide(k + 2 + j, home) for j in range(2)] if k + 2 < n else []
        a, b = f0[0][at : at + 1], f0[0][at + 1 : at + 2]
        bt, c = f1[0][at : at + 1], f1[0][at + 1 : at + 2]
        scale = 1.0 / (a * c - b * bt)

        def pivots(part):
            r0, r1 = part[at : at + 1], part[at + 1 : at + 2]
            u0, u1 = c * r0 - bt * r1, a * r1 - b * r0
            return u0 * scale, u1 * scale, u1

        t0, t1, u1 = pivots(parts[home])
        second = u1 * (1.0 / a)
        coming = []
        for columns in ahead:
            s0, s1, _ = pivots(columns[0])
            coming.append([v - (p * s0 + q * s1) for v, p, q in zip(columns, f0, f1)])
        for i in range(home, n // 8):
            new = parts[i] - (f0[i - home] * t0 + f1[i - home] * t1)
            if i == home:
                kept = jnp.where(row_id == at + 1, second, parts[i])
                new = jnp.where(row_id > at + 1, new, kept)
            parts[i] = new
        if ahead:
            f0, f1 = (columns[(k + 2) // 8 - home :] for columns in coming)
    whole = jnp.concatenate(parts, axis=0)
    diag = jnp.sum(whole[:, :n] * eye, axis=1, keepdims=True)
    whole = whole * (1.0 / jnp.sqrt(diag))
    return [whole[:, n * i : n * i + n] for i in range(1, 2 + len(others))]


def kernel(
    count,
    block,
    labels,
    inv,
    out,
    ray_out,
    xin,
    lab,
    inv_s,
    xt,
    pq,
    sq,
    hb,
    ha,
    sa,
    qb,
    eta,
    eta_in,
    hs,
    hyb,
    hzm,
    ax,
    axm,
    tiles,
    plain_src,
    plain_1,
    plain_mid,
    plain_2,
    split_src,
    split_1,
    split_mid,
    split_2,
    ct,
    in_sem,
    halo_s,
    halo_r,
    late_s,
    late_r,
    swap_s,
    swap_r,
    eta_s,
    eta_r,
    sum_s,
    sum_r,
):
    slabs = CX * CY * CZ
    chips = CX * CY
    s = lax.axis_index("slab")
    k = lax.axis_index("band")
    x = lax.rem(s, CX)
    y = lax.rem(lax.div(s, CX), CY)
    z = lax.div(s, chips)
    up = lax.rem(s + 1, slabs)
    down = lax.rem(s + slabs - 1, slabs)
    base = s - x - CX * y
    sibling = (s, 1 - k)
    plane = [
        base + CX * lax.rem(y + i, CY) + lax.rem(x + j, CX)
        for i, j in sorted(
            ((i, j) for i in range(CY) for j in range(CX) if (i, j) != (0, 0)),
            key=lambda o: -(min(o[0], CY - o[0]) + min(o[1], CX - o[1])),
        )
    ]
    column = [
        s - chips * z + chips * lax.rem(z + i, CZ)
        for i in sorted(range(1, CZ), key=lambda o: -min(o, CZ - o))
    ]
    plane_both = [(chip, c) for chip in plane for c in range(2)] + [sibling]
    column_both = [(chip, c) for chip in column for c in range(2)] + [sibling]
    plane_own = [(chip, k) for chip in plane]
    mine = pl.multiple_of(16 * k, 16)
    theirs = pl.multiple_of(16 * (1 - k), 16)
    own = pl.ds(mine, 16)

    order = (2, 4, 1, 3, 5, 0)
    loads = {
        cp: pltpu.make_async_copy(
            block.at[:, pl.ds(32 * cp, 32)],
            xin.reshape(16, 192, 128).at[:, pl.ds(32 * cp, 32)],
            in_sem.at[cp],
        )
        for cp in order
    }
    for cp in order:
        loads[cp].start()
    label_load = pltpu.make_async_copy(labels, lab, in_sem.at[6])
    label_load.start()
    inv_load = pltpu.make_async_copy(inv, inv_s, in_sem.at[7])
    inv_load.start()

    barrier = pltpu.get_barrier_semaphore()
    greeted = [(down, 0), (down, 1), (up, 0), (up, 1)] + plane_both + column_both[:-1]
    for to in greeted:
        pl.semaphore_signal(barrier, inc=1, device_id=to, device_id_type=MESH)

    turned = set()

    def turn(cp, rows):
        c, p = divmod(cp, 2)
        r = p * 3 + c
        for row in rows:
            if (cp, row) not in turned:
                turned.add((cp, row))
                value = xin[pl.ds(cp * 32 + row, 16, stride=192), :]
                xt[r, row + 1, own] = value
                if row == 31:
                    xt[r, 0, own] = value
                if row < 2:
                    xt[r, row + 33, own] = value

    def piece(n):
        return [16 * to + PIECE * n + i for to in range(2) for i in range(PIECE)]

    def halo(d, n, src, step, dst, to_slab):
        copies = []
        for to in range(2):
            if n == 0:
                copies.append(
                    remote(
                        src(1, pl.ds(step * to, 1)),
                        dst.at[pl.ds(0, 1), pl.ds(0, 1), own],
                        halo_s.at[d, PIECES, to],
                        halo_r.at[d, PIECES],
                        (to_slab, to),
                    )
                )
            copies.append(
                remote(
                    src(2, pl.ds(step * to + PIECE * n + 1, PIECE)),
                    dst.at[:, pl.ds(PIECE * n + 1, PIECE), own],
                    halo_s.at[d, n, to],
                    halo_r.at[d, n],
                    (to_slab, to),
                )
            )
        for c in copies:
            c.start()
        return copies

    sends = []
    for n in range(PIECES):
        if n == 0:
            loads[2].wait()
            turn(2, (31, 15))
            loads[4].wait()
        turn(2, piece(n))
        turn(4, piece(n))
        if n == 0:
            pl.semaphore_wait(barrier, len(greeted))
        sends += halo(0, n, lambda m, rows: xt.at[pl.ds(1, m), rows, own], 16, ha, down)
        if n == 0:
            loads[1].wait()
            turn(1, (31, 15, 0, 16))
            loads[3].wait()
            turn(3, (31, 15))
            for to in range(2):
                row = 16 * to
                pq[0, 17 * to] = xt[4, row, own] + (xt[3, row + 1, own] - xt[3, row, own])
            loads[5].wait()
        turn(1, piece(n) + [(row + 1) % 32 for row in piece(n)])
        turn(3, piece(n))
        turn(5, piece(n))
        for row in piece(n):
            ex = xt[3, row + 1, own]
            at = row + 1 + row // 16
            pq[0, at] = xt[4, row + 1, own] + (xt[3, row + 2, own] - ex)
            pq[1, at] = (rf(ex) - ex) + xt[5, row + 1, own]
        sends += halo(1, n, lambda m, rows: pq.at[pl.ds(0, m), rows], 17, hb, up)

    loads[0].wait()
    turn(0, range(32))
    swap = remote(xt.at[:, :, own], xt.at[:, :, own], swap_s.at[0], swap_r.at[0], sibling)
    swap.start()
    sends.append(swap)

    label_load.wait()
    inv_load.wait()
    for p in range(2):
        regions = lab[p]
        value = jnp.zeros(regions.shape, F32)
        for r in range(3):
            value = value + jnp.where(regions == r, 1.0, 0.0) * inv_s[r]
        eta[p, 1:33] = value
        eta[p, 0:1] = value[31:32]
        eta[p, 33:40] = value[0:7]
    eta_copy = remote(eta.at[1], eta_in, eta_s.at[0], eta_r.at[0], (up, k))
    eta_copy.start()
    sends.append(eta_copy)

    def curl_x(p, row):
        ey = xt[3 * p + 1, row, own]
        return eta[p, pl.ds(row, 1), :] * (
            (xt[3 * p + 2, row + 1, own] - xt[3 * p + 2, row, own]) - (rf(ey) - ey)
        )

    def late(row, before):
        ea = eta[0, pl.ds(row, 1), :]
        ex, ey, ez = xt[0, row, own], xt[1, row, own], xt[2, row, own]
        now = curl_x(0, row)
        hy = ea * ((rf(ex) - ex) - (xt[5, row, own] - ez))
        hz = ea * ((xt[4, row, own] - ey) - (xt[0, row + 1, own] - ex))
        sq[0, row - 1] = hy - (now - before)
        hx = curl_x(1, row)
        sq[1, row - 1] = (hx - rb(hx)) + hz
        return now

    lax.fori_loop(1, 33, late, curl_x(0, 0), unroll=4)

    def send_late(n):
        lo, hi = LATE[n]
        for d, to_slab, dst in ((0, down, sa), (1, up, qb)):
            for to in range(2):
                c = remote(
                    sq.at[d, pl.ds(16 * to + lo, hi - lo)],
                    dst.at[pl.ds(lo, hi - lo), own],
                    late_s.at[d, n, to],
                    late_r.at[d, n],
                    (to_slab, to),
                )
                c.start()
                sends.append(c)

    def scatter(src, dst, send, recv, group):
        for to in group:
            remote(src(to[1]), dst, send, recv, to).start()

    def gathered(src, send, recv, group):
        part = src.at[pl.ds(0, len(group))]
        remote(part, part, send, recv, sibling).wait_recv()

    def total_of(ref):
        values = [ref[i] for i in range(ref.shape[0])]
        while len(values) > 1:
            values = [a + b for a, b in zip(values[::2], values[1::2])]
        return values[0]

    def plain_first(i, value):
        plain_src[i] = value
        at = z * 2 + k
        scatter(
            lambda _: plain_src.at[i], plain_1.at[i, at], sum_s.at[i, 0], sum_r.at[i, 0], column_both
        )
        plain_1[i, at] = value

    def plain_second(i):
        gathered(plain_1.at[i], sum_s.at[i, 0], sum_r.at[i, 0], column_both)
        value = total_of(plain_1.at[i])
        plain_mid[i] = value
        at = y * CX + x
        scatter(
            lambda _: plain_mid.at[i], plain_2.at[i, at], sum_s.at[i, 1], sum_r.at[i, 1], plane_own
        )
        plain_2[i, at] = value

    def plain_end(i):
        gathered(plain_2.at[i], sum_s.at[i, 1], sum_r.at[i, 1], plane_own)
        return unpack(total_of(plain_2.at[i]) * (1.0 / count))

    def sent(i, ref, phase, group):
        part = ref.at[pl.ds(0, len(group))]
        remote(part, part, sum_s.at[i, phase], sum_r.at[i, phase], sibling).wait_send()

    for n in range(len(LATE)):
        send_late(n)

    swap.wait_recv()

    def put(t, at, values):
        hi, lo = (jnp.concatenate(v, axis=1) for v in zip(*(split(v) for v in values)))
        tiles[t, at : at + 32] = hi
        tiles[t, at + 64 : at + 96] = lo
        return hi, lo

    def first_gram(row, total):
        for r in range(0, 6, 2):
            both = jnp.concatenate(
                put((mine + row) * 3 + r // 2, 0, [xt[r + q, mine + row + 1] for q in range(2)]),
                axis=0,
            )
            total = total + lax.dot_general(both, both, NT, preferred_element_type=F32)
        return total

    total = lax.fori_loop(0, 16, first_gram, jnp.zeros((64, 64), F32), unroll=4)
    total = total[:, :32] + total[:, 32:]
    plain_first(0, pack(symmetric(total[:32] + total[32:])))

    def inside(row, carry):
        at = mine + row
        ea, eb = eta[0, pl.ds(at, 1), :], eta[1, pl.ds(at, 1), :]
        ex, ey, ez = xt[0, at], xt[1, at], xt[2, at]
        fy, fz = xt[4, at], xt[5, at]
        hs[0, row] = ea * ((xt[2, at + 1] - ez) - (rf(ey) - ey))
        hs[1, row] = ea * ((rf(ex) - ex) - (fz - ez))
        hs[2, row] = ea * ((fy - ey) - (xt[0, at + 1] - ex))
        hs[3, row] = eb * ((xt[5, at + 1] - fz) - (rf(fy) - fy))
        return carry

    inside(0, 0)
    lax.fori_loop(1, 17, inside, 0, unroll=4)

    def other_block(row, carry):
        for r in range(0, 6, 2):
            put((theirs + row) * 3 + r // 2, 0, [xt[r + q, theirs + row + 1] for q in range(2)])
        return carry

    lax.fori_loop(0, 16, other_block, 0, unroll=4)
    eta_copy.wait_recv()

    def last_z(row):
        at = mine + row
        hz = eta[1, pl.ds(at, 1), :] * ((ha[0, row] - xt[4, at]) - (xt[3, at + 1] - xt[3, at]))
        mz = eta_in[pl.ds(at, 1), :] * (xt[1, at] - hb[0, row])
        return hz, mz

    def image(row, carry):
        hz_old, mz_old = carry
        at = mine + row
        to = mine + row - 1
        hz, mz = last_z(row)
        ex = xt[3, at]
        hy = eta[1, pl.ds(at, 1), :] * ((rf(ex) - ex) - (ha[1, row] - xt[5, at]))
        my = eta_in[pl.ds(at, 1), :] * (hb[1, row] - xt[2, at])
        hyb[row] = hy
        hzm[row] = mz
        ax_, ay_, az_, bx_ = hs[0, row], hs[1, row], hs[2, row], hs[3, row]
        ax[0, to] = 0.25 * ((az_ - hs[2, row - 1]) - (ay_ - rb(ay_)))
        ax[1, to] = 0.25 * ((ax_ - rb(ax_)) - (az_ - mz))
        ax[2, to] = 0.25 * ((ay_ - my) - (ax_ - hs[0, row - 1]))
        ax[3, to] = 0.25 * ((hz - hz_old) - (hy - rb(hy)))
        ax[4, to] = 0.25 * ((bx_ - rb(bx_)) - (hz - az_))
        ax[5, to] = 0.25 * ((hy - ay_) - (bx_ - hs[3, row - 1]))
        axm[row - 1] = 0.25 * ((mz - mz_old) - (my - rb(my)))
        return hz, mz

    def products(row, total):
        at = mine + row - 1
        for r in range(0, 6, 2):
            t = at * 3 + r // 2
            right = jnp.concatenate(put(t, 32, [ax[r + q, at] for q in range(2)]), axis=0)
            total = total + lax.dot_general(tiles[t], right, NT, preferred_element_type=F32)
        return total

    total = jnp.zeros((128, 64), F32)
    carry = None
    swaps = []
    for n in range(PIECES):
        for d, dst in enumerate((ha, hb)):
            arrived = [(dst.at[:, pl.ds(PIECE * n + 1, PIECE)], n)]
            if n == 0:
                arrived.append((dst.at[pl.ds(0, 1), pl.ds(0, 1)], PIECES))
            for ref, i in arrived:
                remote(ref, ref, halo_s.at[d, i, 0], halo_r.at[d, i], sibling).wait_recv()
        if n == 0:
            carry = last_z(0)
        carry = lax.fori_loop(PIECE * n + 1, PIECE * n + PIECE + 1, image, carry, unroll=8)
        rows = pl.ds(mine + PIECE * n, PIECE)
        c = remote(ax.at[:, rows], ax.at[:, rows], swap_s.at[n + 1], swap_r.at[n + 1], sibling)
        c.start()
        swaps.append(c)
        if n == 0:
            c = remote(
                axm.at[0], axm.at[16], swap_s.at[PIECES + 1], swap_r.at[PIECES + 1], sibling
            )
            c.start()
            swaps.append(c)
        total = lax.fori_loop(PIECE * n + 1, PIECE * n + PIECE + 1, products, total, unroll=8)

    total = total[:, :32] + total[:, 32:]
    total = total[:64] + total[64:]
    split_src[0:8] = pack(total[:32])
    split_src[8:16] = pack(symmetric(total[32:]))
    at = z * 2 + k
    scatter(lambda _: split_src, split_1.at[at], sum_s.at[2, 0], sum_r.at[2, 0], column_both)
    split_1[at] = split_src[...]

    for c in swaps:
        c.wait_recv()
    sends += swaps
    for r in range(6):
        ax[r, 32] = ax[r, 0]

    def other_image(row, carry):
        for r in range(0, 6, 2):
            put((theirs + row) * 3 + r // 2, 32, [ax[r + q, theirs + row] for q in range(2)])
        return carry

    lax.fori_loop(0, 16, other_image, 0, unroll=4)

    def third(row, acc):
        at = mine + row
        to = at - 1
        ea, eb = eta[0, pl.ds(at, 1), :], eta[1, pl.ds(at, 1), :]
        em = eta_in[pl.ds(at, 1), :]
        ux, uy, uz = ax[0, to], ax[1, to], ax[2, to]
        vx, vy, vz = ax[3, to], ax[4, to], ax[5, to]
        pz = 0.25 * (sa[row - 1] - hyb[row])
        my = 0.25 * (qb[row - 1] - hzm[row])
        curls = (
            (ea, (ax[2, to + 1] - uz) - (rf(uy) - uy)),
            (ea, (rf(ux) - ux) - (vz - uz)),
            (ea, (vy - uy) - (ax[0, to + 1] - ux)),
            (eb, (ax[5, to + 1] - vz) - (rf(vy) - vy)),
            (eb, (rf(vx) - vx) - (pz - vz)),
            (em, (uy - my) - (axm[row] - axm[row - 1])),
        )
        for i in range(0, 6, 2):
            left, right = [], []
            for e, v in curls[i : i + 2]:
                left.append(jnp.concatenate(split(v), axis=0))
                right.append(jnp.concatenate(split(e * v), axis=0))
            acc = acc + lax.dot_general(
                jnp.concatenate(left, axis=1),
                jnp.concatenate(right, axis=1),
                NT,
                preferred_element_type=F32,
            )
        return acc

    acc = jnp.zeros((64, 64), F32)
    for n, (lo, hi) in enumerate(LATE):
        for d, dst in enumerate((sa, qb)):
            ref = dst.at[pl.ds(lo, hi - lo)]
            remote(ref, ref, late_s.at[d, n, 0], late_r.at[d, n], sibling).wait_recv()
        acc = lax.fori_loop(lo + 1, hi + 1, third, acc, unroll=4)
    acc = acc[:, :32] + acc[:, 32:]
    plain_first(1, pack(0.25 * symmetric(acc[:32] + acc[32:])))

    plain_second(0)

    gathered(split_1, sum_s.at[2, 0], sum_r.at[2, 0], column_both)
    value = total_of(split_1)
    split_mid[...] = value
    at = y * CX + x
    scatter(lambda _: split_mid, split_2.at[at], sum_s.at[2, 1], sum_r.at[2, 1], plane_own)
    split_2[at] = value
    for c in sends:
        c.wait_send()

    g0 = plain_end(0)
    (inv11,) = eliminate(g0)
    plain_second(1)

    gathered(split_2, sum_s.at[2, 1], sum_r.at[2, 1], plane_own)
    value = total_of(split_2) * (1.0 / count)
    halves = [unpack(value[8 * c : 8 * c + 8]) for c in range(2)]
    g1, g2 = halves
    g1t = g1.T
    top = jnp.concatenate([0.5 * (g1 + g1t), g2], axis=1)
    low21 = dot32(g1t, inv11, NT)
    inv22, inv21 = eliminate(g2 - dot32(low21, low21, NT), -dot32(low21, inv11, NN))
    inverse = jnp.concatenate(
        [
            jnp.concatenate([inv11, jnp.zeros((32, 32), F32)], axis=1),
            jnp.concatenate([inv21, inv22], axis=1),
        ],
        axis=0,
    )
    coeffs = dot32(dot32(dot32(inv11, top, NN), inverse, NT), inverse, NN)
    ct[...] = coeffs

    own_h, own_l = split(ct[own, :])
    left = jnp.concatenate([own_h, own_l], axis=0)
    left = jnp.concatenate([left, left], axis=1)

    def fresh(row, carry):
        for r in range(0, 6, 2):
            res = lax.dot_general(
                left, tiles[row * 3 + r // 2], NN, preferred_element_type=F32
            )
            res = res[:16] + res[16:]
            for q in range(2):
                p, c = divmod(r + q, 3)
                out[pl.ds((c * 2 + p) * 32 + row, 16, stride=192), :] = res[
                    :, 128 * q : 128 * q + 128
                ]
        return carry

    lax.fori_loop(0, 32, fresh, 0, unroll=32)

    sent(0, plain_1.at[0], 0, column_both)
    sent(0, plain_2.at[0], 1, plane_own)
    sent(1, plain_1.at[1], 0, column_both)
    sent(1, plain_2.at[1], 1, plane_own)
    sent(2, split_1, 0, column_both)
    sent(2, split_2, 1, plane_own)
    g3 = plain_end(1)
    proj = jnp.concatenate(
        [top, jnp.concatenate([g2, g3], axis=1)], axis=0
    )
    ray_out[...] = dot32(inverse, dot32(inverse, proj, NN), NT)


def finish(block, ray, block_out, ray_out, sem):
    copies = [
        pltpu.make_async_copy(block, block_out, sem.at[0]),
        pltpu.make_async_copy(ray, ray_out, sem.at[1]),
    ]
    for c in copies:
        c.start()
    for c in copies:
        c.wait()


def on_device(block, labels, inverse_eps):
    bands, comps, planes, ny, nz = block.shape
    count = comps * planes * CX * CY * CZ * ny * nz
    dma = pltpu.SemaphoreType.DMA
    vmem = pltpu.VMEM
    chips = CX * CY
    hbm = pl.BlockSpec(memory_space=pltpu.HBM)
    next_block, rayleigh = pl.pallas_call(
        functools.partial(kernel, count),
        out_shape=(
            jax.ShapeDtypeStruct((bands * comps * planes * ny, nz), F32),
            jax.ShapeDtypeStruct((64, 64), F32),
        ),
        in_specs=[hbm, hbm, hbm],
        out_specs=(
            pl.BlockSpec(memory_space=pltpu.VMEM),
            pl.BlockSpec(memory_space=pltpu.VMEM),
        ),
        scratch_shapes=[
            vmem((3072, 128), F32),
            vmem((2, 32, 128), jnp.int32),
            pltpu.SMEM((3,), F32),
            vmem((6, 35, 32, 128), F32),
            vmem((2, 34, 16, 128), F32),
            vmem((2, 32, 16, 128), F32),
            vmem((2, 17, 32, 128), F32),
            vmem((2, 17, 32, 128), F32),
            vmem((16, 32, 128), F32),
            vmem((16, 32, 128), F32),
            vmem((2, 40, 128), F32),
            vmem((40, 128), F32),
            vmem((4, 17, 32, 128), F32),
            vmem((17, 32, 128), F32),
            vmem((17, 32, 128), F32),
            vmem((6, 33, 32, 128), F32),
            vmem((17, 32, 128), F32),
            vmem((96, 128, 256), BF16),
            vmem((2, 8, 128), F32),
            vmem((2, 2 * CZ, 8, 128), F32),
            vmem((2, 8, 128), F32),
            vmem((2, chips, 8, 128), F32),
            vmem((16, 128), F32),
            vmem((2 * CZ, 16, 128), F32),
            vmem((16, 128), F32),
            vmem((chips, 16, 128), F32),
            vmem((32, 64), F32),
            dma((8,)),
            dma((2, PIECES + 1, 2)),
            dma((2, PIECES + 1)),
            dma((2, len(LATE), 2)),
            dma((2, len(LATE))),
            dma((PIECES + 2,)),
            dma((PIECES + 2,)),
            dma((1,)),
            dma((1,)),
            dma((3, 2)),
            dma((3, 2)),
        ],
        compiler_params=pltpu.CompilerParams(
            collective_id=0, has_side_effects=True, vmem_limit_bytes=32 << 20
        ),
        name="subspace",
    )(
        *(
            pltpu.with_memory_space_constraint(a, pltpu.HBM)
            for a in (block.reshape(bands, comps * planes * ny, nz), labels, inverse_eps)
        )
    )
    next_block, rayleigh = pl.pallas_call(
        finish,
        out_shape=(
            jax.ShapeDtypeStruct(next_block.shape, F32),
            jax.ShapeDtypeStruct(rayleigh.shape, F32),
        ),
        in_specs=[pl.BlockSpec(memory_space=pl.ANY)] * 2,
        out_specs=(hbm, hbm),
        scratch_shapes=[dma((2,))],
        compiler_params=pltpu.CompilerParams(vmem_limit_bytes=1 << 20),
        name="finish",
    )(next_block, rayleigh)
    return next_block.reshape(block.shape), rayleigh


def solution(mesh):
    in_specs = (P("band", None, "slab", None, None), P("slab", None, None), P())
    out_specs = (P("band", None, "slab", None, None), P())
    return jax.shard_map(
        on_device, mesh=mesh, in_specs=in_specs, out_specs=out_specs, check_vma=False
    )
```
